32 devices in a mesh: groups: 2 (over y), tensor: 16 (over z, x, core).
Axes of the slice: x: 2, y: 2, z: 4, core: 2. Of those that a mesh axis runs over, the one named last changes fastest.
Arguments:
- input_hidden: bfloat16 [128, 8192], P(('groups', 'tensor')), parts along dimension 0, may hold values from -6 to 6
- input_norm_gain: bfloat16 [8192], replicated, may hold values from 0.099609375 to 1.8984375
- request_adapter: int32 [128, 1], P(('groups', 'tensor')), parts along dimension 0, may hold values from 0 to 31; in each aligned block of 64 rows (0 to 63, 64 to 127, ...) at most 16 rows name the same one
- adapter_storage: int32 [32], replicated, may hold values from 0 to 31, each once
- lengths: int32 [128], P(('groups', 'tensor')), parts along dimension 0, may hold values from 1 to 384, as said below
- projection_weight: bfloat16 [8192, 10240], P(None, 'tensor'), may hold values from -0.0625 to 0.0625
- output_weight: bfloat16 [8192, 8192], P(None, 'tensor'), may hold values from -0.0625 to 0.0625
- adapter_down: bfloat16 [32, 8192, 64], P('tensor'), may hold values from -0.0625 to 0.0625
- projection_up_adapter: bfloat16 [32, 16, 10240], P(None, None, 'tensor'), may hold values from -1.5 to 1.5
- output_up_adapter: bfloat16 [32, 16, 8192], P(None, None, 'tensor'), may hold values from -1.5 to 1.5
- cache_keys: bfloat16 [128, 8, 384, 128], P(('groups', 'tensor')), parts along dimension 0, may hold values from -64 to 64
- cache_values: bfloat16 [128, 8, 384, 128], P(('groups', 'tensor')), parts along dimension 0, may hold values from -12 to 12
Outputs:
- attn_output: bfloat16 [128, 8192], P(('groups', 'tensor')), parts along dimension 0
The draws below stay inside these ranges and needn't reach their ends.
There are 2 independent parts, one for each index of `groups`. The reference program is written for one: setup_inputs(seed, part) draws one part's arguments, and reference() takes and returns one part's arrays. A program takes and returns all parts, laid end to end along the dimension named above; an argument that names none is the same for every part. Nothing has to cross between parts.
Inputs may be any that keep to these rules, and one draw needn't show every extreme that they name: `request_adapter`: among the requests of one replica no adapter is named more than 16 times, a bound that some block reaches. `lengths`: some request of every draw has all 384 positions filled.
All inputs are finite; a program needn't handle non-finite values.
Results may differ from the reference program's by a relative error of at most 0.012.
The reference program's roundings to bfloat16 on the way count: a program that leaves them out, or rounds other values in their place, can miss the bound.
Values may be sent and summed in bfloat16 or wider, within the bound.
No kernel may reach another device: no remote copies, remote signals or barrier semaphores. Data moves between devices by JAX's collectives and lax.ppermute only.
A program may use at most 128 MiB of HBM per device.

```python
import math
import jax
import jax.numpy as jnp
import numpy as np
from jax import lax

MODEL_DIM = 8192
HQ = 64
KVH = 8
HD = 128
ADAPTER_RANK = 16
CTX = 384
MOST = 16
QUERY_KEY_VALUE = 10240
REQUESTS = 64
ADAPTER_COUNT = 32


def draw_lengths(key, part):
    key = jax.random.fold_in(key, 11)
    first, second = jax.random.split(key)
    values = jax.random.randint(first, (REQUESTS,), 1, CTX + 1)
    longest = jax.random.randint(second, (), 0, REQUESTS)
    return jnp.where(jnp.arange(REQUESTS) == longest, CTX, values).astype(jnp.int32)


def draw_cache_keys(key, part):
    key = jax.random.fold_in(key, 23)
    first = jax.random.fold_in(key, 0)
    values = jnp.clip(jax.random.normal(first, (REQUESTS, KVH, CTX, HD), jnp.float32), -6.0, 6.0)
    return values.astype(jnp.bfloat16)


def level_of(rng, shape, pieces, low, top_value):
    loudness, own = 1.0, jax.random.fold_in(rng, 6)
    for axis_at, blocks in pieces:
        steps = jnp.exp(jax.random.uniform(jax.random.fold_in(own, axis_at), (blocks,), jnp.float32, low / len(pieces), top_value / len(pieces)))
        loudness = loudness * jnp.repeat(steps, shape[axis_at] // blocks).reshape([-1 if axis == axis_at else 1 for axis in range(len(shape))])
    return loudness


def shared_out(key, own, number, rows, number_of, top, limit, lean):
    sequence = jax.random.permutation(key, number_of)
    crowded, usual = load_shares(number_of, rows * top, limit, lean, True), load_shares(number_of, rows * top, limit, lean, False)
    places = jnp.arange(number_of)

    def named(tallies, offset_by):
        used = int((tallies > 0).sum())
        fixed = max(1, used // 4)
        passed = fixed + (places - fixed + offset_by * (used - fixed)) % max(1, number_of - fixed)
        return jnp.zeros((number_of,), jnp.int32).at[sequence[jnp.where(places < fixed, places, passed)]].set(jnp.asarray(tallies, jnp.int32))

    tallies = jnp.where(number % 4 == 0, named(crowded, number // 4), named(usual, number - number // 4 - 1))
    mixed = jax.random.permutation(jax.random.fold_in(own, 3), number_of)
    source_of, receiver = mixed[0:number_of // 2 * 2:2], mixed[1:number_of // 2 * 2:2]
    room = jnp.minimum(tallies[source_of] - 1, limit - tallies[receiver]) // 2
    room = jnp.where((source_of == sequence[0]) | (receiver == sequence[0]) | (tallies[receiver] == 0), 0, jnp.maximum(room, 0))
    passed = jax.random.randint(jax.random.fold_in(own, 4), (number_of // 2,), 0, 1 << 20) % (room + 1)
    tallies = tallies.at[source_of].add(-passed).at[receiver].add(passed)
    items = jnp.searchsorted(jnp.cumsum(tallies), jnp.arange(rows * top), side="right").astype(jnp.int32)
    listing = items.reshape(top, rows).T
    listing = listing[jax.random.permutation(jax.random.fold_in(own, 1), rows)]
    offset_by = jax.random.randint(jax.random.fold_in(own, 2), (rows, 1), 0, top)
    return jnp.take_along_axis(listing, (jnp.arange(top)[None, :] + offset_by) % top, axis=1)


def load_shares(number_of, total, limit, skew, full):
    loads = [(1 << 20) // math.isqrt(grade ** skew) + 1 for grade in range(1, number_of + 1)]
    largest = limit if full else min(limit, max(-(-total // number_of), total * loads[0] // sum(loads)))
    least = 1 if total - largest >= number_of - 1 else 0
    given, surplus = [largest] + [least] * (number_of - 1), total - largest - least * (number_of - 1)
    while surplus > 0:
        free = [i for i in range(1, number_of) if given[i] < largest] or [i for i in range(1, number_of) if given[i] < limit]
        pool, remaining = sum([loads[i] for i in free]), surplus
        for i in free:
            extra = min(limit - given[i], max(1, remaining * loads[i] // pool), surplus)
            given[i] = given[i] + extra
            surplus = surplus - extra
    return np.array(given)


def noise(own_key, shape, width, most, pieces=(), kind=jnp.bfloat16):
    level = level_of(own_key, shape, pieces, -0.22, 0.18) if pieces else 1.0
    array = jax.random.normal(own_key, shape, jnp.float32) * width * level
    return jnp.minimum(jnp.maximum(array, -most), most).astype(kind)


def setup_inputs(seed: int = 0, part: int = 0) -> dict:
    key_list = jax.random.split(jax.random.key(seed), 13)
    part_keys = jax.random.split(jax.random.fold_in(key_list[12], part), 13)
    input_hidden = noise(part_keys[0], (REQUESTS, MODEL_DIM), 1.0, 6.0, ((0, 16),))
    input_norm_gain = jnp.clip(1.0 + 0.18 * jax.random.normal(key_list[1], (MODEL_DIM,), jnp.float32), 0.099609375, 1.8984375).astype(jnp.bfloat16)
    request_adapter_keys = jax.random.split(jax.random.fold_in(part_keys[2], 1), REQUESTS // REQUESTS)
    request_adapter_turns = jax.random.permutation(jax.random.fold_in(part_keys[2], 3), REQUESTS // REQUESTS)
    request_adapter = jax.vmap(lambda own, number: shared_out(jax.random.fold_in(part_keys[2], 2), own, number, REQUESTS, ADAPTER_COUNT, 1, MOST, 2))(request_adapter_keys, request_adapter_turns).reshape((REQUESTS, 1))
    adapter_storage = jax.random.permutation(key_list[3], ADAPTER_COUNT).astype(jnp.int32)
    lengths = draw_lengths(jax.random.fold_in(jax.random.fold_in(key_list[12], part), 71), part)
    projection_weight = noise(key_list[5], (MODEL_DIM, QUERY_KEY_VALUE), MODEL_DIM ** -0.5, 0.0625, ((1, 16),))
    output_weight = noise(key_list[6], (MODEL_DIM, MODEL_DIM), MODEL_DIM ** -0.5, 0.0625, ((1, 16),))
    adapter_down = noise(key_list[7], (ADAPTER_COUNT, MODEL_DIM, 4 * ADAPTER_RANK), MODEL_DIM ** -0.5, 0.0625, ((0, 16),))
    projection_up_adapter = noise(key_list[8], (ADAPTER_COUNT, ADAPTER_RANK, QUERY_KEY_VALUE), ADAPTER_RANK ** -0.5, 1.5, ((2, 16),))
    output_up_adapter = noise(key_list[9], (ADAPTER_COUNT, ADAPTER_RANK, MODEL_DIM), ADAPTER_RANK ** -0.5, 1.5, ((2, 16),))
    cache_keys = draw_cache_keys(jax.random.fold_in(jax.random.fold_in(key_list[12], part), 71), part)
    cache_values = noise(part_keys[11], (REQUESTS, KVH, CTX, HD), 2.0, 12.0, ((0, 16),))
    return dict(input_hidden=input_hidden, input_norm_gain=input_norm_gain, request_adapter=request_adapter, adapter_storage=adapter_storage, lengths=lengths, projection_weight=projection_weight, output_weight=output_weight, adapter_down=adapter_down, projection_up_adapter=projection_up_adapter, output_up_adapter=output_up_adapter, cache_keys=cache_keys, cache_values=cache_values)


eps = 1e-05

def reference(input_hidden, input_norm_gain, request_adapter, adapter_storage, lengths, projection_weight, output_weight, adapter_down, projection_up_adapter, output_up_adapter, cache_keys, cache_values):
    hidden32 = input_hidden.astype(jnp.float32)
    power = lax.optimization_barrier(jnp.mean(hidden32 * hidden32, axis=1, keepdims=True))
    normed = (hidden32 * lax.rsqrt(power + eps) * input_norm_gain.astype(jnp.float32)).astype(jnp.bfloat16)
    chosen_ids = request_adapter[:, 0].astype(jnp.int32)
    slots = adapter_storage[chosen_ids].astype(jnp.int32)

    def down_qkv_one(pair):
        request_row, storage_slot = pair
        return jnp.dot(request_row, adapter_down[storage_slot][:, 0:3 * ADAPTER_RANK], preferred_element_type=jnp.float32)
    down_qkv = lax.map(down_qkv_one, (normed, slots)).astype(jnp.bfloat16)
    column_ids = jnp.arange(QUERY_KEY_VALUE, dtype=jnp.int32)
    segment = (column_ids >= MODEL_DIM).astype(jnp.int32) + (column_ids >= MODEL_DIM + KVH * HD).astype(jnp.int32)
    selector = (segment[None, :] == jnp.arange(3, dtype=jnp.int32)[:, None]).astype(jnp.float32)

    def lift_one(pair):
        row_down, adapter_name = pair
        lookup_table = projection_up_adapter[adapter_name].astype(jnp.float32)
        lifted = jnp.dot(row_down.astype(jnp.float32).reshape(3, ADAPTER_RANK), lookup_table)
        return lax.optimization_barrier(jnp.sum(lifted * selector, axis=0))
    base = jnp.dot(normed, projection_weight, preferred_element_type=jnp.float32)
    qkv = (base + lax.map(lift_one, (down_qkv, chosen_ids))).astype(jnp.bfloat16)
    groups_per = HQ // KVH
    query = qkv[:, 0:MODEL_DIM].reshape(REQUESTS, KVH, groups_per, HD)
    key_new = qkv[:, MODEL_DIM:MODEL_DIM + KVH * HD].reshape(REQUESTS, KVH, HD)
    value_new = qkv[:, MODEL_DIM + KVH * HD:].reshape(REQUESTS, KVH, HD)
    scale = HD ** (-0.5)

    def attend_one(items):
        query_row, key_row, value_row, keys, values, length = items
        query32 = query_row.astype(jnp.float32)
        scores = jnp.einsum('hgd,hpd->hgp', query32, keys.astype(jnp.float32)) * scale
        live = jnp.arange(CTX, dtype=jnp.int32) < length
        scores = jnp.where(live[None, None, :], scores, -1e+30)
        own = jnp.einsum('hgd,hd->hg', query32, key_row.astype(jnp.float32)) * scale
        peak = jnp.maximum(lax.optimization_barrier(jnp.max(scores, axis=2)), own)
        weights = jnp.exp(scores - peak[:, :, None])
        own_weight = jnp.exp(own - peak)
        total = lax.optimization_barrier(jnp.sum(weights, axis=2)) + own_weight
        probs = (weights / total[:, :, None]).astype(jnp.bfloat16)
        own_prob = (own_weight / total).astype(jnp.bfloat16)
        mixed = jnp.einsum('hgp,hpd->hgd', probs.astype(jnp.float32), values.astype(jnp.float32))
        mixed = mixed + own_prob.astype(jnp.float32)[:, :, None] * value_row.astype(jnp.float32)[:, None, :]
        return mixed.reshape(MODEL_DIM).astype(jnp.bfloat16)
    attended = lax.map(attend_one, (query, key_new, value_new, cache_keys, cache_values, lengths.astype(jnp.int32)))

    def down_out_one(pair):
        request_row, storage_slot = pair
        return jnp.dot(request_row, adapter_down[storage_slot][:, 3 * ADAPTER_RANK:4 * ADAPTER_RANK], preferred_element_type=jnp.float32)
    output_down = lax.map(down_out_one, (attended, slots)).astype(jnp.bfloat16)

    def lift_out_one(pair):
        row_down, adapter_name = pair
        return jnp.dot(row_down.astype(jnp.float32), output_up_adapter[adapter_name].astype(jnp.float32))
    projected = jnp.dot(attended, output_weight, preferred_element_type=jnp.float32) + lax.map(lift_out_one, (output_down, chosen_ids))
    return projected.astype(jnp.bfloat16)
```

```python
import jax
import jax.numpy as jnp
from jax import lax
from jax.sharding import PartitionSpec as P

eps = 1e-05
AXIS = "tensor"


def swap(x, count, offset):
    return lax.ppermute(x, AXIS, [(i, i ^ offset) for i in range(count)])


def gather_rows(x, count):
    step = count // 4
    held = [jnp.concatenate([x] + [swap(x, count, k * step) for k in (1, 2, 3)], axis=0)]
    order = [[0, step, 2 * step, 3 * step]]
    step //= 2
    while step:
        held = held + [swap(h, count, step) for h in held]
        order = order + [[j ^ step for j in o] for o in order]
        step //= 2
    return jnp.concatenate(held, axis=0), sum(order, [])


def sum_over(x, count):
    step = count
    while step > 1:
        radix = 4 if step % 4 == 0 else 2
        step //= radix
        others = [swap(x, count, k * step) for k in range(1, radix)]
        for other in others:
            x = x + other
    return x


def local(
    input_hidden,
    input_norm_gain,
    request_adapter,
    adapter_storage,
    lengths,
    projection_weight,
    output_weight,
    adapter_down,
    projection_up_adapter,
    output_up_adapter,
    cache_keys,
    cache_values,
    *,
    count,
):
    me = lax.axis_index(AXIS)
    model_width = input_hidden.shape[1]
    local_rows = input_hidden.shape[0]
    adapters, rank = projection_up_adapter.shape[:2]
    held = adapter_down.shape[0]
    kv_heads, context, head_dim = cache_keys.shape[1:]
    kv_width = kv_heads * head_dim
    total = local_rows * count

    hidden32 = input_hidden.astype(jnp.float32)
    power = jnp.mean(hidden32 * hidden32, axis=1, keepdims=True)
    normed = (hidden32 * lax.rsqrt(power + eps) * input_norm_gain.astype(jnp.float32)).astype(
        jnp.bfloat16
    )
    ids = jnp.broadcast_to(request_adapter.astype(jnp.bfloat16), (local_rows, 128))
    rows, order = gather_rows(jnp.concatenate([normed, ids], axis=1), count)
    ids = rows[:, model_width].astype(jnp.int32)
    normed_all = rows[:, :model_width]

    devices = me ^ jnp.array(order, jnp.int32)
    place = (devices[:, None] * local_rows + jnp.arange(local_rows, dtype=jnp.int32)).reshape(-1)
    to_place = (jnp.arange(total, dtype=jnp.int32)[:, None] == place[None, :]).astype(jnp.bfloat16)
    named = ids[:, None] == jnp.arange(adapters, dtype=jnp.int32)[None, :]
    slots = jnp.sum(jnp.where(named, adapter_storage[None, :], 0), axis=1)
    spread = jnp.repeat(named, rank, axis=1)

    def move(matrix, x):
        return jnp.dot(matrix, x, preferred_element_type=jnp.float32).astype(jnp.bfloat16)

    def downs(x, low, high):
        summed = jnp.zeros((total, high - low), jnp.float32)
        for s in range(held):
            product = jnp.dot(x, adapter_down[s, :, low:high], preferred_element_type=jnp.float32)
            summed = jnp.where((slots == me * held + s)[:, None], product, summed)
        mine = move(to_place, summed.astype(jnp.bfloat16))
        return move(to_place.T, sum_over(mine, count))

    def lift(down, up):
        wide = jnp.where(spread, jnp.tile(down, (1, adapters)), 0)
        return jnp.dot(
            wide, up.reshape(adapters * rank, up.shape[2]), preferred_element_type=jnp.float32
        )

    down_qkv = downs(normed_all, 0, 3 * rank)
    columns = projection_weight.shape[1]
    column_ids = me * columns + jnp.arange(columns, dtype=jnp.int32)
    segment = (column_ids >= model_width).astype(jnp.int32) + (
        column_ids >= model_width + kv_width
    ).astype(jnp.int32)
    base = jnp.dot(normed_all, projection_weight, preferred_element_type=jnp.float32)
    for g in range(3):
        lifted = lift(down_qkv[:, g * rank : (g + 1) * rank], projection_up_adapter)
        base = base + jnp.where((segment == g)[None, :], lifted, 0.0)
    qkv_columns = move(to_place, base.astype(jnp.bfloat16))
    qkv_mine = lax.all_to_all(qkv_columns, AXIS, split_axis=0, concat_axis=1, tiled=True)

    groups_per = model_width // head_dim // kv_heads
    query = qkv_mine[:, 0:model_width].reshape(local_rows, kv_heads, groups_per, head_dim)
    key_new = qkv_mine[:, model_width : model_width + kv_width].reshape(
        local_rows, kv_heads, head_dim
    )
    value_new = qkv_mine[:, model_width + kv_width :].reshape(local_rows, kv_heads, head_dim)
    scale = head_dim ** (-0.5)
    scores = (
        jnp.einsum("bhgd,bhpd->bhgp", query, cache_keys, preferred_element_type=jnp.float32) * scale
    )
    live = jnp.arange(context, dtype=jnp.int32)[None, :] < lengths[:, None]
    scores = jnp.where(live[:, None, None, :], scores, -1e30)
    own = jnp.einsum("bhgd,bhd->bhg", query, key_new, preferred_element_type=jnp.float32) * scale
    peak = jnp.maximum(jnp.max(scores, axis=3), own)
    weights = jnp.exp(scores - peak[..., None])
    own_weight = jnp.exp(own - peak)
    denominator = jnp.sum(weights, axis=3) + own_weight
    probs = (weights / denominator[..., None]).astype(jnp.bfloat16)
    own_prob = (own_weight / denominator).astype(jnp.bfloat16)
    mixed = jnp.einsum("bhgp,bhpd->bhgd", probs, cache_values, preferred_element_type=jnp.float32)
    mixed = (
        mixed
        + own_prob.astype(jnp.float32)[..., None] * value_new.astype(jnp.float32)[:, :, None, :]
    )
    attended = mixed.reshape(local_rows, model_width).astype(jnp.bfloat16)

    attended_all, _ = gather_rows(attended, count)
    output_down = downs(attended_all, 3 * rank, 4 * rank)
    projected = jnp.dot(attended_all, output_weight, preferred_element_type=jnp.float32)
    projected = projected + lift(output_down, output_up_adapter)
    sent = move(to_place, projected.astype(jnp.bfloat16))
    return lax.all_to_all(sent, AXIS, split_axis=0, concat_axis=1, tiled=True)


def solution(mesh):
    count = mesh.shape[AXIS]

    def body(*arrays):
        return local(*arrays, count=count)

    return jax.shard_map(
        body,
        mesh=mesh,
        in_specs=(
            P(("groups", "tensor"), None),
            P(),
            P(("groups", "tensor"), None),
            P(),
            P(("groups", "tensor")),
            P(None, "tensor"),
            P(None, "tensor"),
            P("tensor", None, None),
            P(None, None, "tensor"),
            P(None, None, "tensor"),
            P(("groups", "tensor"), None, None, None),
            P(("groups", "tensor"), None, None, None),
        ),
        out_specs=P(("groups", "tensor"), None),
        check_vma=False,
    )
```

```python
import functools

import jax
import jax.numpy as jnp
from jax import lax
from jax.experimental import pallas as pl
from jax.experimental.pallas import tpu as pltpu
from jax.sharding import PartitionSpec as P

eps = 1e-05
AXIS = "tensor"
LANES = 128
VMEM = pltpu.VMEM
SMEM = pltpu.SMEM


def swap(x, count, offset):
    return lax.ppermute(x, AXIS, [(i, i ^ offset) for i in range(count)])


def gather_rows(x, count):
    step = count // 4
    held = [jnp.concatenate([x] + [swap(x, count, k * step) for k in (1, 2, 3)], axis=0)]
    step //= 2
    while step:
        held = held + [swap(h, count, step) for h in held]
        step //= 2
    return held


def place_of(row, me, count, rows):
    block = row // rows
    source = (block % 4) * (count // 4)
    piece, step = block // 4, count // 8
    while step:
        source = source + (piece % 2) * step
        piece, step = piece // 2, step // 2
    return (source ^ me) * rows + row % rows


def limit(total):
    return (16 if total <= 64 else 60) * 1024 * 1024


def spec(space=VMEM):
    return pl.BlockSpec(memory_space=space)


def norm_kernel(hidden_ref, gain_ref, ids_ref, out_ref):
    rows, width = hidden_ref.shape
    hidden = hidden_ref[...].astype(jnp.float32)
    power = jnp.sum(hidden * hidden, axis=1, keepdims=True) / width
    gain = gain_ref[...].astype(jnp.float32)
    out_ref[:, :width] = (hidden * lax.rsqrt(power + eps) * gain).astype(jnp.bfloat16)
    row = lax.broadcasted_iota(jnp.int32, (rows, LANES), 0)
    ids = jnp.zeros((rows, LANES), jnp.float32)
    for r in range(rows):
        ids = jnp.where(row == r, ids_ref[r].astype(jnp.float32), ids)
    out_ref[:, width:] = ids.astype(jnp.bfloat16)


def down_kernel(count, rows, pieces, first, *refs):
    storage_ref, me_ref, down_ref = refs[:3]
    piece_refs, refs = refs[3 : 3 + pieces], refs[3 + pieces :]
    if first:
        out_ref, ids_out_ref = refs
    else:
        ids_ref, out_ref = refs
    total = count * rows
    held, rank, width = down_ref.shape
    me = me_ref[0]
    adapters = storage_ref.shape[0]
    if first:
        ids = jnp.concatenate([p[:, width:] for p in piece_refs], axis=0).astype(jnp.float32)
        ids_out_ref[...] = ids
    else:
        ids = ids_ref[...]
    chunk = 1024
    sums = [jnp.zeros((total, rank), jnp.float32) for _ in range(held)]
    for k in range(0, width, chunk):
        x = jnp.concatenate([p[:, k : k + chunk] for p in piece_refs], axis=0)
        for s in range(held):
            sums[s] = sums[s] + lax.dot_general(
                x,
                down_ref[s, :, k : k + chunk],
                (((1,), (1,)), ((), ())),
                preferred_element_type=jnp.float32,
            )
    chosen = jnp.zeros((total, rank), jnp.float32)
    for s in range(held):
        name = lax.fori_loop(
            0,
            adapters,
            lambda a, found, s=s: jnp.where(storage_ref[a] == me * held + s, a, found),
            jnp.int32(0),
        )
        chosen = jnp.where(ids[:, :rank] == name.astype(jnp.float32), sums[s], chosen)
    lane = lax.broadcasted_iota(jnp.int32, (total, total), 1)
    sub = lax.broadcasted_iota(jnp.int32, (total, total), 0)
    order = jnp.where(place_of(lane, me, count, rows) == sub, 1.0, 0.0).astype(jnp.bfloat16)
    out_ref[...] = jnp.dot(
        order, chosen.astype(jnp.bfloat16), preferred_element_type=jnp.float32
    ).astype(jnp.bfloat16)


def base_kernel(pieces, *refs):
    weight_ref, out_ref = refs[pieces], refs[pieces + 1]
    x = jnp.concatenate([p[...] for p in refs[:pieces]], axis=0)
    term = jnp.dot(x, weight_ref[...], preferred_element_type=jnp.float32)

    @pl.when(pl.program_id(0) == 0)
    def _():
        out_ref[...] = term

    @pl.when(pl.program_id(0) > 0)
    def _():
        out_ref[...] += term


def lift_kernel(count, rows, parts, bounds, *refs):
    me_ref, down_ref, ids_ref, up_ref = refs[:4]
    base_refs, out_ref = refs[4 : 4 + parts], refs[4 + parts]
    total = count * rows
    me = me_ref[0]
    adapters, rank, columns = up_ref.shape
    wide = adapters * rank
    value = base_refs[0][...]
    for b in base_refs[1:]:
        value = value + b[...]
    lane = lax.broadcasted_iota(jnp.int32, (total, total), 1)
    sub = lax.broadcasted_iota(jnp.int32, (total, total), 0)
    back = jnp.where(place_of(sub, me, count, rows) == lane, 1.0, 0.0).astype(jnp.bfloat16)
    order = jnp.where(place_of(lane, me, count, rows) == sub, 1.0, 0.0).astype(jnp.bfloat16)
    down = jnp.dot(back, down_ref[...], preferred_element_type=jnp.float32).astype(jnp.bfloat16)
    groups = down.shape[1] // rank
    up = up_ref[...].reshape(wide, columns)
    spread_at = lax.broadcasted_iota(jnp.int32, (groups * rank, wide), 1)
    spread_from = lax.broadcasted_iota(jnp.int32, (groups * rank, wide), 0)
    own = lax.broadcasted_iota(jnp.int32, (total, wide), 1) // rank
    named = own.astype(jnp.float32) == ids_ref[:, :1]
    column = lax.broadcasted_iota(jnp.int32, (total, columns), 1) + me * columns
    for g in range(groups):
        spread = jnp.where(spread_at % rank + g * rank == spread_from, 1.0, 0.0).astype(
            jnp.bfloat16
        )
        copies = jnp.dot(down, spread, preferred_element_type=jnp.float32)
        chosen = jnp.where(named, copies, 0.0).astype(jnp.bfloat16)
        lifted = jnp.dot(chosen, up, preferred_element_type=jnp.float32)
        low, high = bounds[g], bounds[g + 1]
        value = value + jnp.where((column >= low) & (column < high), lifted, 0.0)
    placed = jnp.dot(
        order, value.astype(jnp.bfloat16), preferred_element_type=jnp.float32
    ).astype(jnp.bfloat16)
    for d in range(count):
        out_ref[d] = placed[d * rows : (d + 1) * rows]


def local(
    input_hidden,
    input_norm_gain,
    request_adapter,
    adapter_storage,
    lengths,
    projection_weight,
    output_weight,
    adapter_down,
    projection_up_adapter,
    output_up_adapter,
    cache_keys,
    cache_values,
    *,
    count,
):
    me = lax.axis_index(AXIS).astype(jnp.int32).reshape(1)
    rows, width = input_hidden.shape
    rank = projection_up_adapter.shape[1]
    held = adapter_down.shape[0]
    kv_heads, context, head_dim = cache_keys.shape[1:]
    kv_width = kv_heads * head_dim
    total = rows * count
    params = pltpu.CompilerParams(vmem_limit_bytes=limit(total))
    down_maps = jnp.swapaxes(adapter_down, 1, 2)

    normed = pl.pallas_call(
        norm_kernel,
        out_shape=jax.ShapeDtypeStruct((rows, width + LANES), jnp.bfloat16),
        in_specs=[spec(), spec(), spec(SMEM)],
        out_specs=spec(),
        compiler_params=params,
        name="norm",
    )(input_hidden, input_norm_gain.reshape(1, width), request_adapter.reshape(rows))

    def downs(pieces, low, high, ids):
        ranks = high - low
        first = ids is None
        down_spec = pl.BlockSpec((held, ranks, width), lambda i: (0, low // ranks, 0))
        shapes = [jax.ShapeDtypeStruct((total, ranks), jnp.bfloat16)]
        if first:
            shapes.append(jax.ShapeDtypeStruct((total, LANES), jnp.float32))
        return pl.pallas_call(
            functools.partial(down_kernel, count, rows, len(pieces), first),
            grid=(1,),
            out_shape=shapes,
            in_specs=[spec(SMEM), spec(SMEM), down_spec]
            + [spec()] * (len(pieces) + (0 if first else 1)),
            out_specs=[spec()] * len(shapes),
            compiler_params=params,
            cost_estimate=pl.CostEstimate(
                flops=2 * total * width * held * ranks,
                bytes_accessed=2 * width * (held * ranks + total),
                transcendentals=0,
            ),
            name="down",
        )(adapter_storage, me, down_maps, *pieces, *([] if first else [ids]))

    def base(pieces, weight, part, parts):
        columns = weight.shape[1]
        chunk = 1024
        steps = width // chunk // parts
        piece_rows = pieces[0].shape[0]
        return pl.pallas_call(
            functools.partial(base_kernel, len(pieces)),
            grid=(steps,),
            out_shape=jax.ShapeDtypeStruct((total, columns), jnp.float32),
            in_specs=[pl.BlockSpec((piece_rows, chunk), lambda i: (0, part * steps + i))]
            * len(pieces)
            + [pl.BlockSpec((chunk, columns), lambda i: (part * steps + i, 0))],
            out_specs=pl.BlockSpec((total, columns), lambda i: (0, 0)),
            compiler_params=params,
            cost_estimate=pl.CostEstimate(
                flops=2 * total * width * columns // parts,
                bytes_accessed=2 * width * columns // parts,
                transcendentals=0,
            ),
            name="base",
        )(*pieces, weight)

    def lift(down, ids, up, bases, bounds):
        columns = up.shape[2]
        return pl.pallas_call(
            functools.partial(lift_kernel, count, rows, len(bases), bounds),
            out_shape=jax.ShapeDtypeStruct((count, rows, columns), jnp.bfloat16),
            in_specs=[spec(SMEM)] + [spec()] * (3 + len(bases)),
            out_specs=spec(),
            compiler_params=params,
            name="lift",
        )(me, down, ids, up, *bases)

    def project(pieces, ids, low, high, weight, up, bounds):
        down = downs(pieces, low, high, ids)
        if ids is None:
            down, ids = down
        else:
            (down,) = down
        parts, step, bases = 4, count, []
        part = 0
        while step > 1:
            step //= 2
            other = swap(down, count, step)
            if part < parts:
                bases.append(base(pieces, weight, part, parts))
                part += 1
            down = down + other
        columns = lift(down, ids, up, bases, bounds)
        mine = lax.all_to_all(columns, AXIS, split_axis=0, concat_axis=0, tiled=True)
        return jnp.swapaxes(mine, 0, 1).reshape(rows, -1), ids

    bounds = (0, width, width + kv_width, width + 2 * kv_width)
    qkv_mine, ids = project(
        gather_rows(normed, count),
        None,
        0,
        3 * rank,
        projection_weight,
        projection_up_adapter,
        bounds,
    )

    groups_per = width // head_dim // kv_heads
    query = qkv_mine[:, 0:width].reshape(rows, kv_heads, groups_per, head_dim)
    key_new = qkv_mine[:, width : width + kv_width].reshape(rows, kv_heads, head_dim)
    value_new = qkv_mine[:, width + kv_width :].reshape(rows, kv_heads, head_dim)
    scale = head_dim ** (-0.5)
    scores = (
        jnp.einsum("bhgd,bhpd->bhgp", query, cache_keys, preferred_element_type=jnp.float32) * scale
    )
    live = jnp.arange(context, dtype=jnp.int32)[None, :] < lengths[:, None]
    scores = jnp.where(live[:, None, None, :], scores, -1e30)
    own = jnp.einsum("bhgd,bhd->bhg", query, key_new, preferred_element_type=jnp.float32) * scale
    peak = jnp.maximum(jnp.max(scores, axis=3), own)
    weights = jnp.exp(scores - peak[..., None])
    own_weight = jnp.exp(own - peak)
    denominator = jnp.sum(weights, axis=3) + own_weight
    probs = (weights / denominator[..., None]).astype(jnp.bfloat16)
    own_prob = (own_weight / denominator).astype(jnp.bfloat16)
    mixed = jnp.einsum("bhgp,bhpd->bhgd", probs, cache_values, preferred_element_type=jnp.float32)
    mixed = (
        mixed
        + own_prob.astype(jnp.float32)[..., None] * value_new.astype(jnp.float32)[:, :, None, :]
    )
    attended = mixed.reshape(rows, width).astype(jnp.bfloat16)

    output, _ = project(
        gather_rows(attended, count),
        ids,
        3 * rank,
        4 * rank,
        output_weight,
        output_up_adapter,
        (0, width),
    )
    return output


def solution(mesh):
    count = mesh.shape[AXIS]

    def body(*arrays):
        return local(*arrays, count=count)

    return jax.shard_map(
        body,
        mesh=mesh,
        in_specs=(
            P(("groups", "tensor"), None),
            P(),
            P(("groups", "tensor"), None),
            P(),
            P(("groups", "tensor")),
            P(None, "tensor"),
            P(None, "tensor"),
            P("tensor", None, None),
            P(None, None, "tensor"),
            P(None, None, "tensor"),
            P(("groups", "tensor"), None, None, None),
            P(("groups", "tensor"), None, None, None),
        ),
        out_specs=P(("groups", "tensor"), None),
        check_vma=False,
    )
```

```python
import functools

import jax
import jax.numpy as jnp
from jax import lax
from jax.experimental import pallas as pl
from jax.experimental.pallas import tpu as pltpu
from jax.sharding import PartitionSpec as P

eps = 1e-05
AXIS = "tensor"
LANES = 128
VMEM = pltpu.VMEM
SMEM = pltpu.SMEM


def swap(x, count, offset):
    return lax.ppermute(x, AXIS, [(i, i ^ offset) for i in range(count)])


def exchange(x, groups=None):
    return lax.all_to_all(
        x, AXIS, split_axis=0, concat_axis=0, axis_index_groups=groups, tiled=True
    )


def gather_rows(x, count):
    step = count // 4
    far, middle, near = (swap(x, count, k * step) for k in (3, 2, 1))
    parts = [x, near, middle, far]
    step //= 2
    held = [jnp.concatenate(parts, axis=0)]
    if step:
        across = [swap(p, count, step) for p in (x, far, near, middle)]
        held.append(jnp.concatenate([across[i] for i in (0, 2, 3, 1)], axis=0))
        step //= 2
    while step:
        held = held + [swap(h, count, step) for h in held]
        step //= 2
    return held


def place_of(row, me, count, rows):
    block = row // rows
    source = (block % 4) * (count // 4)
    piece, step = block // 4, count // 8
    while step:
        source = source + (piece % 2) * step
        piece, step = piece // 2, step // 2
    return (source ^ me) * rows + row % rows


def limit(total):
    return (10 if total <= 64 else 60) * 1024 * 1024


def spec(space=VMEM):
    return pl.BlockSpec(memory_space=space)


def iota(shape, dim):
    return lax.broadcasted_iota(jnp.int32, shape, dim)


def one_hot(condition):
    return jnp.where(condition, 1.0, 0.0).astype(jnp.bfloat16)


def setup_kernel(count, rows, held, storage_ref, order_ref, back_ref, names_ref):
    total = count * rows
    me = lax.axis_index(AXIS)
    row, column = iota((total, total), 0), iota((total, total), 1)
    order_ref[...] = one_hot(place_of(column, me, count, rows) == row)
    back_ref[...] = one_hot(place_of(row, me, count, rows) == column)
    for s in range(held):
        name = lax.fori_loop(
            0,
            storage_ref.shape[0],
            lambda a, found, s=s: jnp.where(storage_ref[a] == me * held + s, a, found),
            jnp.int32(0),
        )
        names_ref[s] = jnp.full((8, LANES), name, jnp.int32).astype(jnp.float32)


def norm_kernel(hidden_hbm, gain_hbm, ids_hbm, out_ref, hidden_ref, gain_ref, ids_ref, sems):
    copies = [
        pltpu.make_async_copy(source, target, sems.at[i])
        for i, (source, target) in enumerate(
            ((hidden_hbm, hidden_ref), (gain_hbm, gain_ref), (ids_hbm, ids_ref))
        )
    ]
    for copy in copies:
        copy.start()
    for copy in copies:
        copy.wait()
    rows, width = hidden_ref.shape
    hidden = hidden_ref[...].astype(jnp.float32)
    power = jnp.sum(hidden * hidden, axis=1, keepdims=True) / width
    gain = gain_ref[...].reshape(1, width).astype(jnp.float32)
    out_ref[:, :width] = (hidden * lax.rsqrt(power + eps) * gain).astype(jnp.bfloat16)
    row = iota((rows, LANES), 0)
    ids = jnp.zeros((rows, LANES), jnp.float32)
    for r in range(rows):
        ids = jnp.where(row == r, ids_ref[r].astype(jnp.float32), ids)
    out_ref[:, width:] = ids.astype(jnp.bfloat16)


NT = (((1,), (1,)), ((), ()))


def down_kernel(pieces, first, *refs):
    names_ref, back_ref, down_ref = refs[:3]
    piece_refs, refs = refs[3 : 3 + pieces], refs[3 + pieces :]
    if first:
        out_ref, ids_out_ref = refs
    else:
        ids_ref, out_ref = refs
    total = back_ref.shape[0]
    held, rank, width = down_ref.shape
    if first:
        ids = jnp.concatenate([p[:, width:] for p in piece_refs], axis=0)
        ids_out_ref[...] = ids
    else:
        ids = ids_ref[...]
    chunk = 1024
    sums = jnp.zeros((held * rank, total), jnp.float32)
    for k in range(0, width, chunk):
        x = jnp.concatenate([p[:, k : k + chunk] for p in piece_refs], axis=0)
        maps = down_ref[:, :, k : k + chunk].reshape(held * rank, chunk)
        sums = sums + lax.dot_general(maps, x, NT, preferred_element_type=jnp.float32)
    first_lane = one_hot(iota((16, LANES), 1) == 0)
    across = lax.dot_general(first_lane, ids, NT, preferred_element_type=jnp.float32)
    chosen = jnp.zeros((rank, total), jnp.float32)
    for s in range(held):
        mine = across[:1] == names_ref[s, :1, :1]
        chosen = jnp.where(mine, sums[s * rank : (s + 1) * rank], chosen)
    placed = jnp.dot(
        chosen.astype(jnp.bfloat16), back_ref[...], preferred_element_type=jnp.float32
    )
    lanes = out_ref.shape[2]
    folds = lanes // total
    part = rank // folds
    folded = [placed[f * part : (f + 1) * part] for f in range(folds)]
    value = jnp.concatenate(folded, axis=1).astype(jnp.bfloat16)
    for d in range(out_ref.shape[0]):
        out_ref[d] = value


def base_kernel(pieces, *refs):
    weight_ref, out_ref = refs[pieces], refs[pieces + 1]
    x = jnp.concatenate([p[...] for p in refs[:pieces]], axis=0)
    columns = weight_ref.shape[1]
    for c in range(0, columns, 512):
        at = slice(c, min(c + 512, columns))
        term = jnp.dot(x, weight_ref[:, at], preferred_element_type=jnp.float32)

        @pl.when(pl.program_id(0) == 0)
        def _():
            out_ref[:, at] = term

        @pl.when(pl.program_id(0) > 0)
        def _():
            out_ref[:, at] += term


def lift_kernel(rows, bounds, rank, *refs):
    down_ref, ids_ref, order_ref, back_ref, up_ref, base_ref, out_ref, sum_ref = refs
    total = order_ref.shape[0]
    me = lax.axis_index(AXIS)
    adapters, per, columns = up_ref.shape
    wide = adapters * per
    folded = down_ref[0].astype(jnp.float32)
    for d in range(1, down_ref.shape[0]):
        folded = folded + down_ref[d].astype(jnp.float32)
    folds = folded.shape[1] // total
    down = jnp.concatenate([folded[:, f * total : (f + 1) * total] for f in range(folds)], axis=0)
    down = lax.dot_general(
        back_ref[...], down.astype(jnp.bfloat16), NT, preferred_element_type=jnp.float32
    ).astype(jnp.bfloat16)
    named = (iota((total, wide), 1) // per).astype(jnp.float32) == ids_ref[:, :1].astype(
        jnp.float32
    )
    start = me * columns
    sum_ref[...] = base_ref[...]
    for g in range(rank // per):
        low, high = bounds[g], bounds[g + 1]

        @pl.when((start < high) & (start + columns > low))
        def _():
            at = iota((rank, wide), 1) % per + g * per
            spread = one_hot(at == iota((rank, wide), 0))
            copies = jnp.dot(down, spread, preferred_element_type=jnp.float32)
            chosen = jnp.where(named, copies, 0.0).astype(jnp.bfloat16)
            for c in range(0, columns, 512):
                end = min(c + 512, columns)
                up = up_ref[:, :, c:end].reshape(wide, end - c)
                lifted = jnp.dot(chosen, up, preferred_element_type=jnp.float32)
                column = iota((total, end - c), 1) + (start + c)
                inside = (column >= low) & (column < high)
                sum_ref[:, c:end] += jnp.where(inside, lifted, 0.0)

    placed = jnp.dot(
        order_ref[...], sum_ref[...].astype(jnp.bfloat16), preferred_element_type=jnp.float32
    ).astype(jnp.bfloat16)
    for d in range(total // rows):
        out_ref[d] = placed[d * rows : (d + 1) * rows]


def local(
    input_hidden,
    input_norm_gain,
    request_adapter,
    adapter_storage,
    lengths,
    projection_weight,
    output_weight,
    adapter_down,
    projection_up_adapter,
    output_up_adapter,
    cache_keys,
    cache_values,
    *,
    count,
):
    rows, width = input_hidden.shape
    rank = projection_up_adapter.shape[1]
    held = adapter_down.shape[0]
    kv_heads, context, head_dim = cache_keys.shape[1:]
    kv_width = kv_heads * head_dim
    total = rows * count
    params = pltpu.CompilerParams(vmem_limit_bytes=limit(total))
    down_maps = jnp.swapaxes(adapter_down, 1, 2)
    bf16, f32 = jnp.bfloat16, jnp.float32

    normed = pl.pallas_call(
        norm_kernel,
        out_shape=jax.ShapeDtypeStruct((rows, width + LANES), bf16),
        in_specs=[spec(pltpu.HBM)] * 3,
        out_specs=spec(),
        scratch_shapes=[
            VMEM((rows, width), bf16),
            VMEM((width,), bf16),
            SMEM((rows,), jnp.int32),
            pltpu.SemaphoreType.DMA((3,)),
        ],
        compiler_params=params,
        name="norm",
    )(input_hidden, input_norm_gain, request_adapter.reshape(rows))

    order, back, names = pl.pallas_call(
        functools.partial(setup_kernel, count, rows, held),
        out_shape=[
            jax.ShapeDtypeStruct((total, total), bf16),
            jax.ShapeDtypeStruct((total, total), bf16),
            jax.ShapeDtypeStruct((held, 8, LANES), f32),
        ],
        in_specs=[spec(SMEM)],
        out_specs=[spec()] * 3,
        compiler_params=params,
        name="setup",
    )(adapter_storage)

    def downs(pieces, low, high, ids, copies):
        ranks = high - low
        first = ids is None
        lanes = max(LANES, total)
        down_spec = pl.BlockSpec((held, ranks, width), lambda i: (0, low // ranks, 0))
        shapes = [jax.ShapeDtypeStruct((copies, ranks * total // lanes, lanes), bf16)]
        if first:
            shapes.append(jax.ShapeDtypeStruct((total, LANES), bf16))
        return pl.pallas_call(
            functools.partial(down_kernel, len(pieces), first),
            grid=(1,),
            out_shape=shapes,
            in_specs=[spec(), spec(), down_spec]
            + [spec()] * (len(pieces) + (0 if first else 1)),
            out_specs=[spec()] * len(shapes),
            compiler_params=params,
            cost_estimate=pl.CostEstimate(
                flops=2 * total * width * held * ranks,
                bytes_accessed=2 * width * (held * ranks + total),
                transcendentals=0,
            ),
            name="down",
        )(names, back, down_maps, *pieces, *([] if first else [ids]))

    def base(pieces, weight):
        columns = weight.shape[1]
        chunk = 1024
        piece_rows = pieces[0].shape[0]
        return pl.pallas_call(
            functools.partial(base_kernel, len(pieces)),
            grid=(width // chunk,),
            out_shape=jax.ShapeDtypeStruct((total, columns), f32),
            in_specs=[pl.BlockSpec((piece_rows, chunk), lambda i: (0, i))] * len(pieces)
            + [pl.BlockSpec((chunk, columns), lambda i: (i, 0))],
            out_specs=pl.BlockSpec((total, columns), lambda i: (0, 0)),
            compiler_params=params,
            cost_estimate=pl.CostEstimate(
                flops=2 * total * width * columns,
                bytes_accessed=2 * width * columns,
                transcendentals=0,
            ),
            name="base",
        )(*pieces, weight)

    def lift(down, ids, up, base_term, bounds, ranks):
        columns = up.shape[2]
        return pl.pallas_call(
            functools.partial(lift_kernel, rows, bounds, ranks),
            out_shape=jax.ShapeDtypeStruct((count, rows, columns), bf16),
            in_specs=[spec()] * 6,
            out_specs=spec(),
            scratch_shapes=[VMEM((total, columns), f32)],
            compiler_params=params,
            name="lift",
        )(down, ids, order, back, up, base_term)

    def project(pieces, ids, low, high, weight, up, bounds):
        if ids is None:
            down, ids = downs(pieces, low, high, ids, count)
            down = exchange(down)
        else:
            outer = [[i + j for i in range(0, count, 4)] for j in range(4)]
            inner = [[i + j for j in range(4)] for i in range(0, count, 4)]
            (down,) = downs(pieces, low, high, ids, count // 4)
            down = jnp.sum(exchange(down, outer).astype(f32), axis=0).astype(bf16)
            down = exchange(jnp.broadcast_to(down[None], (4,) + down.shape), inner)
        base_term = base(pieces, weight)
        columns = lift(down, ids, up, base_term, bounds, high - low)
        mine = exchange(columns)
        return jnp.swapaxes(mine, 0, 1).reshape(rows, -1), ids

    bounds = (0, width, width + kv_width, width + 2 * kv_width)
    qkv_mine, ids = project(
        gather_rows(normed, count),
        None,
        0,
        3 * rank,
        projection_weight,
        projection_up_adapter,
        bounds,
    )

    groups_per = width // head_dim // kv_heads
    query = qkv_mine[:, 0:width].reshape(rows, kv_heads, groups_per, head_dim)
    key_new = qkv_mine[:, width : width + kv_width].reshape(rows, kv_heads, head_dim)
    value_new = qkv_mine[:, width + kv_width :].reshape(rows, kv_heads, head_dim)
    scale = head_dim ** (-0.5)
    scores = (
        jnp.einsum("bhgd,bhpd->bhgp", query, cache_keys, preferred_element_type=jnp.float32) * scale
    )
    live = jnp.arange(context, dtype=jnp.int32)[None, :] < lengths[:, None]
    scores = jnp.where(live[:, None, None, :], scores, -1e30)
    own = jnp.einsum("bhgd,bhd->bhg", query, key_new, preferred_element_type=jnp.float32) * scale
    peak = jnp.maximum(jnp.max(scores, axis=3), own)
    weights = jnp.exp(scores - peak[..., None])
    own_weight = jnp.exp(own - peak)
    denominator = jnp.sum(weights, axis=3) + own_weight
    probs = (weights / denominator[..., None]).astype(jnp.bfloat16)
    own_prob = (own_weight / denominator).astype(jnp.bfloat16)
    mixed = jnp.einsum("bhgp,bhpd->bhgd", probs, cache_values, preferred_element_type=jnp.float32)
    mixed = (
        mixed
        + own_prob.astype(jnp.float32)[..., None] * value_new.astype(jnp.float32)[:, :, None, :]
    )
    attended = mixed.reshape(rows, width).astype(jnp.bfloat16)

    output, _ = project(
        gather_rows(attended, count),
        ids,
        3 * rank,
        4 * rank,
        output_weight,
        output_up_adapter,
        (0, width),
    )
    return output


def solution(mesh):
    count = mesh.shape[AXIS]

    def body(*arrays):
        return local(*arrays, count=count)

    return jax.shard_map(
        body,
        mesh=mesh,
        in_specs=(
            P(("groups", "tensor"), None),
            P(),
            P(("groups", "tensor"), None),
            P(),
            P(("groups", "tensor")),
            P(None, "tensor"),
            P(None, "tensor"),
            P("tensor", None, None),
            P(None, None, "tensor"),
            P(None, None, "tensor"),
            P(("groups", "tensor"), None, None, None),
            P(("groups", "tensor"), None, None, None),
        ),
        out_specs=P(("groups", "tensor"), None),
        check_vma=False,
    )
```

```python
import functools

import jax
import jax.numpy as jnp
from jax import lax
from jax.experimental import pallas as pl
from jax.experimental.pallas import tpu as pltpu
from jax.sharding import PartitionSpec as P

eps = 1e-05
AXIS = "tensor"
LANES = 128
VMEM = pltpu.VMEM
SMEM = pltpu.SMEM


def swap(x, count, offset):
    return lax.ppermute(x, AXIS, [(i, i ^ offset) for i in range(count)])


def exchange(x, groups=None):
    return lax.all_to_all(
        x, AXIS, split_axis=0, concat_axis=0, axis_index_groups=groups, tiled=True
    )


def gather_rows(x, count):
    step = count // 4
    far, middle, near = (swap(x, count, k * step) for k in (3, 2, 1))
    step //= 2
    held = [jnp.concatenate([x, near, middle, far], axis=0)]
    across = [swap(p, count, step) for p in (x, far, near, middle)]
    held.append(jnp.concatenate([across[i] for i in (0, 2, 3, 1)], axis=0))
    step //= 2
    while step > 1:
        held = held + [swap(h, count, step) for h in held]
        step //= 2
    return held, held + [swap(h, count, 1) for h in held]


def place_of(row, me, count, rows):
    block = row // rows
    source = (block % 4) * (count // 4)
    piece, step = block // 4, count // 8
    while step:
        source = source + (piece % 2) * step
        piece, step = piece // 2, step // 2
    return (source ^ me) * rows + row % rows


def limit(total, room):
    if not room:
        return 60 * 1024 * 1024
    return (16 if total <= 64 else 60) * 1024 * 1024


def spec(space=VMEM):
    return pl.BlockSpec(memory_space=space)


def iota(shape, dim):
    return lax.broadcasted_iota(jnp.int32, shape, dim)


def one_hot(condition):
    return jnp.where(condition, 1.0, 0.0).astype(jnp.bfloat16)


def norm_kernel(
    hidden_hbm, gain_hbm, names_hbm, slots_hbm, out_ref, hidden_ref, gain_ref, names_ref, slots_ref, sems
):
    copies = [
        pltpu.make_async_copy(source, target, sems.at[i])
        for i, (source, target) in enumerate(
            (
                (hidden_hbm, hidden_ref),
                (gain_hbm, gain_ref),
                (names_hbm, names_ref),
                (slots_hbm, slots_ref),
            )
        )
    ]
    for copy in copies:
        copy.start()
    for copy in copies:
        copy.wait()
    rows, width = hidden_ref.shape
    hidden = hidden_ref[...].astype(jnp.float32)
    power = jnp.sum(hidden * hidden, axis=1, keepdims=True) / width
    gain = gain_ref[...].reshape(1, width).astype(jnp.float32)
    out_ref[:, :width] = (hidden * lax.rsqrt(power + eps) * gain).astype(jnp.bfloat16)
    row, lane = iota((rows, LANES), 0), iota((rows, LANES), 1)
    tags = jnp.zeros((rows, LANES), jnp.float32)
    for r in range(rows):
        name = names_ref[r]
        tag = jnp.where(lane < LANES // 2, name, slots_ref[name]).astype(jnp.float32)
        tags = jnp.where(row == r, tag, tags)
    out_ref[:, width:] = tags.astype(jnp.bfloat16)


NT = (((1,), (1,)), ((), ()))


def down_kernel(count, rows, pieces, *refs):
    map_refs, piece_refs = refs[:2], refs[2 : 2 + pieces]
    tag_refs, out_ref = refs[2 + pieces : 2 + 2 * pieces], refs[2 + 2 * pieces]
    me = lax.axis_index(AXIS)
    held, rank, width = map_refs[0].shape
    total, half = count * rows, count * rows // 2
    chunk = 1024
    sums = jnp.zeros((2 * held * rank, half), jnp.float32)
    for k in range(0, width, chunk):
        x = jnp.concatenate([p[:, k : k + chunk] for p in piece_refs], axis=0)
        maps = jnp.concatenate(
            [m[:, :, k : k + chunk].reshape(held * rank, chunk) for m in map_refs], axis=0
        )
        sums = sums + lax.dot_general(maps, x, NT, preferred_element_type=jnp.float32)
    tags = jnp.concatenate([t[...] for t in tag_refs], axis=0)
    pick = one_hot(iota((16, LANES), 1) == LANES // 2)
    slots = lax.dot_general(pick, tags, NT, preferred_element_type=jnp.float32)[:1]
    chosen = jnp.zeros((rank, half), jnp.float32)
    for m in range(2):
        for s in range(held):
            slot = ((me ^ m) * held + s).astype(jnp.float32)
            at = (m * held + s) * rank
            chosen = jnp.where(slots == slot, sums[at : at + rank], chosen)
    row, column = iota((half, total), 0), iota((half, total), 1)
    back = one_hot(place_of(row, me, count, rows) == column)
    placed = jnp.dot(chosen.astype(jnp.bfloat16), back, preferred_element_type=jnp.float32)
    folds = out_ref.shape[2] // total
    part = rank // folds
    folded = [placed[f * part : (f + 1) * part] for f in range(folds)]
    value = jnp.concatenate(folded, axis=1).astype(jnp.bfloat16)
    for d in range(count):
        out_ref[d] = value


def base_kernel(pieces, *refs):
    weight_ref, _, out_ref = refs[pieces:]
    x = jnp.concatenate([p[...] for p in refs[:pieces]], axis=0)
    total, depth = x.shape
    columns = weight_ref.shape[1]
    whole = columns // 256 * 256
    terms = []
    if whole:
        terms.append(jnp.dot(x, weight_ref[:, :whole], preferred_element_type=jnp.float32))
    if columns - whole == 128:
        half = depth // 2
        left = jnp.concatenate([x[:, :half], x[:, half:]], axis=0)
        right = jnp.concatenate(
            [weight_ref[:half, whole:], weight_ref[half:, whole:]], axis=1
        )
        both = jnp.dot(left, right, preferred_element_type=jnp.float32)
        terms.append(both[:total, :128] + both[total:, 128:])
    elif columns > whole:
        terms.append(jnp.dot(x, weight_ref[:, whole:], preferred_element_type=jnp.float32))
    term = terms[0] if len(terms) == 1 else jnp.concatenate(terms, axis=1)

    @pl.when(pl.program_id(0) == 0)
    def _():
        out_ref[...] = term

    @pl.when(pl.program_id(0) > 0)
    def _():
        out_ref[...] += term


def lift_kernel(count, rows, pieces, bounds, rank, *refs):
    tag_refs, refs = refs[:pieces], refs[pieces:]
    down_ref, up_ref, base_ref, out_ref, sum_ref = refs
    total = count * rows
    me = lax.axis_index(AXIS)
    adapters, per, columns = up_ref.shape
    wide = adapters * per
    row, column = iota((total, total), 0), iota((total, total), 1)
    order = one_hot(place_of(column, me, count, rows) == row)
    back = one_hot(place_of(row, me, count, rows) == column)
    folded = down_ref[0].astype(jnp.float32)
    for d in range(1, count):
        folded = folded + down_ref[d].astype(jnp.float32)
    folds = folded.shape[1] // total
    down = jnp.concatenate([folded[:, f * total : (f + 1) * total] for f in range(folds)], axis=0)
    down = lax.dot_general(
        back, down.astype(jnp.bfloat16), NT, preferred_element_type=jnp.float32
    ).astype(jnp.bfloat16)
    names = jnp.concatenate([t[...] for t in tag_refs], axis=0).astype(jnp.float32)[:, :1]
    named = (iota((total, wide), 1) // per).astype(jnp.float32) == names
    start = me * columns
    sum_ref[...] = base_ref[...]
    for g in range(rank // per):
        low, high = bounds[g], bounds[g + 1]

        @pl.when((start < high) & (start + columns > low))
        def _():
            at = iota((rank, wide), 1) % per + g * per
            spread = one_hot(at == iota((rank, wide), 0))
            copies = jnp.dot(down, spread, preferred_element_type=jnp.float32)
            chosen = jnp.where(named, copies, 0.0).astype(jnp.bfloat16)
            up = up_ref[...].reshape(wide, columns)
            lifted = jnp.dot(chosen, up, preferred_element_type=jnp.float32)
            at = iota((total, columns), 1) + start
            sum_ref[...] += jnp.where((at >= low) & (at < high), lifted, 0.0)

    placed = jnp.dot(
        order, sum_ref[...].astype(jnp.bfloat16), preferred_element_type=jnp.float32
    ).astype(jnp.bfloat16)
    for d in range(count):
        out_ref[d] = placed[d * rows : (d + 1) * rows]


def local(
    input_hidden,
    input_norm_gain,
    request_adapter,
    adapter_storage,
    lengths,
    projection_weight,
    output_weight,
    adapter_down,
    projection_up_adapter,
    output_up_adapter,
    cache_keys,
    cache_values,
    *,
    count,
):
    rows, width = input_hidden.shape
    rank = projection_up_adapter.shape[1]
    held = adapter_down.shape[0]
    kv_heads, context, head_dim = cache_keys.shape[1:]
    kv_width = kv_heads * head_dim
    total = rows * count
    bf16, f32 = jnp.bfloat16, jnp.float32
    roomy = pltpu.CompilerParams(vmem_limit_bytes=limit(total, True))
    full = pltpu.CompilerParams(vmem_limit_bytes=limit(total, False))
    own_maps = jnp.swapaxes(adapter_down, 1, 2)
    sibling_maps = jnp.swapaxes(swap(adapter_down, count, 1), 1, 2)

    normed = pl.pallas_call(
        norm_kernel,
        out_shape=jax.ShapeDtypeStruct((rows, width + LANES), bf16),
        in_specs=[spec(pltpu.HBM)] * 4,
        out_specs=spec(),
        scratch_shapes=[
            VMEM((rows, width), bf16),
            VMEM((width,), bf16),
            SMEM((rows,), jnp.int32),
            SMEM(adapter_storage.shape, jnp.int32),
            pltpu.SemaphoreType.DMA((4,)),
        ],
        compiler_params=full,
        cost_estimate=pl.CostEstimate(flops=0, bytes_accessed=1 << 24, transcendentals=0),
        name="norm",
    )(input_hidden, input_norm_gain, request_adapter.reshape(rows), adapter_storage)

    def tag_specs(pieces):
        return [pl.BlockSpec((p.shape[0], LANES), lambda i: (0, width // LANES)) for p in pieces]

    def downs(pieces, tagged, low, high):
        ranks = high - low
        lanes = max(LANES, total)
        down_spec = pl.BlockSpec((held, ranks, width), lambda i: (0, low // ranks, 0))
        return pl.pallas_call(
            functools.partial(down_kernel, count, rows, len(pieces)),
            grid=(1,),
            out_shape=jax.ShapeDtypeStruct((count, ranks * total // lanes, lanes), bf16),
            in_specs=[down_spec] * 2
            + [pl.BlockSpec((p.shape[0], width), lambda i: (0, 0)) for p in pieces]
            + tag_specs(tagged),
            out_specs=spec(),
            compiler_params=roomy,
            cost_estimate=pl.CostEstimate(
                flops=2 * total * width * held * ranks,
                bytes_accessed=2 * width * (2 * held * ranks + total),
                transcendentals=0,
            ),
            name="down",
        )(own_maps, sibling_maps, *pieces, *tagged)

    def base(pieces, weight, after):
        columns = weight.shape[1]
        chunk = 1024
        return pl.pallas_call(
            functools.partial(base_kernel, len(pieces)),
            grid=(width // chunk,),
            out_shape=jax.ShapeDtypeStruct((total, columns), f32),
            in_specs=[pl.BlockSpec((p.shape[0], chunk), lambda i: (0, i)) for p in pieces]
            + [pl.BlockSpec((chunk, columns), lambda i: (i, 0)), spec(pl.ANY)],
            out_specs=pl.BlockSpec((total, columns), lambda i: (0, 0)),
            compiler_params=full,
            cost_estimate=pl.CostEstimate(
                flops=2 * total * width * columns,
                bytes_accessed=2 * width * columns,
                transcendentals=0,
            ),
            name="base",
        )(*pieces, weight, after)

    def lift(down, tagged, up, base_term, bounds, ranks):
        columns = up.shape[2]
        whole = lambda x: pl.BlockSpec(x.shape, lambda i: (0,) * x.ndim)
        return pl.pallas_call(
            functools.partial(lift_kernel, count, rows, len(tagged), bounds, ranks),
            grid=(1,),
            out_shape=jax.ShapeDtypeStruct((count, rows, columns), bf16),
            in_specs=tag_specs(tagged) + [whole(down), whole(up), whole(base_term)],
            out_specs=pl.BlockSpec((count, rows, columns), lambda i: (0, 0, 0)),
            scratch_shapes=[VMEM((total, columns), f32)],
            compiler_params=full,
            name="lift",
        )(*tagged, down, up, base_term)

    def project(x, tagged, low, high, weight, up, bounds):
        column, pieces = gather_rows(x, count)
        tagged = pieces if tagged is None else tagged
        mine = downs(column, tagged[: len(column)], low, high)
        down = exchange(mine)
        base_term = base(pieces, weight, mine)
        columns = lift(down, tagged, up, base_term, bounds, high - low)
        mine = exchange(columns)
        return jnp.swapaxes(mine, 0, 1).reshape(rows, -1), tagged

    bounds = (0, width, width + kv_width, width + 2 * kv_width)
    qkv_mine, tagged = project(
        normed, None, 0, 3 * rank, projection_weight, projection_up_adapter, bounds
    )

    groups_per = width // head_dim // kv_heads
    query = qkv_mine[:, 0:width].reshape(rows, kv_heads, groups_per, head_dim)
    key_new = qkv_mine[:, width : width + kv_width].reshape(rows, kv_heads, head_dim)
    value_new = qkv_mine[:, width + kv_width :].reshape(rows, kv_heads, head_dim)
    scale = head_dim ** (-0.5)
    scores = (
        jnp.einsum("bhgd,bhpd->bhgp", query, cache_keys, preferred_element_type=jnp.float32) * scale
    )
    live = jnp.arange(context, dtype=jnp.int32)[None, :] < lengths[:, None]
    scores = jnp.where(live[:, None, None, :], scores, -1e30)
    own = jnp.einsum("bhgd,bhd->bhg", query, key_new, preferred_element_type=jnp.float32) * scale
    peak = jnp.maximum(jnp.max(scores, axis=3), own)
    weights = jnp.exp(scores - peak[..., None])
    own_weight = jnp.exp(own - peak)
    denominator = jnp.sum(weights, axis=3) + own_weight
    probs = (weights / denominator[..., None]).astype(jnp.bfloat16)
    own_prob = (own_weight / denominator).astype(jnp.bfloat16)
    mixed = jnp.einsum("bhgp,bhpd->bhgd", probs, cache_values, preferred_element_type=jnp.float32)
    mixed = (
        mixed
        + own_prob.astype(jnp.float32)[..., None] * value_new.astype(jnp.float32)[:, :, None, :]
    )
    attended = mixed.reshape(rows, width).astype(jnp.bfloat16)

    output, _ = project(
        attended, tagged, 3 * rank, 4 * rank, output_weight, output_up_adapter, (0, width)
    )
    return output


def solution(mesh):
    count = mesh.shape[AXIS]

    def body(*arrays):
        return local(*arrays, count=count)

    return jax.shard_map(
        body,
        mesh=mesh,
        in_specs=(
            P(("groups", "tensor"), None),
            P(),
            P(("groups", "tensor"), None),
            P(),
            P(("groups", "tensor")),
            P(None, "tensor"),
            P(None, "tensor"),
            P("tensor", None, None),
            P(None, None, "tensor"),
            P(None, None, "tensor"),
            P(("groups", "tensor"), None, None, None),
            P(("groups", "tensor"), None, None, None),
        ),
        out_specs=P(("groups", "tensor"), None),
        check_vma=False,
    )
```

```python
import functools

import jax
import jax.numpy as jnp
from jax import lax
from jax.experimental import pallas as pl
from jax.experimental.pallas import tpu as pltpu
from jax.sharding import PartitionSpec as P

eps = 1e-05
AXIS = "tensor"
LANES = 128
VMEM = pltpu.VMEM
SMEM = pltpu.SMEM


def swap(x, count, offset):
    return lax.ppermute(x, AXIS, [(i, i ^ offset) for i in range(count)])


def exchange(x, groups=None):
    return lax.all_to_all(
        x, AXIS, split_axis=0, concat_axis=0, axis_index_groups=groups, tiled=True
    )


def sum_over(x, count, beside):
    step, turn, terms = count, 0, []
    while step > 1:
        radix = 4 if step % 4 == 0 else 2
        step //= radix
        others = [swap(x, count, k * step) for k in range(1, radix)]
        terms.append(beside(turn, x))
        for other in others:
            x = x + other
        if terms[-1] is not None:
            x, terms[-1] = lax.optimization_barrier((x, terms[-1]))
        turn += 1
    return x, [t for t in terms if t is not None]


def gather_rows(x, count):
    step = count // 4
    far, middle, near = (swap(x, count, k * step) for k in (3, 2, 1))
    step //= 2
    held = [jnp.concatenate([x, near, middle, far], axis=0)]
    across = [swap(p, count, step) for p in (x, far, near, middle)]
    held.append(jnp.concatenate([across[i] for i in (0, 2, 3, 1)], axis=0))
    step //= 2
    while step > 1:
        held = held + [swap(h, count, step) for h in held]
        step //= 2
    return held, held + [swap(h, count, 1) for h in held]


def place_of(row, me, count, rows):
    block = row // rows
    source = (block % 4) * (count // 4)
    piece, step = block // 4, count // 8
    while step:
        source = source + (piece % 2) * step
        piece, step = piece // 2, step // 2
    return (source ^ me) * rows + row % rows


def limit(total, megabytes):
    return (megabytes if total <= 64 else 60) * 1024 * 1024


def spec(space=VMEM):
    return pl.BlockSpec(memory_space=space)


def iota(shape, dim):
    return lax.broadcasted_iota(jnp.int32, shape, dim)


def one_hot(condition):
    return jnp.where(condition, 1.0, 0.0).astype(jnp.bfloat16)


def norm_kernel(
    hidden_hbm, gain_hbm, names_hbm, slots_hbm, out_ref, hidden_ref, gain_ref, names_ref, slots_ref, sems
):
    copies = [
        pltpu.make_async_copy(source, target, sems.at[i])
        for i, (source, target) in enumerate(
            (
                (hidden_hbm, hidden_ref),
                (gain_hbm, gain_ref),
                (names_hbm, names_ref),
                (slots_hbm, slots_ref),
            )
        )
    ]
    for copy in copies:
        copy.start()
    for copy in copies:
        copy.wait()
    rows, width = hidden_ref.shape
    hidden = hidden_ref[...].astype(jnp.float32)
    power = jnp.sum(hidden * hidden, axis=1, keepdims=True) / width
    gain = gain_ref[...].reshape(1, width).astype(jnp.float32)
    out_ref[:, :width] = (hidden * lax.rsqrt(power + eps) * gain).astype(jnp.bfloat16)
    row, lane = iota((rows, LANES), 0), iota((rows, LANES), 1)
    tags = jnp.zeros((rows, LANES), jnp.float32)
    for r in range(rows):
        name = names_ref[r]
        tag = jnp.where(lane < LANES // 2, name, slots_ref[name]).astype(jnp.float32)
        tags = jnp.where(row == r, tag, tags)
    out_ref[:, width:] = tags.astype(jnp.bfloat16)


NT = (((1,), (1,)), ((), ()))


def down_kernel(count, rows, pieces, low, *refs):
    maps_hbm, piece_refs = refs[:2], refs[2 : 2 + pieces]
    tag_refs, (out_ref, maps_ref, sems) = refs[2 + pieces : 2 + 2 * pieces], refs[2 + 2 * pieces :]
    me = lax.axis_index(AXIS)
    _, held, rank, width = maps_ref.shape
    total, half = count * rows, count * rows // 2
    chunk = 2048
    copies = []
    for k in range(0, width, chunk):
        for m in range(2):
            copies.append(
                pltpu.make_async_copy(
                    maps_hbm[m].at[:, low : low + rank, k : k + chunk],
                    maps_ref.at[m, :, :, k : k + chunk],
                    sems.at[len(copies)],
                )
            )
            copies[-1].start()
    sums = jnp.zeros((2 * held * rank, half), jnp.float32)
    for k in range(0, width, chunk):
        for m in range(2):
            copies[k // chunk * 2 + m].wait()
        x = jnp.concatenate([p[:, k : k + chunk] for p in piece_refs], axis=0)
        maps = maps_ref[:, :, :, k : k + chunk].reshape(2 * held * rank, chunk)
        sums = sums + lax.dot_general(maps, x, NT, preferred_element_type=jnp.float32)
    tags = jnp.concatenate([t[...] for t in tag_refs], axis=0)
    pick = one_hot(iota((16, LANES), 1) == LANES // 2)
    slots = lax.dot_general(pick, tags, NT, preferred_element_type=jnp.float32)[:1]
    chosen = jnp.zeros((rank, half), jnp.float32)
    for m in range(2):
        for s in range(held):
            slot = ((me ^ m) * held + s).astype(jnp.float32)
            at = (m * held + s) * rank
            chosen = jnp.where(slots == slot, sums[at : at + rank], chosen)
    row, column = iota((half, total), 0), iota((half, total), 1)
    back = one_hot(place_of(row, me, count, rows) == column)
    placed = jnp.dot(chosen.astype(jnp.bfloat16), back, preferred_element_type=jnp.float32)
    folds = out_ref.shape[1] // total
    part = rank // folds
    folded = [placed[f * part : (f + 1) * part] for f in range(folds)]
    value = jnp.concatenate(folded, axis=1).astype(jnp.bfloat16)
    out_ref[...] = value


def base_kernel(pieces, part, *refs):
    weight_hbm, _, out_ref, weight_ref, sems = refs[pieces:]
    total, columns = out_ref.shape
    whole = columns // 256 * 256
    depth = weight_ref.shape[0]
    chunk = 1024
    copies = [
        pltpu.make_async_copy(
            weight_hbm.at[part * depth + k : part * depth + k + chunk],
            weight_ref.at[k : k + chunk],
            sems.at[k // chunk],
        )
        for k in range(0, depth, chunk)
    ]
    for copy in copies:
        copy.start()
    for k in range(0, depth, chunk):
        at = part * depth + k
        x = jnp.concatenate([p[:, at : at + chunk] for p in refs[:pieces]], axis=0)
        copies[k // chunk].wait()
        terms = []
        if whole:
            weight = weight_ref[k : k + chunk, :whole]
            terms.append(jnp.dot(x, weight, preferred_element_type=jnp.float32))
        if columns - whole == 128:
            half = chunk // 2
            left = jnp.concatenate([x[:, :half], x[:, half:]], axis=0)
            right = [weight_ref[k + h : k + h + half, whole:] for h in (0, half)]
            both = jnp.dot(
                left, jnp.concatenate(right, axis=1), preferred_element_type=jnp.float32
            )
            terms.append(both[:total, :128] + both[total:, 128:])
        elif columns > whole:
            weight = weight_ref[k : k + chunk, whole:]
            terms.append(jnp.dot(x, weight, preferred_element_type=jnp.float32))
        term = terms[0] if len(terms) == 1 else jnp.concatenate(terms, axis=1)
        if k == 0:
            out_ref[...] = term
        else:
            out_ref[...] += term


def lift_kernel(count, rows, pieces, bounds, rank, *refs):
    tag_refs, refs = refs[:pieces], refs[pieces:]
    (down_ref, up_ref), base_refs, (out_ref, sum_ref) = refs[:2], refs[2:-2], refs[-2:]
    total = count * rows
    me = lax.axis_index(AXIS)
    adapters, per, columns = up_ref.shape
    wide = adapters * per
    row, column = iota((total, total), 0), iota((total, total), 1)
    order = one_hot(place_of(column, me, count, rows) == row)
    back = one_hot(place_of(row, me, count, rows) == column)
    folded = down_ref[...].astype(jnp.float32)
    folds = folded.shape[1] // total
    down = jnp.concatenate([folded[:, f * total : (f + 1) * total] for f in range(folds)], axis=0)
    down = lax.dot_general(
        back, down.astype(jnp.bfloat16), NT, preferred_element_type=jnp.float32
    ).astype(jnp.bfloat16)
    names = jnp.concatenate([t[...] for t in tag_refs], axis=0).astype(jnp.float32)[:, :1]
    named = (iota((total, wide), 1) // per).astype(jnp.float32) == names
    start = me * columns
    value = base_refs[0][...]
    for b in base_refs[1:]:
        value = value + b[...]
    sum_ref[...] = value
    for g in range(rank // per):
        low, high = bounds[g], bounds[g + 1]

        @pl.when((start < high) & (start + columns > low))
        def _():
            at = iota((rank, wide), 1) % per + g * per
            spread = one_hot(at == iota((rank, wide), 0))
            copies = jnp.dot(down, spread, preferred_element_type=jnp.float32)
            chosen = jnp.where(named, copies, 0.0).astype(jnp.bfloat16)
            up = up_ref[...].reshape(wide, columns)
            lifted = jnp.dot(chosen, up, preferred_element_type=jnp.float32)
            at = iota((total, columns), 1) + start
            sum_ref[...] += jnp.where((at >= low) & (at < high), lifted, 0.0)

    placed = jnp.dot(
        order, sum_ref[...].astype(jnp.bfloat16), preferred_element_type=jnp.float32
    ).astype(jnp.bfloat16)
    for d in range(count):
        out_ref[d] = placed[d * rows : (d + 1) * rows]


def local(
    input_hidden,
    input_norm_gain,
    request_adapter,
    adapter_storage,
    lengths,
    projection_weight,
    output_weight,
    adapter_down,
    projection_up_adapter,
    output_up_adapter,
    cache_keys,
    cache_values,
    *,
    count,
):
    rows, width = input_hidden.shape
    rank = projection_up_adapter.shape[1]
    held = adapter_down.shape[0]
    kv_heads, context, head_dim = cache_keys.shape[1:]
    kv_width = kv_heads * head_dim
    total = rows * count
    bf16, f32 = jnp.bfloat16, jnp.float32
    roomy = pltpu.CompilerParams(vmem_limit_bytes=limit(total, 16))
    tight = {
        projection_weight.shape[1]: pltpu.CompilerParams(vmem_limit_bytes=limit(total, 52)),
        output_weight.shape[1]: pltpu.CompilerParams(vmem_limit_bytes=limit(total, 52)),
    }
    full = pltpu.CompilerParams(vmem_limit_bytes=limit(total, 60))
    own_maps = jnp.swapaxes(adapter_down, 1, 2)
    sibling_maps = jnp.swapaxes(swap(adapter_down, count, 1), 1, 2)

    normed = pl.pallas_call(
        norm_kernel,
        out_shape=jax.ShapeDtypeStruct((rows, width + LANES), bf16),
        in_specs=[spec(pltpu.HBM)] * 4,
        out_specs=spec(),
        scratch_shapes=[
            VMEM((rows, width), bf16),
            VMEM((width,), bf16),
            SMEM((rows,), jnp.int32),
            SMEM(adapter_storage.shape, jnp.int32),
            pltpu.SemaphoreType.DMA((4,)),
        ],
        compiler_params=full,
        name="norm",
    )(input_hidden, input_norm_gain, request_adapter.reshape(rows), adapter_storage)

    def tag_specs(pieces):
        return [pl.BlockSpec((p.shape[0], LANES), lambda i: (0, width // LANES)) for p in pieces]

    def downs(pieces, tagged, low, high, columns):
        ranks = high - low
        lanes = max(LANES, total)
        return pl.pallas_call(
            functools.partial(down_kernel, count, rows, len(pieces), low),
            grid=(1,),
            out_shape=jax.ShapeDtypeStruct((ranks * total // lanes, lanes), bf16),
            in_specs=[spec(pl.ANY)] * 2
            + [pl.BlockSpec((p.shape[0], width), lambda i: (0, 0)) for p in pieces]
            + tag_specs(tagged),
            out_specs=spec(),
            scratch_shapes=[
                VMEM((2, held, ranks, width), bf16),
                pltpu.SemaphoreType.DMA((2 * (width // 2048),)),
            ],
            compiler_params=tight[columns],
            cost_estimate=pl.CostEstimate(
                flops=2 * total * width * held * ranks,
                bytes_accessed=2 * width * (2 * held * ranks + total),
                transcendentals=0,
            ),
            name="down",
        )(own_maps, sibling_maps, *pieces, *tagged)

    def base(pieces, weight, after, part, parts):
        columns = weight.shape[1]
        return pl.pallas_call(
            functools.partial(base_kernel, len(pieces), part),
            out_shape=jax.ShapeDtypeStruct((total, columns), f32),
            in_specs=[spec()] * len(pieces) + [spec(pl.ANY)] * 2,
            out_specs=spec(),
            scratch_shapes=[
                VMEM((width // parts, columns), bf16),
                pltpu.SemaphoreType.DMA((width // parts // 1024,)),
            ],
            compiler_params=tight[columns],
            cost_estimate=pl.CostEstimate(
                flops=2 * total * width * columns // parts,
                bytes_accessed=2 * width * columns // parts,
                transcendentals=0,
            ),
            name="base",
        )(*pieces, weight, after)

    def lift(down, tagged, up, base_terms, bounds, ranks):
        columns = up.shape[2]
        whole = lambda x: pl.BlockSpec(x.shape, lambda i: (0,) * x.ndim)
        operands = [down, up] + base_terms
        return pl.pallas_call(
            functools.partial(lift_kernel, count, rows, len(tagged), bounds, ranks),
            grid=(1,),
            out_shape=jax.ShapeDtypeStruct((count, rows, columns), bf16),
            in_specs=tag_specs(tagged) + [whole(x) for x in operands],
            out_specs=pl.BlockSpec((count, rows, columns), lambda i: (0, 0, 0)),
            scratch_shapes=[VMEM((total, columns), f32)],
            compiler_params=roomy,
            name="lift",
        )(*tagged, *operands)

    def project(x, tagged, low, high, weight, up, bounds):
        column, pieces = gather_rows(x, count)
        tagged = pieces if tagged is None else tagged
        parts = 2

        def beside(turn, after):
            return base(pieces, weight, after, turn, parts) if turn < parts else None

        down = downs(column, tagged[: len(column)], low, high, weight.shape[1])
        down, base_terms = sum_over(down, count, beside)
        columns = lift(down, tagged, up, base_terms, bounds, high - low)
        mine = exchange(columns)
        return jnp.swapaxes(mine, 0, 1).reshape(rows, -1), tagged

    bounds = (0, width, width + kv_width, width + 2 * kv_width)
    qkv_mine, tagged = project(
        normed, None, 0, 3 * rank, projection_weight, projection_up_adapter, bounds
    )

    groups_per = width // head_dim // kv_heads
    query = qkv_mine[:, 0:width].reshape(rows, kv_heads, groups_per, head_dim)
    key_new = qkv_mine[:, width : width + kv_width].reshape(rows, kv_heads, head_dim)
    value_new = qkv_mine[:, width + kv_width :].reshape(rows, kv_heads, head_dim)
    scale = head_dim ** (-0.5)
    scores = (
        jnp.einsum("bhgd,bhpd->bhgp", query, cache_keys, preferred_element_type=jnp.float32) * scale
    )
    lengths, query = lax.optimization_barrier((lengths, query))
    live = jnp.arange(context, dtype=jnp.int32)[None, :] < lengths[:, None]
    scores = jnp.where(live[:, None, None, :], scores, -1e30)
    own = jnp.einsum("bhgd,bhd->bhg", query, key_new, preferred_element_type=jnp.float32) * scale
    peak = jnp.maximum(jnp.max(scores, axis=3), own)
    weights = jnp.exp(scores - peak[..., None])
    own_weight = jnp.exp(own - peak)
    denominator = jnp.sum(weights, axis=3) + own_weight
    probs = (weights / denominator[..., None]).astype(jnp.bfloat16)
    own_prob = (own_weight / denominator).astype(jnp.bfloat16)
    mixed = jnp.einsum("bhgp,bhpd->bhgd", probs, cache_values, preferred_element_type=jnp.float32)
    mixed = (
        mixed
        + own_prob.astype(jnp.float32)[..., None] * value_new.astype(jnp.float32)[:, :, None, :]
    )
    attended = mixed.reshape(rows, width).astype(jnp.bfloat16)

    output, _ = project(
        attended, tagged, 3 * rank, 4 * rank, output_weight, output_up_adapter, (0, width)
    )
    return output


def solution(mesh):
    count = mesh.shape[AXIS]

    def body(*arrays):
        return local(*arrays, count=count)

    return jax.shard_map(
        body,
        mesh=mesh,
        in_specs=(
            P(("groups", "tensor"), None),
            P(),
            P(("groups", "tensor"), None),
            P(),
            P(("groups", "tensor")),
            P(None, "tensor"),
            P(None, "tensor"),
            P("tensor", None, None),
            P(None, None, "tensor"),
            P(None, None, "tensor"),
            P(("groups", "tensor"), None, None, None),
            P(("groups", "tensor"), None, None, None),
        ),
        out_specs=P(("groups", "tensor"), None),
        check_vma=False,
    )
```

```python
import functools

import jax
import jax.numpy as jnp
from jax import lax
from jax.experimental import pallas as pl
from jax.experimental.pallas import tpu as pltpu
from jax.sharding import PartitionSpec as P

eps = 1e-05
AXIS = "tensor"
LANES = 128
VMEM = pltpu.VMEM
SMEM = pltpu.SMEM


def swap(x, count, offset):
    return lax.ppermute(x, AXIS, [(i, i ^ offset) for i in range(count)])


def exchange(x, groups=None):
    return lax.all_to_all(
        x, AXIS, split_axis=0, concat_axis=0, axis_index_groups=groups, tiled=True
    )


def sum_over(x, count, beside):
    step, turn, terms = count, 0, []
    while step > 1:
        radix = 4 if step % 4 == 0 else 2
        step //= radix
        others = [swap(x, count, k * step) for k in range(1, radix)]
        term = beside(turn, x)
        if term is not None:
            *others, term = lax.optimization_barrier((*others, term))
        terms.append(term)
        for other in others:
            x = x + other
        turn += 1
    return x, [t for t in terms if t is not None]


def gather_rows(x, count):
    step = count // 4
    far, middle, near = (swap(x, count, k * step) for k in (3, 2, 1))
    step //= 2
    held = [jnp.concatenate([x, near, middle, far], axis=0)]
    across = [swap(p, count, step) for p in (x, far, near, middle)]
    held.append(jnp.concatenate([across[i] for i in (0, 2, 3, 1)], axis=0))
    step //= 2
    while step > 1:
        held = held + [swap(h, count, step) for h in held]
        step //= 2
    return held, held + [swap(h, count, 1) for h in held]


def place_of(row, me, count, rows):
    block = row // rows
    source = (block % 4) * (count // 4)
    piece, step = block // 4, count // 8
    while step:
        source = source + (piece % 2) * step
        piece, step = piece // 2, step // 2
    return (source ^ me) * rows + row % rows


def limit(total, megabytes):
    return (megabytes if total <= 64 else 60) * 1024 * 1024


def spec(space=VMEM):
    return pl.BlockSpec(memory_space=space)


def iota(shape, dim):
    return lax.broadcasted_iota(jnp.int32, shape, dim)


def one_hot(condition):
    return jnp.where(condition, 1.0, 0.0).astype(jnp.bfloat16)


def norm_kernel(
    hidden_hbm,
    gain_hbm,
    names_hbm,
    slots_hbm,
    maps_hbm,
    out_ref,
    maps_ref,
    hidden_ref,
    gain_ref,
    names_ref,
    slots_ref,
    sems,
):
    ranks = maps_ref.shape[1]
    copies = [
        pltpu.make_async_copy(source, target, sems.at[i])
        for i, (source, target) in enumerate(
            (
                (hidden_hbm, hidden_ref),
                (gain_hbm, gain_ref),
                (names_hbm, names_ref),
                (slots_hbm, slots_ref),
                (maps_hbm.at[:, :ranks], maps_ref),
            )
        )
    ]
    for copy in copies:
        copy.start()
    for copy in copies[:-1]:
        copy.wait()
    rows, width = hidden_ref.shape
    hidden = hidden_ref[...].astype(jnp.float32)
    power = jnp.sum(hidden * hidden, axis=1, keepdims=True) / width
    gain = gain_ref[...].reshape(1, width).astype(jnp.float32)
    out_ref[:, :width] = (hidden * lax.rsqrt(power + eps) * gain).astype(jnp.bfloat16)
    row, lane = iota((rows, LANES), 0), iota((rows, LANES), 1)
    tags = jnp.zeros((rows, LANES), jnp.float32)
    for r in range(rows):
        name = names_ref[r]
        tag = jnp.where(lane < LANES // 2, name, slots_ref[name]).astype(jnp.float32)
        tags = jnp.where(row == r, tag, tags)
    out_ref[:, width:] = tags.astype(jnp.bfloat16)
    copies[-1].wait()


NT = (((1,), (1,)), ((), ()))


def down_kernel(count, rows, pieces, ranks, *refs):
    map_refs, piece_refs = refs[:2], refs[2 : 2 + pieces]
    tag_refs, out_refs = refs[2 + pieces : 2 + 2 * pieces], refs[2 + 2 * pieces :]
    out_ref = out_refs[0]
    me = lax.axis_index(AXIS)
    held, _, width = map_refs[0].shape
    rank = ranks[1] - ranks[0]
    total, half = count * rows, count * rows // 2
    chunk = 1024
    sums = jnp.zeros((2 * held * rank, half), jnp.float32)
    for k in range(0, width, chunk):
        x = jnp.concatenate([p[:, k : k + chunk] for p in piece_refs], axis=0)
        maps = jnp.concatenate(
            [m[:, :rank, k : k + chunk].reshape(held * rank, chunk) for m in map_refs], axis=0
        )
        sums = sums + lax.dot_general(maps, x, NT, preferred_element_type=jnp.float32)
    if len(out_refs) > 1:
        out_refs[1][...] = map_refs[1][:, rank:]
    tags = jnp.concatenate([t[...] for t in tag_refs], axis=0)
    pick = one_hot(iota((16, LANES), 1) == LANES // 2)
    slots = lax.dot_general(pick, tags, NT, preferred_element_type=jnp.float32)[:1]
    chosen = jnp.zeros((rank, half), jnp.float32)
    for m in range(2):
        for s in range(held):
            slot = ((me ^ m) * held + s).astype(jnp.float32)
            at = (m * held + s) * rank
            chosen = jnp.where(slots == slot, sums[at : at + rank], chosen)
    row, column = iota((half, total), 0), iota((half, total), 1)
    back = one_hot(place_of(row, me, count, rows) == column)
    placed = jnp.dot(chosen.astype(jnp.bfloat16), back, preferred_element_type=jnp.float32)
    folds = out_ref.shape[1] // total
    part = rank // folds
    folded = [placed[f * part : (f + 1) * part] for f in range(folds)]
    value = jnp.concatenate(folded, axis=1).astype(jnp.bfloat16)
    out_ref[...] = value


def base_kernel(pieces, part, *refs):
    weight_hbm, _, out_ref, weight_ref, sems = refs[pieces:]
    total, columns = out_ref.shape
    whole = columns // 256 * 256
    depth = weight_ref.shape[0]
    chunk = 512
    copies = [
        pltpu.make_async_copy(
            weight_hbm.at[part * depth + k : part * depth + k + chunk],
            weight_ref.at[k : k + chunk],
            sems.at[k // chunk],
        )
        for k in range(0, depth, chunk)
    ]
    for copy in copies:
        copy.start()
    for k in range(0, depth, chunk):
        at = part * depth + k
        x = jnp.concatenate([p[:, at : at + chunk] for p in refs[:pieces]], axis=0)
        copies[k // chunk].wait()
        terms = []
        if whole:
            weight = weight_ref[k : k + chunk, :whole]
            terms.append(jnp.dot(x, weight, preferred_element_type=jnp.float32))
        if columns - whole == 128:
            half = chunk // 2
            left = jnp.concatenate([x[:, :half], x[:, half:]], axis=0)
            right = [weight_ref[k + h : k + h + half, whole:] for h in (0, half)]
            both = jnp.dot(
                left, jnp.concatenate(right, axis=1), preferred_element_type=jnp.float32
            )
            terms.append(both[:total, :128] + both[total:, 128:])
        elif columns > whole:
            weight = weight_ref[k : k + chunk, whole:]
            terms.append(jnp.dot(x, weight, preferred_element_type=jnp.float32))
        term = terms[0] if len(terms) == 1 else jnp.concatenate(terms, axis=1)
        if k == 0:
            out_ref[...] = term
        else:
            out_ref[...] += term


def lift_kernel(count, rows, pieces, bounds, rank, *refs):
    tag_refs, refs = refs[:pieces], refs[pieces:]
    (down_ref, up_ref), base_refs, (out_ref, sum_ref) = refs[:2], refs[2:-2], refs[-2:]
    total = count * rows
    me = lax.axis_index(AXIS)
    adapters, per, columns = up_ref.shape
    wide = adapters * per
    row, column = iota((total, total), 0), iota((total, total), 1)
    order = one_hot(place_of(column, me, count, rows) == row)
    back = one_hot(place_of(row, me, count, rows) == column)
    folded = down_ref[...].astype(jnp.float32)
    folds = folded.shape[1] // total
    down = jnp.concatenate([folded[:, f * total : (f + 1) * total] for f in range(folds)], axis=0)
    down = lax.dot_general(
        back, down.astype(jnp.bfloat16), NT, preferred_element_type=jnp.float32
    ).astype(jnp.bfloat16)
    names = jnp.concatenate([t[...] for t in tag_refs], axis=0).astype(jnp.float32)[:, :1]
    named = (iota((total, wide), 1) // per).astype(jnp.float32) == names
    start = me * columns
    value = base_refs[0][...]
    for b in base_refs[1:]:
        value = value + b[...]
    sum_ref[...] = value
    for g in range(rank // per):
        low, high = bounds[g], bounds[g + 1]

        @pl.when((start < high) & (start + columns > low))
        def _():
            at = iota((rank, wide), 1) % per + g * per
            spread = one_hot(at == iota((rank, wide), 0))
            copies = jnp.dot(down, spread, preferred_element_type=jnp.float32)
            chosen = jnp.where(named, copies, 0.0).astype(jnp.bfloat16)
            up = up_ref[...].reshape(wide, columns)
            lifted = jnp.dot(chosen, up, preferred_element_type=jnp.float32)
            at = iota((total, columns), 1) + start
            sum_ref[...] += jnp.where((at >= low) & (at < high), lifted, 0.0)

    placed = jnp.dot(
        order, sum_ref[...].astype(jnp.bfloat16), preferred_element_type=jnp.float32
    ).astype(jnp.bfloat16)
    for d in range(count):
        out_ref[d] = placed[d * rows : (d + 1) * rows]


def local(
    input_hidden,
    input_norm_gain,
    request_adapter,
    adapter_storage,
    lengths,
    projection_weight,
    output_weight,
    adapter_down,
    projection_up_adapter,
    output_up_adapter,
    cache_keys,
    cache_values,
    *,
    count,
):
    rows, width = input_hidden.shape
    rank = projection_up_adapter.shape[1]
    held = adapter_down.shape[0]
    kv_heads, context, head_dim = cache_keys.shape[1:]
    kv_width = kv_heads * head_dim
    total = rows * count
    bf16, f32 = jnp.bfloat16, jnp.float32
    roomy = pltpu.CompilerParams(vmem_limit_bytes=limit(total, 16))
    tight = {
        projection_weight.shape[1]: pltpu.CompilerParams(vmem_limit_bytes=limit(total, 52)),
        output_weight.shape[1]: pltpu.CompilerParams(vmem_limit_bytes=limit(total, 52)),
    }
    full = pltpu.CompilerParams(vmem_limit_bytes=limit(total, 58))
    own_maps = jnp.swapaxes(adapter_down, 1, 2)
    sibling_maps = jnp.swapaxes(swap(adapter_down, count, 1), 1, 2)

    normed, first_maps = pl.pallas_call(
        norm_kernel,
        out_shape=[
            VMEM((rows, width + LANES), bf16),
            VMEM((held, 3 * rank, width), bf16),
        ],
        in_specs=[spec(pltpu.HBM)] * 5,
        out_specs=[spec()] * 2,
        scratch_shapes=[
            VMEM((rows, width), bf16),
            VMEM((width,), bf16),
            SMEM((rows,), jnp.int32),
            SMEM(adapter_storage.shape, jnp.int32),
            pltpu.SemaphoreType.DMA((5,)),
        ],
        compiler_params=full,
        name="norm",
    )(input_hidden, input_norm_gain, request_adapter.reshape(rows), adapter_storage, own_maps)

    def tag_specs(pieces):
        return [pl.BlockSpec((p.shape[0], LANES), lambda i: (0, width // LANES)) for p in pieces]

    def downs(own, sibling, pieces, tagged, low, high):
        ranks = high - low
        lanes = max(LANES, total)
        whole = lambda x: pl.BlockSpec(x.shape, lambda i: (0,) * x.ndim)
        own_spec = pl.BlockSpec((held, ranks, width), lambda i: (0, low // ranks, 0))
        shapes = [jax.ShapeDtypeStruct((ranks * total // lanes, lanes), bf16)]
        if low == 0:
            rest = sibling.shape[1] - ranks
            shapes.append(jax.ShapeDtypeStruct((held, rest, width), bf16))
        return pl.pallas_call(
            functools.partial(down_kernel, count, rows, len(pieces), (low, high)),
            grid=(1,),
            out_shape=shapes,
            in_specs=[own_spec, whole(sibling)]
            + [pl.BlockSpec((p.shape[0], width), lambda i: (0, 0)) for p in pieces]
            + tag_specs(tagged),
            out_specs=[whole(x) for x in shapes],
            compiler_params=roomy,
            cost_estimate=pl.CostEstimate(
                flops=2 * total * width * held * ranks,
                bytes_accessed=2 * width * (2 * held * ranks + total),
                transcendentals=0,
            ),
            name="down",
        )(own, sibling, *pieces, *tagged)

    def base(pieces, weight, after, part, parts):
        columns = weight.shape[1]
        return pl.pallas_call(
            functools.partial(base_kernel, len(pieces), part),
            out_shape=jax.ShapeDtypeStruct((total, columns), f32),
            in_specs=[spec()] * len(pieces) + [spec(pl.ANY)] * 2,
            out_specs=spec(),
            scratch_shapes=[
                VMEM((width // parts, columns), bf16),
                pltpu.SemaphoreType.DMA((width // parts // 512,)),
            ],
            compiler_params=tight[columns],
            cost_estimate=pl.CostEstimate(
                flops=2 * total * width * columns // parts,
                bytes_accessed=4 * width * columns // parts,
                transcendentals=0,
            ),
            name="base",
        )(*pieces, weight, after)

    def lift(down, tagged, up, base_terms, bounds, ranks):
        columns = up.shape[2]
        whole = lambda x: pl.BlockSpec(x.shape, lambda i: (0,) * x.ndim)
        operands = [down, up] + base_terms
        return pl.pallas_call(
            functools.partial(lift_kernel, count, rows, len(tagged), bounds, ranks),
            grid=(1,),
            out_shape=jax.ShapeDtypeStruct((count, rows, columns), bf16),
            in_specs=tag_specs(tagged) + [whole(x) for x in operands],
            out_specs=pl.BlockSpec((count, rows, columns), lambda i: (0, 0, 0)),
            scratch_shapes=[VMEM((total, columns), f32)],
            compiler_params=roomy,
            name="lift",
        )(*tagged, *operands)

    def project(x, tagged, maps, low, high, weight, up, bounds):
        column, pieces = gather_rows(x, count)
        tagged = pieces if tagged is None else tagged
        parts = 2

        def beside(turn, after):
            return base(pieces, weight, after, turn, parts) if turn < parts else None

        down, *rest = downs(*maps, column, tagged[: len(column)], low, high)
        down, base_terms = sum_over(down, count, beside)
        columns = lift(down, tagged, up, base_terms, bounds, high - low)
        mine = exchange(columns)
        return jnp.swapaxes(mine, 0, 1).reshape(rows, -1), tagged, rest

    bounds = (0, width, width + kv_width, width + 2 * kv_width)
    qkv_mine, tagged, rest = project(
        normed,
        None,
        (first_maps, sibling_maps),
        0,
        3 * rank,
        projection_weight,
        projection_up_adapter,
        bounds,
    )

    groups_per = width // head_dim // kv_heads
    query = qkv_mine[:, 0:width].reshape(rows, kv_heads, groups_per, head_dim)
    key_new = qkv_mine[:, width : width + kv_width].reshape(rows, kv_heads, head_dim)
    value_new = qkv_mine[:, width + kv_width :].reshape(rows, kv_heads, head_dim)
    scale = head_dim ** (-0.5)
    scores = (
        jnp.einsum("bhgd,bhpd->bhgp", query, cache_keys, preferred_element_type=jnp.float32) * scale
    )
    lengths, query = lax.optimization_barrier((lengths, query))
    live = jnp.arange(context, dtype=jnp.int32)[None, :] < lengths[:, None]
    scores = jnp.where(live[:, None, None, :], scores, -1e30)
    own = jnp.einsum("bhgd,bhd->bhg", query, key_new, preferred_element_type=jnp.float32) * scale
    peak = jnp.maximum(jnp.max(scores, axis=3), own)
    weights = jnp.exp(scores - peak[..., None])
    own_weight = jnp.exp(own - peak)
    denominator = jnp.sum(weights, axis=3) + own_weight
    probs = (weights / denominator[..., None]).astype(jnp.bfloat16)
    own_prob = (own_weight / denominator).astype(jnp.bfloat16)
    mixed = jnp.einsum("bhgp,bhpd->bhgd", probs, cache_values, preferred_element_type=jnp.float32)
    mixed = (
        mixed
        + own_prob.astype(jnp.float32)[..., None] * value_new.astype(jnp.float32)[:, :, None, :]
    )
    attended = mixed.reshape(rows, width).astype(jnp.bfloat16)

    output, _, _ = project(
        attended,
        tagged,
        (own_maps, rest[0]),
        3 * rank,
        4 * rank,
        output_weight,
        output_up_adapter,
        (0, width),
    )
    return output


def solution(mesh):
    count = mesh.shape[AXIS]

    def body(*arrays):
        return local(*arrays, count=count)

    return jax.shard_map(
        body,
        mesh=mesh,
        in_specs=(
            P(("groups", "tensor"), None),
            P(),
            P(("groups", "tensor"), None),
            P(),
            P(("groups", "tensor")),
            P(None, "tensor"),
            P(None, "tensor"),
            P("tensor", None, None),
            P(None, None, "tensor"),
            P(None, None, "tensor"),
            P(("groups", "tensor"), None, None, None),
            P(("groups", "tensor"), None, None, None),
        ),
        out_specs=P(("groups", "tensor"), None),
        check_vma=False,
    )
```

```python
import functools

import jax
import jax.numpy as jnp
from jax import lax
from jax.experimental import pallas as pl
from jax.experimental.pallas import tpu as pltpu
from jax.sharding import PartitionSpec as P

eps = 1e-05
AXIS = "tensor"
LANES = 128
VMEM = pltpu.VMEM
SMEM = pltpu.SMEM


def swap(x, count, offset):
    return lax.ppermute(x, AXIS, [(i, i ^ offset) for i in range(count)])


def exchange(x, groups=None):
    return lax.all_to_all(
        x, AXIS, split_axis=0, concat_axis=0, axis_index_groups=groups, tiled=True
    )


def sum_over(x, count, beside):
    step, turn, terms = count, 0, []
    while step > 1:
        radix = 4 if step % 4 == 0 else 2
        step //= radix
        others = [swap(x, count, k * step) for k in range(1, radix)]
        term = beside(turn, x)
        if term is not None:
            *others, term = lax.optimization_barrier((*others, term))
        terms.append(term)
        for other in others:
            x = x + other
        turn += 1
    return x, [t for t in terms if t is not None]


def gather_rows(x, count, beside, other=None):
    step = count // 4
    far, middle, near = (swap(x, count, k * step) for k in (3, 2, 1))
    if other is not None:
        middle, other = lax.optimization_barrier((middle, other))
        other = swap(other, count, 1)
    step //= 2
    held = [jnp.concatenate([x, near, middle, far], axis=0)]
    across = [swap(p, count, step) for p in (x, far, near, middle)]
    *across, result = lax.optimization_barrier((*across, beside(held[0])))
    held.append(jnp.concatenate([across[i] for i in (0, 2, 3, 1)], axis=0))
    step //= 2
    while step > 1:
        held = held + [swap(h, count, step) for h in held]
        step //= 2
    return held, held + [swap(h, count, 1) for h in held], result, other


def place_of(row, me, count, rows):
    block = row // rows
    source = (block % 4) * (count // 4)
    piece, step = block // 4, count // 8
    while step:
        source = source + (piece % 2) * step
        piece, step = piece // 2, step // 2
    return (source ^ me) * rows + row % rows


def spec(space=VMEM):
    return pl.BlockSpec(memory_space=space)


def hbm(x):
    return pltpu.with_memory_space_constraint(x, pltpu.HBM)


def iota(shape, dim):
    return lax.broadcasted_iota(jnp.int32, shape, dim)


def one_hot(condition):
    return jnp.where(condition, 1.0, 0.0).astype(jnp.bfloat16)


def norm_kernel(
    hidden_hbm,
    gain_hbm,
    names_hbm,
    slots_hbm,
    maps_hbm,
    weight_hbm,
    out_ref,
    maps_ref,
    weight_ref,
    hidden_ref,
    gain_ref,
    names_ref,
    slots_ref,
    sems,
):
    ranks = maps_ref.shape[1]
    copies = [
        pltpu.make_async_copy(source, target, sems.at[i])
        for i, (source, target) in enumerate(
            (
                (hidden_hbm, hidden_ref),
                (gain_hbm, gain_ref),
                (names_hbm, names_ref),
                (slots_hbm, slots_ref),
                (maps_hbm.at[:, :ranks], maps_ref),
                (weight_hbm.at[: weight_ref.shape[0]], weight_ref),
            )
        )
    ]
    for copy in copies:
        copy.start()
    for copy in copies[:4]:
        copy.wait()
    rows, width = hidden_ref.shape
    hidden = hidden_ref[...].astype(jnp.float32)
    power = jnp.sum(hidden * hidden, axis=1, keepdims=True) / width
    gain = gain_ref[...].reshape(1, width).astype(jnp.float32)
    out_ref[:, :width] = (hidden * lax.rsqrt(power + eps) * gain).astype(jnp.bfloat16)
    row, lane = iota((rows, LANES), 0), iota((rows, LANES), 1)
    tags = jnp.zeros((rows, LANES), jnp.float32)
    for r in range(rows):
        name = names_ref[r]
        tag = jnp.where(lane < LANES // 2, name, slots_ref[name]).astype(jnp.float32)
        tags = jnp.where(row == r, tag, tags)
    out_ref[:, width:] = tags.astype(jnp.bfloat16)
    for copy in copies[4:]:
        copy.wait()


NT = (((1,), (1,)), ((), ()))


def down_kernel(count, rows, pieces, ranks, *refs):
    map_refs, piece_refs = refs[:2], refs[2 : 2 + pieces]
    tag_refs, out_refs = refs[2 + pieces : 2 + 2 * pieces], refs[2 + 2 * pieces :]
    out_ref = out_refs[0]
    me = lax.axis_index(AXIS)
    held, _, width = map_refs[0].shape
    rank = ranks[1] - ranks[0]
    total, half = count * rows, count * rows // 2
    chunk = 1024
    sums = jnp.zeros((2 * held * rank, half), jnp.float32)
    for k in range(0, width, chunk):
        x = jnp.concatenate([p[:, k : k + chunk] for p in piece_refs], axis=0)
        maps = jnp.concatenate(
            [m[:, :rank, k : k + chunk].reshape(held * rank, chunk) for m in map_refs], axis=0
        )
        sums = sums + lax.dot_general(maps, x, NT, preferred_element_type=jnp.float32)
    if len(out_refs) > 1:
        out_refs[1][...] = map_refs[1][:, rank:]
    tags = jnp.concatenate([t[...] for t in tag_refs], axis=0)
    pick = one_hot(iota((16, LANES), 1) == LANES // 2)
    slots = lax.dot_general(pick, tags, NT, preferred_element_type=jnp.float32)[:1]
    chosen = jnp.zeros((rank, half), jnp.float32)
    for m in range(2):
        for s in range(held):
            slot = ((me ^ m) * held + s).astype(jnp.float32)
            at = (m * held + s) * rank
            chosen = jnp.where(slots == slot, sums[at : at + rank], chosen)
    row, column = iota((half, total), 0), iota((half, total), 1)
    back = one_hot(place_of(row, me, count, rows) == column)
    placed = jnp.dot(chosen.astype(jnp.bfloat16), back, preferred_element_type=jnp.float32)
    folds = out_ref.shape[1] // total
    part = rank // folds
    folded = [placed[f * part : (f + 1) * part] for f in range(folds)]
    value = jnp.concatenate(folded, axis=1).astype(jnp.bfloat16)
    out_ref[...] = value


def load_kernel(start, after_ref, weight_hbm, out_ref, sems):
    rows = out_ref.shape[0]
    chunk = 512
    copies = [
        pltpu.make_async_copy(
            weight_hbm.at[start + k : start + k + chunk],
            out_ref.at[k : k + chunk],
            sems.at[k // chunk],
        )
        for k in range(0, rows, chunk)
    ]
    for copy in copies:
        copy.start()
    for copy in copies:
        copy.wait()


def base_kernel(pieces, start, *refs):
    ready_ref, weight_hbm, _, out_ref, weight_ref, sems = refs[pieces:]
    total, columns = out_ref.shape
    whole = columns // 256 * 256
    ready = ready_ref.shape[0]
    chunk = 1024
    copies = [
        pltpu.make_async_copy(
            weight_hbm.at[start + ready + k : start + ready + k + chunk],
            weight_ref.at[k : k + chunk],
            sems.at[k // chunk],
        )
        for k in range(0, weight_ref.shape[0], chunk)
    ]
    for copy in copies:
        copy.start()
    for k in range(0, ready + weight_ref.shape[0], chunk):
        x = jnp.concatenate([p[:, start + k : start + k + chunk] for p in refs[:pieces]], axis=0)
        from_ref, at = (ready_ref, k) if k < ready else (weight_ref, k - ready)
        if k >= ready:
            copies[at // chunk].wait()
        terms = []
        if whole:
            weight = from_ref[at : at + chunk, :whole]
            terms.append(jnp.dot(x, weight, preferred_element_type=jnp.float32))
        if columns - whole == 128:
            half = chunk // 2
            left = jnp.concatenate([x[:, :half], x[:, half:]], axis=0)
            right = [from_ref[at + h : at + h + half, whole:] for h in (0, half)]
            both = jnp.dot(
                left, jnp.concatenate(right, axis=1), preferred_element_type=jnp.float32
            )
            terms.append(both[:total, :128] + both[total:, 128:])
        elif columns > whole:
            weight = from_ref[at : at + chunk, whole:]
            terms.append(jnp.dot(x, weight, preferred_element_type=jnp.float32))
        term = terms[0] if len(terms) == 1 else jnp.concatenate(terms, axis=1)
        if k == 0:
            out_ref[...] = term
        else:
            out_ref[...] += term


def lift_kernel(count, rows, pieces, bounds, rank, *refs):
    tag_refs, refs = refs[:pieces], refs[pieces:]
    (down_ref, up_ref), base_refs, (out_ref, sum_ref) = refs[:2], refs[2:-2], refs[-2:]
    total = count * rows
    me = lax.axis_index(AXIS)
    adapters, per, columns = up_ref.shape
    wide = adapters * per
    row, column = iota((total, total), 0), iota((total, total), 1)
    order = one_hot(place_of(column, me, count, rows) == row)
    back = one_hot(place_of(row, me, count, rows) == column)
    folded = down_ref[...].astype(jnp.float32)
    folds = folded.shape[1] // total
    down = jnp.concatenate([folded[:, f * total : (f + 1) * total] for f in range(folds)], axis=0)
    down = lax.dot_general(
        back, down.astype(jnp.bfloat16), NT, preferred_element_type=jnp.float32
    ).astype(jnp.bfloat16)
    names = jnp.concatenate([t[...] for t in tag_refs], axis=0).astype(jnp.float32)[:, :1]
    named = (iota((total, wide), 1) // per).astype(jnp.float32) == names
    start = me * columns
    value = base_refs[0][...]
    for b in base_refs[1:]:
        value = value + b[...]
    sum_ref[...] = value
    for g in range(rank // per):
        low, high = bounds[g], bounds[g + 1]

        @pl.when((start < high) & (start + columns > low))
        def _():
            at = iota((rank, wide), 1) % per + g * per
            spread = one_hot(at == iota((rank, wide), 0))
            copies = jnp.dot(down, spread, preferred_element_type=jnp.float32)
            chosen = jnp.where(named, copies, 0.0).astype(jnp.bfloat16)
            up = up_ref[...].reshape(wide, columns)
            lifted = jnp.dot(chosen, up, preferred_element_type=jnp.float32)
            at = iota((total, columns), 1) + start
            sum_ref[...] += jnp.where((at >= low) & (at < high), lifted, 0.0)

    placed = jnp.dot(
        order, sum_ref[...].astype(jnp.bfloat16), preferred_element_type=jnp.float32
    ).astype(jnp.bfloat16)
    for d in range(count):
        out_ref[d] = placed[d * rows : (d + 1) * rows]


def attend_kernel(lengths_ref, qkv_ref, keys_ref, values_ref, out_ref):
    rows, kv_heads, context, dim = keys_ref.shape
    width = out_ref.shape[1]
    groups = width // dim // kv_heads
    mixed_rows = groups * rows
    request = iota((mixed_rows, 1), 0) % rows
    length = jnp.zeros((mixed_rows, 1), jnp.int32)
    for b in range(rows):
        length = jnp.where(request == b, lengths_ref[b], length)
    live = iota((mixed_rows, context), 1) < length
    scale = dim ** (-0.5)

    def columns(at):
        return qkv_ref[:, at : at + dim].astype(jnp.float32)

    for h in range(kv_heads):
        at = [(h * groups + g) * dim for g in range(groups)]
        query = jnp.concatenate([columns(a) for a in at], axis=0)
        key = jnp.concatenate([columns(width + h * dim)] * groups, axis=0)
        value = jnp.concatenate([columns(width + (kv_heads + h) * dim)] * groups, axis=0)
        half = query.astype(jnp.bfloat16)
        scores = jnp.zeros((mixed_rows, context), jnp.float32)
        for b in range(rows):
            one = lax.dot_general(half, keys_ref[b, h], NT, preferred_element_type=jnp.float32)
            scores = jnp.where(request == b, one, scores)
        scores = jnp.where(live, scores * scale, -1e30)
        own = jnp.sum(query * key, axis=1, keepdims=True) * scale
        peak = jnp.maximum(jnp.max(scores, axis=1, keepdims=True), own)
        weights = jnp.exp(scores - peak)
        own_weight = jnp.exp(own - peak)
        denominator = jnp.sum(weights, axis=1, keepdims=True) + own_weight
        probs = (weights / denominator).astype(jnp.bfloat16)
        own_prob = (own_weight / denominator).astype(jnp.bfloat16).astype(jnp.float32)
        mixed = jnp.zeros((mixed_rows, dim), jnp.float32)
        for b in range(rows):
            one = jnp.dot(probs, values_ref[b, h], preferred_element_type=jnp.float32)
            mixed = jnp.where(request == b, one, mixed)
        mixed = (mixed + own_prob * value).astype(jnp.bfloat16)
        for g in range(groups):
            out_ref[:, at[g] : at[g] + dim] = mixed[g * rows : (g + 1) * rows]


def local(
    input_hidden,
    input_norm_gain,
    request_adapter,
    adapter_storage,
    lengths,
    projection_weight,
    output_weight,
    adapter_down,
    projection_up_adapter,
    output_up_adapter,
    cache_keys,
    cache_values,
    *,
    count,
):
    rows, width = input_hidden.shape
    rank = projection_up_adapter.shape[1]
    held = adapter_down.shape[0]
    kv_heads, context, head_dim = cache_keys.shape[1:]
    kv_width = kv_heads * head_dim
    total = rows * count
    bf16, f32 = jnp.bfloat16, jnp.float32
    params = pltpu.CompilerParams(vmem_limit_bytes=(16 if total <= 64 else 60) * 1024 * 1024)
    own_maps = jnp.swapaxes(adapter_down, 1, 2)

    normed, first_maps, first_rows = pl.pallas_call(
        norm_kernel,
        out_shape=[
            VMEM((rows, width + LANES), bf16),
            VMEM((held, 3 * rank, width), bf16),
            VMEM((1024, projection_weight.shape[1]), bf16),
        ],
        in_specs=[spec(pltpu.HBM)] * 6,
        out_specs=[spec()] * 3,
        scratch_shapes=[
            VMEM((rows, width), bf16),
            VMEM((width,), bf16),
            SMEM((rows,), jnp.int32),
            SMEM(adapter_storage.shape, jnp.int32),
            pltpu.SemaphoreType.DMA((6,)),
        ],
        compiler_params=params,
        name="norm",
    )(
        hbm(input_hidden),
        hbm(input_norm_gain),
        hbm(request_adapter.reshape(rows)),
        hbm(adapter_storage),
        hbm(own_maps),
        hbm(projection_weight),
    )

    def tag_specs(pieces):
        return [pl.BlockSpec((p.shape[0], LANES), lambda i: (0, width // LANES)) for p in pieces]

    def downs(own, sibling, pieces, tagged, low, high):
        ranks = high - low
        lanes = max(LANES, total)
        whole = lambda x: pl.BlockSpec(x.shape, lambda i: (0,) * x.ndim)
        own_spec = pl.BlockSpec((held, ranks, width), lambda i: (0, low // ranks, 0))
        shapes = [jax.ShapeDtypeStruct((ranks * total // lanes, lanes), bf16)]
        if low == 0:
            rest = sibling.shape[1] - ranks
            shapes.append(jax.ShapeDtypeStruct((held, rest, width), bf16))
        return pl.pallas_call(
            functools.partial(down_kernel, count, rows, len(pieces), (low, high)),
            grid=(1,),
            out_shape=shapes,
            in_specs=[own_spec, whole(sibling)]
            + [pl.BlockSpec((p.shape[0], width), lambda i: (0, 0)) for p in pieces]
            + tag_specs(tagged),
            out_specs=[whole(x) for x in shapes],
            compiler_params=params,
            cost_estimate=pl.CostEstimate(
                flops=2 * total * width * held * ranks,
                bytes_accessed=2 * width * (2 * held * ranks + total),
                transcendentals=0,
            ),
            name="down",
        )(own, sibling, *pieces, *tagged)

    def load(after, weight, start, length):
        columns = weight.shape[1]
        return pl.pallas_call(
            functools.partial(load_kernel, start),
            out_shape=VMEM((length, columns), bf16),
            in_specs=[spec(pl.ANY), spec(pltpu.HBM)],
            out_specs=spec(),
            scratch_shapes=[pltpu.SemaphoreType.DMA((length // 512,))],
            compiler_params=params,
            cost_estimate=pl.CostEstimate(
                flops=0, bytes_accessed=4 * length * columns, transcendentals=0
            ),
            name="load",
        )(after, hbm(weight))

    def base(pieces, weight, after, start, ready, length):
        columns = weight.shape[1]
        stream = length - ready.shape[0]
        return pl.pallas_call(
            functools.partial(base_kernel, len(pieces), start),
            out_shape=jax.ShapeDtypeStruct((total, columns), f32),
            in_specs=[spec()] * (len(pieces) + 1) + [spec(pltpu.HBM), spec(pl.ANY)],
            out_specs=spec(),
            scratch_shapes=[
                VMEM((stream, columns), bf16),
                pltpu.SemaphoreType.DMA((stream // 1024,)),
            ],
            compiler_params=params,
            cost_estimate=pl.CostEstimate(
                flops=2 * total * length * columns,
                bytes_accessed=4 * length * columns,
                transcendentals=0,
            ),
            name="base",
        )(*pieces, ready, hbm(weight), after)

    def lift(down, tagged, up, base_terms, bounds, ranks):
        columns = up.shape[2]
        whole = lambda x: pl.BlockSpec(x.shape, lambda i: (0,) * x.ndim)
        operands = [down, up] + base_terms
        return pl.pallas_call(
            functools.partial(lift_kernel, count, rows, len(tagged), bounds, ranks),
            grid=(1,),
            out_shape=jax.ShapeDtypeStruct((count, rows, columns), bf16),
            in_specs=tag_specs(tagged) + [whole(x) for x in operands],
            out_specs=pl.BlockSpec((count, rows, columns), lambda i: (0, 0, 0)),
            scratch_shapes=[VMEM((total, columns), f32)],
            compiler_params=params,
            name="lift",
        )(*tagged, *operands)

    def project(x, tagged, own, sibling, ready, low, high, weight, up, bounds):
        half, quarter = width // 2, width // 4

        def beside(rows_here):
            last = load(rows_here, weight, half, quarter)
            return (load(rows_here, weight, 0, 1024) if ready is None else ready), last

        column, pieces, loaded, swapped = gather_rows(x, count, beside, sibling[0])
        tagged = pieces if tagged is None else tagged
        theirs = sibling[1] if swapped is None else jnp.swapaxes(swapped, 1, 2)

        def term(turn, after):
            if turn > 1:
                return None
            return base(pieces, weight, after, turn * half, loaded[turn], half)

        down, *rest = downs(own, theirs, column, tagged[: len(column)], low, high)
        down, base_terms = sum_over(down, count, term)
        columns = lift(down, tagged, up, base_terms, bounds, high - low)
        mine = exchange(columns)
        return jnp.swapaxes(mine, 0, 1).reshape(rows, -1), tagged, rest

    bounds = (0, width, width + kv_width, width + 2 * kv_width)
    qkv_mine, tagged, rest = project(
        normed,
        None,
        first_maps,
        (adapter_down, None),
        first_rows,
        0,
        3 * rank,
        projection_weight,
        projection_up_adapter,
        bounds,
    )
    attended = pl.pallas_call(
        attend_kernel,
        out_shape=jax.ShapeDtypeStruct((rows, width), bf16),
        in_specs=[spec(SMEM)] + [spec()] * 3,
        out_specs=spec(),
        compiler_params=params,
        cost_estimate=pl.CostEstimate(
            flops=4 * rows * width * context,
            bytes_accessed=4 * cache_keys.size,
            transcendentals=rows * width // head_dim * context,
        ),
        name="attend",
    )(lengths, qkv_mine, cache_keys, cache_values)
    output, _, _ = project(
        attended,
        tagged,
        own_maps,
        (None, rest[0]),
        None,
        3 * rank,
        4 * rank,
        output_weight,
        output_up_adapter,
        (0, width),
    )
    return output


def solution(mesh):
    count = mesh.shape[AXIS]

    def body(*arrays):
        return local(*arrays, count=count)

    return jax.shard_map(
        body,
        mesh=mesh,
        in_specs=(
            P(("groups", "tensor"), None),
            P(),
            P(("groups", "tensor"), None),
            P(),
            P(("groups", "tensor")),
            P(None, "tensor"),
            P(None, "tensor"),
            P("tensor", None, None),
            P(None, None, "tensor"),
            P(None, None, "tensor"),
            P(("groups", "tensor"), None, None, None),
            P(("groups", "tensor"), None, None, None),
        ),
        out_specs=P(("groups", "tensor"), None),
        check_vma=False,
    )
```

```python
import functools

import jax
import jax.numpy as jnp
from jax import lax
from jax.experimental import pallas as pl
from jax.experimental.pallas import tpu as pltpu
from jax.sharding import PartitionSpec as P

eps = 1e-05
AXIS = "tensor"
LANES = 128
VMEM = pltpu.VMEM
SMEM = pltpu.SMEM


def swap(x, count, offset):
    return lax.ppermute(x, AXIS, [(i, i ^ offset) for i in range(count)])


def exchange(x, groups=None):
    return lax.all_to_all(
        x, AXIS, split_axis=0, concat_axis=0, axis_index_groups=groups, tiled=True
    )


def sum_over(x, count, beside):
    step, turn, terms = count, 0, []
    while step > 1:
        radix = 4 if step % 4 == 0 else 2
        step //= radix
        others = [swap(x, count, k * step) for k in range(1, radix)]
        term = beside(turn, x)
        if term is not None:
            *others, term = lax.optimization_barrier((*others, term))
        terms.append(term)
        for other in others:
            x = x + other
        turn += 1
    return x, [t for t in terms if t is not None]


def gather_rows(x, count, beside, other=None):
    step = count // 4
    far, near = swap(x, count, 3 * step), swap(x, count, step)
    middle = swap(far, count, step)
    if other is not None:
        other = swap(other, count, 1)
    step //= 2
    held = [jnp.concatenate([x, near, middle, far], axis=0)]
    across = [swap(p, count, step) for p in (x, far, near, middle)]
    *across, result = lax.optimization_barrier((*across, beside(held[0])))
    held.append(jnp.concatenate([across[i] for i in (0, 2, 3, 1)], axis=0))
    step //= 2
    while step > 1:
        held = held + [swap(h, count, step) for h in held]
        step //= 2
    return held, held + [swap(h, count, 1) for h in held], result, other


def place_of(row, me, count, rows):
    block = row // rows
    source = (block % 4) * (count // 4)
    piece, step = block // 4, count // 8
    while step:
        source = source + (piece % 2) * step
        piece, step = piece // 2, step // 2
    return (source ^ me) * rows + row % rows


def spec(space=VMEM):
    return pl.BlockSpec(memory_space=space)


def hbm(x):
    return pltpu.with_memory_space_constraint(x, pltpu.HBM)


def iota(shape, dim):
    return lax.broadcasted_iota(jnp.int32, shape, dim)


def one_hot(condition):
    return jnp.where(condition, 1.0, 0.0).astype(jnp.bfloat16)


def norm_kernel(
    hidden_hbm,
    gain_hbm,
    names_hbm,
    slots_hbm,
    maps_hbm,
    weight_hbm,
    out_ref,
    maps_ref,
    weight_ref,
    hidden_ref,
    gain_ref,
    names_ref,
    slots_ref,
    sems,
):
    ranks = maps_ref.shape[1]
    copies = [
        pltpu.make_async_copy(source, target, sems.at[i])
        for i, (source, target) in enumerate(
            (
                (hidden_hbm, hidden_ref),
                (gain_hbm, gain_ref),
                (names_hbm, names_ref),
                (slots_hbm, slots_ref),
                (maps_hbm.at[:, :ranks], maps_ref),
                (weight_hbm.at[: weight_ref.shape[0]], weight_ref),
            )
        )
    ]
    for copy in copies:
        copy.start()
    for copy in copies[:4]:
        copy.wait()
    rows, width = hidden_ref.shape
    hidden = hidden_ref[...].astype(jnp.float32)
    power = jnp.sum(hidden * hidden, axis=1, keepdims=True) / width
    gain = gain_ref[...].reshape(1, width).astype(jnp.float32)
    out_ref[:, :width] = (hidden * lax.rsqrt(power + eps) * gain).astype(jnp.bfloat16)
    row, lane = iota((rows, LANES), 0), iota((rows, LANES), 1)
    tags = jnp.zeros((rows, LANES), jnp.float32)
    for r in range(rows):
        name = names_ref[r]
        tag = jnp.where(lane < LANES // 2, name, slots_ref[name]).astype(jnp.float32)
        tags = jnp.where(row == r, tag, tags)
    out_ref[:, width:] = tags.astype(jnp.bfloat16)
    for copy in copies[4:]:
        copy.wait()


NT = (((1,), (1,)), ((), ()))


def down_kernel(count, rows, pieces, ranks, *refs):
    map_refs, piece_refs = refs[:2], refs[2 : 2 + pieces]
    tag_refs, out_refs = refs[2 + pieces : 2 + 2 * pieces], refs[2 + 2 * pieces :]
    out_ref = out_refs[0]
    me = lax.axis_index(AXIS)
    held, _, width = map_refs[0].shape
    rank = ranks[1] - ranks[0]
    total, half = count * rows, count * rows // 2
    chunk = 4096
    sums = jnp.zeros((2 * held * rank, half), jnp.float32)
    for k in range(0, width, chunk):
        x = jnp.concatenate([p[:, k : k + chunk] for p in piece_refs], axis=0)
        maps = jnp.concatenate(
            [m[:, :rank, k : k + chunk].reshape(held * rank, chunk) for m in map_refs], axis=0
        )
        sums = sums + lax.dot_general(maps, x, NT, preferred_element_type=jnp.float32)
    if len(out_refs) > 1:
        out_refs[1][...] = map_refs[1][:, rank:]
    tags = jnp.concatenate([t[...] for t in tag_refs], axis=0)
    pick = one_hot(iota((16, LANES), 1) == LANES // 2)
    slots = lax.dot_general(pick, tags, NT, preferred_element_type=jnp.float32)[:1]
    chosen = jnp.zeros((rank, half), jnp.float32)
    for m in range(2):
        for s in range(held):
            slot = ((me ^ m) * held + s).astype(jnp.float32)
            at = (m * held + s) * rank
            chosen = jnp.where(slots == slot, sums[at : at + rank], chosen)
    row, column = iota((half, total), 0), iota((half, total), 1)
    back = one_hot(place_of(row, me, count, rows) == column)
    placed = jnp.dot(chosen.astype(jnp.bfloat16), back, preferred_element_type=jnp.float32)
    folds = out_ref.shape[1] // total
    part = rank // folds
    folded = [placed[f * part : (f + 1) * part] for f in range(folds)]
    value = jnp.concatenate(folded, axis=1).astype(jnp.bfloat16)
    out_ref[...] = value


def load_kernel(start, after_ref, weight_hbm, out_ref, sems):
    rows = out_ref.shape[0]
    chunk = 512
    copies = [
        pltpu.make_async_copy(
            weight_hbm.at[start + k : start + k + chunk],
            out_ref.at[k : k + chunk],
            sems.at[k // chunk],
        )
        for k in range(0, rows, chunk)
    ]
    for copy in copies:
        copy.start()
    for copy in copies:
        copy.wait()


def base_kernel(pieces, start, ready, *refs):
    ready_ref = refs[pieces] if ready else None
    weight_hbm, _, out_ref, weight_ref, sems = refs[-5:]
    total, columns = out_ref.shape
    whole = columns // 256 * 256
    stream = weight_ref.shape[0]
    chunk = 1024
    copies = [
        pltpu.make_async_copy(
            weight_hbm.at[start + ready + k : start + ready + k + chunk],
            weight_ref.at[k : k + chunk],
            sems.at[k // chunk],
        )
        for k in range(0, stream, chunk)
    ]
    for copy in copies:
        copy.start()

    def rows_of(at, length):
        return jnp.concatenate([p[:, at : at + length] for p in refs[:pieces]], axis=0)

    def dot(x, weight):
        return jnp.dot(x, weight, preferred_element_type=jnp.float32)

    if whole and ready:
        out_ref[:, :whole] = dot(rows_of(start, ready), ready_ref[:, :whole])
    last = stream - chunk
    for k, length in ((0, last), (last, chunk)):
        for copy in copies[k // chunk : (k + length) // chunk]:
            copy.wait()
        if whole:
            x = rows_of(start + ready + k, length)
            term = dot(x, weight_ref[k : k + length, :whole])
            out_ref[:, :whole] = term if k == 0 and not ready else out_ref[:, :whole] + term
    if columns > whole:
        weight = weight_ref[:, whole:]
        if ready:
            weight = jnp.concatenate([ready_ref[:, whole:], weight], axis=0)
        half = (ready + stream) // 2
        if columns - whole == 128:
            left = jnp.concatenate([rows_of(start, half), rows_of(start + half, half)], axis=0)
            both = dot(left, jnp.concatenate([weight[:half], weight[half:]], axis=1))
            out_ref[:, whole:] = both[:total, :128] + both[total:, 128:]
        else:
            out_ref[:, whole:] = dot(rows_of(start, ready + stream), weight)


def lift_kernel(count, rows, pieces, bounds, rank, *refs):
    tag_refs, refs = refs[:pieces], refs[pieces:]
    (down_ref, up_ref), base_refs, (out_ref, sum_ref) = refs[:2], refs[2:-2], refs[-2:]
    total = count * rows
    me = lax.axis_index(AXIS)
    adapters, per, columns = up_ref.shape
    wide = adapters * per
    row, column = iota((total, total), 0), iota((total, total), 1)
    order = one_hot(place_of(column, me, count, rows) == row)
    back = one_hot(place_of(row, me, count, rows) == column)
    folded = down_ref[...].astype(jnp.float32)
    folds = folded.shape[1] // total
    down = jnp.concatenate([folded[:, f * total : (f + 1) * total] for f in range(folds)], axis=0)
    down = lax.dot_general(
        back, down.astype(jnp.bfloat16), NT, preferred_element_type=jnp.float32
    ).astype(jnp.bfloat16)
    names = jnp.concatenate([t[...] for t in tag_refs], axis=0).astype(jnp.float32)[:, :1]
    named = (iota((total, wide), 1) // per).astype(jnp.float32) == names
    start = me * columns
    value = base_refs[0][...]
    for b in base_refs[1:]:
        value = value + b[...]
    sum_ref[...] = value
    for g in range(rank // per):
        low, high = bounds[g], bounds[g + 1]

        @pl.when((start < high) & (start + columns > low))
        def _():
            at = iota((rank, wide), 1) % per + g * per
            spread = one_hot(at == iota((rank, wide), 0))
            copies = jnp.dot(down, spread, preferred_element_type=jnp.float32)
            chosen = jnp.where(named, copies, 0.0).astype(jnp.bfloat16)
            up = up_ref[...].reshape(wide, columns)
            lifted = jnp.dot(chosen, up, preferred_element_type=jnp.float32)
            at = iota((total, columns), 1) + start
            sum_ref[...] += jnp.where((at >= low) & (at < high), lifted, 0.0)

    placed = jnp.dot(
        order, sum_ref[...].astype(jnp.bfloat16), preferred_element_type=jnp.float32
    ).astype(jnp.bfloat16)
    for d in range(count):
        out_ref[d] = placed[d * rows : (d + 1) * rows]


def attend_kernel(lengths_ref, qkv_ref, keys_ref, values_ref, out_ref):
    rows, kv_heads, context, dim = keys_ref.shape
    width = out_ref.shape[1]
    groups = width // dim // kv_heads
    per_head = groups * rows
    together = max(1, LANES // per_head)
    lanes = together * per_head
    lane = iota((1, lanes), 1)
    length = jnp.zeros((1, lanes), jnp.int32)
    for b in range(rows):
        length = jnp.where(lane % rows == b, lengths_ref[b], length)
    live = iota((context, lanes), 0) < length
    request = iota((per_head, 1), 0) % rows
    scale = dim ** (-0.5)

    def columns(at):
        return qkv_ref[:, at : at + dim].astype(jnp.float32)

    for first in range(0, kv_heads, together):
        heads = range(first, first + together)
        query = jnp.concatenate(
            [columns((h * groups + g) * dim) for h in heads for g in range(groups)], axis=0
        )
        key = jnp.concatenate([columns(width + h * dim) for h in heads for _ in range(groups)], axis=0)
        at = width + kv_heads * dim
        value = jnp.concatenate([columns(at + h * dim) for h in heads for _ in range(groups)], axis=0)
        half = query.astype(jnp.bfloat16)
        scores = jnp.zeros((context, lanes), jnp.float32)
        for n, h in enumerate(heads):
            cached = keys_ref[:, h].reshape(rows * context, dim)
            every = lax.dot_general(cached, half, NT, preferred_element_type=jnp.float32)
            for b in range(rows):
                mine = (lane // per_head == n) & (lane % rows == b)
                scores = jnp.where(mine, every[b * context : (b + 1) * context], scores)
        scores = jnp.where(live, scores * scale, -1e30)
        own = jnp.sum((query * key).T, axis=0, keepdims=True) * scale
        peak = jnp.maximum(jnp.max(scores, axis=0, keepdims=True), own)
        weights = jnp.exp(scores - peak)
        own_weight = jnp.exp(own - peak)
        denominator = jnp.sum(weights, axis=0, keepdims=True) + own_weight
        probs = (weights / denominator).T.astype(jnp.bfloat16)
        own_prob = (own_weight / denominator).astype(jnp.bfloat16).astype(jnp.float32)
        own_term = jnp.broadcast_to(own_prob, (dim, lanes)).T * value
        for n, h in enumerate(heads):
            span = slice(n * per_head, (n + 1) * per_head)
            mixed = jnp.zeros((per_head, dim), jnp.float32)
            for b in range(rows):
                one = jnp.dot(probs[span], values_ref[b, h], preferred_element_type=jnp.float32)
                mixed = jnp.where(request == b, one, mixed)
            mixed = (mixed + own_term[span]).astype(jnp.bfloat16)
            for g in range(groups):
                at = (h * groups + g) * dim
                out_ref[:, at : at + dim] = mixed[g * rows : (g + 1) * rows]


def local(
    input_hidden,
    input_norm_gain,
    request_adapter,
    adapter_storage,
    lengths,
    projection_weight,
    output_weight,
    adapter_down,
    projection_up_adapter,
    output_up_adapter,
    cache_keys,
    cache_values,
    *,
    count,
):
    rows, width = input_hidden.shape
    rank = projection_up_adapter.shape[1]
    held = adapter_down.shape[0]
    kv_heads, context, head_dim = cache_keys.shape[1:]
    kv_width = kv_heads * head_dim
    total = rows * count
    bf16, f32 = jnp.bfloat16, jnp.float32
    params = pltpu.CompilerParams(vmem_limit_bytes=(16 if total <= 64 else 60) * 1024 * 1024)
    own_maps = jnp.swapaxes(adapter_down, 1, 2)

    normed, first_maps, first_rows = pl.pallas_call(
        norm_kernel,
        out_shape=[
            VMEM((rows, width + LANES), bf16),
            VMEM((held, 3 * rank, width), bf16),
            VMEM((1024, projection_weight.shape[1]), bf16),
        ],
        in_specs=[spec(pltpu.HBM)] * 6,
        out_specs=[spec()] * 3,
        scratch_shapes=[
            VMEM((rows, width), bf16),
            VMEM((width,), bf16),
            SMEM((rows,), jnp.int32),
            SMEM(adapter_storage.shape, jnp.int32),
            pltpu.SemaphoreType.DMA((6,)),
        ],
        compiler_params=params,
        name="norm",
    )(
        hbm(input_hidden),
        hbm(input_norm_gain),
        hbm(request_adapter.reshape(rows)),
        hbm(adapter_storage),
        hbm(own_maps),
        hbm(projection_weight),
    )

    def tag_specs(pieces):
        return [pl.BlockSpec((p.shape[0], LANES), lambda i: (0, width // LANES)) for p in pieces]

    def downs(own, sibling, pieces, tagged, low, high):
        ranks = high - low
        lanes = max(LANES, total)
        whole = lambda x: pl.BlockSpec(x.shape, lambda i: (0,) * x.ndim)
        own_spec = pl.BlockSpec((held, ranks, width), lambda i: (0, low // ranks, 0))
        shapes = [jax.ShapeDtypeStruct((ranks * total // lanes, lanes), bf16)]
        if low == 0:
            rest = sibling.shape[1] - ranks
            shapes.append(jax.ShapeDtypeStruct((held, rest, width), bf16))
        return pl.pallas_call(
            functools.partial(down_kernel, count, rows, len(pieces), (low, high)),
            grid=(1,),
            out_shape=shapes,
            in_specs=[own_spec, whole(sibling)]
            + [pl.BlockSpec((p.shape[0], width), lambda i: (0, 0)) for p in pieces]
            + tag_specs(tagged),
            out_specs=[whole(x) for x in shapes],
            compiler_params=params,
            cost_estimate=pl.CostEstimate(
                flops=2 * total * width * held * ranks,
                bytes_accessed=2 * width * (2 * held * ranks + total),
                transcendentals=0,
            ),
            name="down",
        )(own, sibling, *pieces, *tagged)

    def load(after, weight, start, length):
        columns = weight.shape[1]
        return pl.pallas_call(
            functools.partial(load_kernel, start),
            out_shape=VMEM((length, columns), bf16),
            in_specs=[spec(pl.ANY), spec(pltpu.HBM)],
            out_specs=spec(),
            scratch_shapes=[pltpu.SemaphoreType.DMA((length // 512,))],
            compiler_params=params,
            cost_estimate=pl.CostEstimate(
                flops=0, bytes_accessed=4 * length * columns, transcendentals=0
            ),
            name="load",
        )(after, hbm(weight))

    def base(pieces, weight, after, start, ready, length):
        columns = weight.shape[1]
        first = [] if ready is None else [ready]
        stream = length - sum(r.shape[0] for r in first)
        return pl.pallas_call(
            functools.partial(base_kernel, len(pieces), start, length - stream),
            out_shape=jax.ShapeDtypeStruct((total, columns), f32),
            in_specs=[spec()] * (len(pieces) + len(first)) + [spec(pltpu.HBM), spec(pl.ANY)],
            out_specs=spec(),
            scratch_shapes=[
                VMEM((stream, columns), bf16),
                pltpu.SemaphoreType.DMA((stream // 1024,)),
            ],
            compiler_params=params,
            cost_estimate=pl.CostEstimate(
                flops=2 * total * length * columns,
                bytes_accessed=4 * length * columns,
                transcendentals=0,
            ),
            name="base",
        )(*pieces, *first, hbm(weight), after)

    def lift(down, tagged, up, base_terms, bounds, ranks):
        columns = up.shape[2]
        whole = lambda x: pl.BlockSpec(x.shape, lambda i: (0,) * x.ndim)
        operands = [down, up] + base_terms
        return pl.pallas_call(
            functools.partial(lift_kernel, count, rows, len(tagged), bounds, ranks),
            grid=(1,),
            out_shape=jax.ShapeDtypeStruct((count, rows, columns), bf16),
            in_specs=tag_specs(tagged) + [whole(x) for x in operands],
            out_specs=pl.BlockSpec((count, rows, columns), lambda i: (0, 0, 0)),
            scratch_shapes=[VMEM((total, columns), f32)],
            compiler_params=params,
            name="lift",
        )(*tagged, *operands)

    def project(x, tagged, own, sibling, ready, low, high, weight, up, bounds):
        half = width // 2

        def beside(rows_here):
            return None if ready is None else load(rows_here, weight, half, ready.shape[0])

        column, pieces, loaded, swapped = gather_rows(x, count, beside, sibling[0])
        tagged = pieces if tagged is None else tagged
        theirs = sibling[1] if swapped is None else jnp.swapaxes(swapped, 1, 2)

        def term(turn, after):
            if turn > 1:
                return None
            return base(pieces, weight, after, turn * half, (ready, loaded)[turn], half)

        down, *rest = downs(own, theirs, column, tagged[: len(column)], low, high)
        down, base_terms = sum_over(down, count, term)
        columns = lift(down, tagged, up, base_terms, bounds, high - low)
        mine = exchange(columns)
        return jnp.swapaxes(mine, 0, 1).reshape(rows, -1), tagged, rest

    bounds = (0, width, width + kv_width, width + 2 * kv_width)
    qkv_mine, tagged, rest = project(
        normed,
        None,
        first_maps,
        (adapter_down, None),
        first_rows,
        0,
        3 * rank,
        projection_weight,
        projection_up_adapter,
        bounds,
    )
    attended = pl.pallas_call(
        attend_kernel,
        out_shape=jax.ShapeDtypeStruct((rows, width), bf16),
        in_specs=[spec(SMEM)] + [spec()] * 3,
        out_specs=spec(),
        compiler_params=params,
        cost_estimate=pl.CostEstimate(
            flops=4 * rows * width * context,
            bytes_accessed=4 * cache_keys.size,
            transcendentals=rows * width // head_dim * context,
        ),
        name="attend",
    )(lengths, qkv_mine, cache_keys, cache_values)
    output, _, _ = project(
        attended,
        tagged,
        own_maps,
        (None, rest[0]),
        None,
        3 * rank,
        4 * rank,
        output_weight,
        output_up_adapter,
        (0, width),
    )
    return output


def solution(mesh):
    count = mesh.shape[AXIS]

    def body(*arrays):
        return local(*arrays, count=count)

    return jax.shard_map(
        body,
        mesh=mesh,
        in_specs=(
            P(("groups", "tensor"), None),
            P(),
            P(("groups", "tensor"), None),
            P(),
            P(("groups", "tensor")),
            P(None, "tensor"),
            P(None, "tensor"),
            P("tensor", None, None),
            P(None, None, "tensor"),
            P(None, None, "tensor"),
            P(("groups", "tensor"), None, None, None),
            P(("groups", "tensor"), None, None, None),
        ),
        out_specs=P(("groups", "tensor"), None),
        check_vma=False,
    )
```

```python
import functools

import jax
import jax.numpy as jnp
from jax import lax
from jax.experimental import pallas as pl
from jax.experimental.pallas import tpu as pltpu
from jax.sharding import PartitionSpec as P

eps = 1e-05
AXIS = "tensor"
LANES = 128
VMEM = pltpu.VMEM
SMEM = pltpu.SMEM


def swap(x, count, offset):
    return lax.ppermute(x, AXIS, [(i, i ^ offset) for i in range(count)])


def exchange(x, groups=None):
    return lax.all_to_all(
        x, AXIS, split_axis=0, concat_axis=0, axis_index_groups=groups, tiled=True
    )


def sum_over(x, count, beside):
    step, turn, terms = count, 0, []
    while step > 1:
        radix = 4 if step % 4 == 0 else 2
        step //= radix
        others = [swap(x, count, k * step) for k in range(1, radix)]
        term = beside(turn, x)
        if term is not None:
            *others, term = lax.optimization_barrier((*others, term))
        terms.append(term)
        for other in others:
            x = x + other
        turn += 1
    return x, [t for t in terms if t is not None]


def pack_kernel(*refs):
    *in_refs, out_ref = refs
    rows, width = in_refs[0].shape
    per = 16 // rows
    for first in range(0, len(in_refs), per):
        parts = [r[...].astype(jnp.float32) for r in in_refs[first : first + per]]
        at = slice(first * rows, (first + per) * rows)
        out_ref[at] = jnp.concatenate(parts, axis=0).astype(jnp.bfloat16)


def pack(parts):
    rows, width = parts[0].shape
    return pl.pallas_call(
        pack_kernel,
        out_shape=jax.ShapeDtypeStruct((rows * len(parts), width), jnp.bfloat16),
        in_specs=[spec()] * len(parts),
        out_specs=spec(),
        compiler_params=pltpu.CompilerParams(vmem_limit_bytes=16 * 1024 * 1024),
        name="pack",
    )(*parts)


def gather_rows(x, count):
    step = count // 4
    far, middle, near = (swap(x, count, k * step) for k in (3, 2, 1))
    step //= 2
    across = [swap(p, count, step) for p in (x, far, middle, near)]
    parts = [x, near, middle, far] + [across[i] for i in (0, 3, 2, 1)]
    held = [pack(parts)]
    step //= 2
    while step > 1:
        held = held + [swap(h, count, step) for h in held]
        step //= 2
    return held, held + [swap(h, count, 1) for h in held]


def place_of(row, me, count, rows):
    block = row // rows
    source = (block % 4) * (count // 4)
    piece, step = block // 4, count // 8
    while step:
        source = source + (piece % 2) * step
        piece, step = piece // 2, step // 2
    return (source ^ me) * rows + row % rows


def spec(space=VMEM):
    return pl.BlockSpec(memory_space=space)


def hbm(x):
    return pltpu.with_memory_space_constraint(x, pltpu.HBM)


def iota(shape, dim):
    return lax.broadcasted_iota(jnp.int32, shape, dim)


def one_hot(condition):
    return jnp.where(condition, 1.0, 0.0).astype(jnp.bfloat16)


def norm_kernel(
    hidden_hbm,
    gain_hbm,
    names_hbm,
    slots_hbm,
    maps_hbm,
    weight_hbm,
    out_ref,
    maps_ref,
    weight_ref,
    hidden_ref,
    gain_ref,
    names_ref,
    slots_ref,
    sems,
):
    ranks = maps_ref.shape[1]
    copies = [
        pltpu.make_async_copy(source, target, sems.at[i])
        for i, (source, target) in enumerate(
            (
                (hidden_hbm, hidden_ref),
                (gain_hbm, gain_ref),
                (names_hbm, names_ref),
                (slots_hbm, slots_ref),
                (maps_hbm.at[:, :ranks], maps_ref),
                (weight_hbm.at[: weight_ref.shape[0]], weight_ref),
            )
        )
    ]
    for copy in copies:
        copy.start()
    for copy in copies[:4]:
        copy.wait()
    rows, width = hidden_ref.shape
    hidden = hidden_ref[...].astype(jnp.float32)
    power = jnp.sum(hidden * hidden, axis=1, keepdims=True) / width
    gain = gain_ref[...].reshape(1, width).astype(jnp.float32)
    out_ref[:, :width] = (hidden * lax.rsqrt(power + eps) * gain).astype(jnp.bfloat16)
    row, lane = iota((rows, LANES), 0), iota((rows, LANES), 1)
    tags = jnp.zeros((rows, LANES), jnp.float32)
    for r in range(rows):
        name = names_ref[r]
        tag = jnp.where(lane < LANES // 2, name, slots_ref[name]).astype(jnp.float32)
        tags = jnp.where(row == r, tag, tags)
    out_ref[:, width:] = tags.astype(jnp.bfloat16)
    for copy in copies[4:]:
        copy.wait()


NT = (((1,), (1,)), ((), ()))


def rows_copy(weight_hbm, start, rows_ref, sem):
    return pltpu.make_async_copy(weight_hbm.at[start : start + rows_ref.shape[0]], rows_ref, sem)


def down_kernel(count, rows, pieces, ranks, *refs):
    map_refs, piece_refs = refs[:2], refs[2 : 2 + pieces]
    tag_refs, refs = refs[2 + pieces : 2 + 2 * pieces], refs[2 + 2 * pieces :]
    if len(refs) > 1:
        weight_hbm, out_ref, rest_ref, rows_ref, sems = refs
        copy = rows_copy(weight_hbm, weight_hbm.shape[0] // 2, rows_ref, sems.at[0])
        copy.start()
    else:
        (out_ref,) = refs
    me = lax.axis_index(AXIS)
    held, _, width = map_refs[0].shape
    rank = ranks[1] - ranks[0]
    total, half = count * rows, count * rows // 2
    chunk = 4096
    sums = jnp.zeros((2 * held * rank, half), jnp.float32)
    for k in range(0, width, chunk):
        x = jnp.concatenate([p[:, k : k + chunk] for p in piece_refs], axis=0)
        maps = jnp.concatenate(
            [m[:, :rank, k : k + chunk].reshape(held * rank, chunk) for m in map_refs], axis=0
        )
        sums = sums + lax.dot_general(maps, x, NT, preferred_element_type=jnp.float32)
    if len(refs) > 1:
        rest_ref[...] = map_refs[1][:, rank:]
    tags = jnp.concatenate([t[...] for t in tag_refs], axis=0)
    pick = one_hot(iota((16, LANES), 1) == LANES // 2)
    slots = lax.dot_general(pick, tags, NT, preferred_element_type=jnp.float32)[:1]
    chosen = jnp.zeros((rank, half), jnp.float32)
    for m in range(2):
        for s in range(held):
            slot = ((me ^ m) * held + s).astype(jnp.float32)
            at = (m * held + s) * rank
            chosen = jnp.where(slots == slot, sums[at : at + rank], chosen)
    row, column = iota((half, total), 0), iota((half, total), 1)
    back = one_hot(place_of(row, me, count, rows) == column)
    placed = jnp.dot(chosen.astype(jnp.bfloat16), back, preferred_element_type=jnp.float32)
    folds = out_ref.shape[1] // total
    part = rank // folds
    folded = [placed[f * part : (f + 1) * part] for f in range(folds)]
    value = jnp.concatenate(folded, axis=1).astype(jnp.bfloat16)
    out_ref[...] = value
    if len(refs) > 1:
        copy.wait()


def base_kernel(pieces, start, ready, *refs):
    ready_ref = refs[pieces]
    weight_hbm, _, out_ref, weight_ref, sems = refs[pieces + 1 :]
    total, columns = out_ref.shape
    whole = columns // 256 * 256
    stream = weight_ref.shape[0]
    spans = [(k, 1024) for k in range(0, stream - 1024, 1024)]
    spans += [(stream - 1024, 512), (stream - 512, 512)]
    copies = [
        pltpu.make_async_copy(
            weight_hbm.at[start + ready + k : start + ready + k + length],
            weight_ref.at[k : k + length],
            sems.at[i],
        )
        for i, (k, length) in enumerate(spans)
    ]
    for copy in copies:
        copy.start()

    def dot(x, weight):
        return jnp.dot(x, weight, preferred_element_type=jnp.float32)

    steps = [(ready_ref, k, 1024, k, None) for k in range(0, ready, 1024)]
    steps += [(weight_ref, k, n, ready + k, copy) for (k, n), copy in zip(spans, copies)]
    for from_ref, k, length, offset, copy in steps:
        at = start + offset
        x = jnp.concatenate([p[:, at : at + length] for p in refs[:pieces]], axis=0)
        if copy is not None:
            copy.wait()
        terms = []
        if whole:
            terms.append(dot(x, from_ref[k : k + length, :whole]))
        if columns - whole == 128:
            half = length // 2
            left = jnp.concatenate([x[:, :half], x[:, half:]], axis=0)
            right = [from_ref[k + h : k + h + half, whole:] for h in (0, half)]
            both = dot(left, jnp.concatenate(right, axis=1))
            terms.append(both[:total, :128] + both[total:, 128:])
        elif columns > whole:
            terms.append(dot(x, from_ref[k : k + length, whole:]))
        term = terms[0] if len(terms) == 1 else jnp.concatenate(terms, axis=1)
        out_ref[...] = term if offset == 0 else out_ref[...] + term


def lift_kernel(count, rows, pieces, bounds, rank, *refs):
    tag_refs, refs = refs[:pieces], refs[pieces:]
    (down_ref, up_ref), base_refs, (out_ref, sum_ref) = refs[:2], refs[2:-2], refs[-2:]
    total = count * rows
    me = lax.axis_index(AXIS)
    adapters, per, columns = up_ref.shape
    wide = adapters * per
    row, column = iota((total, total), 0), iota((total, total), 1)
    order = one_hot(place_of(column, me, count, rows) == row)
    back = one_hot(place_of(row, me, count, rows) == column)
    folded = down_ref[...].astype(jnp.float32)
    folds = folded.shape[1] // total
    down = jnp.concatenate([folded[:, f * total : (f + 1) * total] for f in range(folds)], axis=0)
    down = lax.dot_general(
        back, down.astype(jnp.bfloat16), NT, preferred_element_type=jnp.float32
    ).astype(jnp.bfloat16)
    names = jnp.concatenate([t[...] for t in tag_refs], axis=0).astype(jnp.float32)[:, :1]
    named = (iota((total, wide), 1) // per).astype(jnp.float32) == names
    start = me * columns
    value = base_refs[0][...]
    for b in base_refs[1:]:
        value = value + b[...]
    sum_ref[...] = value
    for g in range(rank // per):
        low, high = bounds[g], bounds[g + 1]

        @pl.when((start < high) & (start + columns > low))
        def _():
            at = iota((rank, wide), 1) % per + g * per
            spread = one_hot(at == iota((rank, wide), 0))
            copies = jnp.dot(down, spread, preferred_element_type=jnp.float32)
            chosen = jnp.where(named, copies, 0.0).astype(jnp.bfloat16)
            up = up_ref[...].reshape(wide, columns)
            lifted = jnp.dot(chosen, up, preferred_element_type=jnp.float32)
            at = iota((total, columns), 1) + start
            sum_ref[...] += jnp.where((at >= low) & (at < high), lifted, 0.0)

    placed = jnp.dot(
        order, sum_ref[...].astype(jnp.bfloat16), preferred_element_type=jnp.float32
    ).astype(jnp.bfloat16)
    for d in range(count):
        out_ref[d] = placed[d * rows : (d + 1) * rows]


def attend_kernel(
    lengths_ref, qkv_ref, keys_ref, values_ref, weight_hbm, out_ref, low_ref, high_ref, sems
):
    copies = [
        rows_copy(weight_hbm, 0, low_ref, sems.at[0]),
        rows_copy(weight_hbm, weight_hbm.shape[0] // 2, high_ref, sems.at[1]),
    ]
    for copy in copies:
        copy.start()
    rows, kv_heads, context, dim = keys_ref.shape
    width = out_ref.shape[1]
    groups = width // dim // kv_heads
    per_head = groups * rows
    together = max(1, LANES // per_head)
    lanes = together * per_head
    lane = iota((1, lanes), 1)
    length = jnp.zeros((1, lanes), jnp.int32)
    for b in range(rows):
        length = jnp.where(lane % rows == b, lengths_ref[b], length)
    live = iota((context, lanes), 0) < length
    request = iota((per_head, 1), 0) % rows
    scale = dim ** (-0.5)

    def columns(at):
        return qkv_ref[:, at : at + dim].astype(jnp.float32)

    for first in range(0, kv_heads, together):
        heads = range(first, first + together)
        query = jnp.concatenate(
            [columns((h * groups + g) * dim) for h in heads for g in range(groups)], axis=0
        )
        key = jnp.concatenate([columns(width + h * dim) for h in heads for _ in range(groups)], axis=0)
        at = width + kv_heads * dim
        value = jnp.concatenate([columns(at + h * dim) for h in heads for _ in range(groups)], axis=0)
        half = query.astype(jnp.bfloat16)
        scores = jnp.zeros((context, lanes), jnp.float32)
        for n, h in enumerate(heads):
            cached = keys_ref[:, h].reshape(rows * context, dim)
            every = lax.dot_general(cached, half, NT, preferred_element_type=jnp.float32)
            for b in range(rows):
                mine = (lane // per_head == n) & (lane % rows == b)
                scores = jnp.where(mine, every[b * context : (b + 1) * context], scores)
        scores = jnp.where(live, scores * scale, -1e30)
        own = jnp.sum((query * key).T, axis=0, keepdims=True) * scale
        peak = jnp.maximum(jnp.max(scores, axis=0, keepdims=True), own)
        weights = jnp.exp(scores - peak)
        own_weight = jnp.exp(own - peak)
        denominator = jnp.sum(weights, axis=0, keepdims=True) + own_weight
        probs = (weights / denominator).T.astype(jnp.bfloat16)
        own_prob = (own_weight / denominator).astype(jnp.bfloat16).astype(jnp.float32)
        own_term = jnp.broadcast_to(own_prob, (dim, lanes)).T * value
        for n, h in enumerate(heads):
            span = slice(n * per_head, (n + 1) * per_head)
            mixed = jnp.zeros((per_head, dim), jnp.float32)
            for b in range(rows):
                one = jnp.dot(probs[span], values_ref[b, h], preferred_element_type=jnp.float32)
                mixed = jnp.where(request == b, one, mixed)
            mixed = (mixed + own_term[span]).astype(jnp.bfloat16)
            for g in range(groups):
                at = (h * groups + g) * dim
                out_ref[:, at : at + dim] = mixed[g * rows : (g + 1) * rows]
    for copy in copies:
        copy.wait()


def local(
    input_hidden,
    input_norm_gain,
    request_adapter,
    adapter_storage,
    lengths,
    projection_weight,
    output_weight,
    adapter_down,
    projection_up_adapter,
    output_up_adapter,
    cache_keys,
    cache_values,
    *,
    count,
):
    rows, width = input_hidden.shape
    rank = projection_up_adapter.shape[1]
    held = adapter_down.shape[0]
    kv_heads, context, head_dim = cache_keys.shape[1:]
    kv_width = kv_heads * head_dim
    total = rows * count
    bf16, f32 = jnp.bfloat16, jnp.float32
    params = pltpu.CompilerParams(vmem_limit_bytes=(16 if total <= 64 else 60) * 1024 * 1024)
    own_maps = jnp.swapaxes(adapter_down, 1, 2)

    normed, first_maps, first_rows = pl.pallas_call(
        norm_kernel,
        out_shape=[
            VMEM((rows, width + LANES), bf16),
            VMEM((held, 3 * rank, width), bf16),
            VMEM((1024, projection_weight.shape[1]), bf16),
        ],
        in_specs=[spec(pltpu.HBM)] * 6,
        out_specs=[spec()] * 3,
        scratch_shapes=[
            VMEM((rows, width), bf16),
            VMEM((width,), bf16),
            SMEM((rows,), jnp.int32),
            SMEM(adapter_storage.shape, jnp.int32),
            pltpu.SemaphoreType.DMA((6,)),
        ],
        compiler_params=params,
        name="norm",
    )(
        hbm(input_hidden),
        hbm(input_norm_gain),
        hbm(request_adapter.reshape(rows)),
        hbm(adapter_storage),
        hbm(own_maps),
        hbm(projection_weight),
    )

    def tag_specs(pieces):
        return [pl.BlockSpec((p.shape[0], LANES), lambda i: (0, width // LANES)) for p in pieces]

    def downs(own, sibling, pieces, tagged, low, high, weight):
        ranks = high - low
        lanes = max(LANES, total)
        whole = lambda x: pl.BlockSpec(x.shape, lambda i: (0,) * len(x.shape))
        own_spec = pl.BlockSpec((held, ranks, width), lambda i: (0, low // ranks, 0))
        outs = [jax.ShapeDtypeStruct((ranks * total // lanes, lanes), bf16)]
        extra = []
        if low == 0:
            rest = sibling.shape[1] - ranks
            outs.append(jax.ShapeDtypeStruct((held, rest, width), bf16))
            extra = [hbm(weight)]
        out_specs = [whole(x) for x in outs]
        if extra:
            outs.append(VMEM((1024, weight.shape[1]), bf16))
            out_specs.append(spec(pl.ANY))
        return pl.pallas_call(
            functools.partial(down_kernel, count, rows, len(pieces), (low, high)),
            grid=(1,),
            out_shape=outs,
            in_specs=[own_spec, whole(sibling)]
            + [pl.BlockSpec((p.shape[0], width), lambda i: (0, 0)) for p in pieces]
            + tag_specs(tagged)
            + [spec(pltpu.HBM)] * len(extra),
            out_specs=out_specs,
            scratch_shapes=[pltpu.SemaphoreType.DMA((1,))] * len(extra),
            compiler_params=params,
            cost_estimate=pl.CostEstimate(
                flops=2 * total * width * held * ranks,
                bytes_accessed=2 * width * (2 * held * ranks + total),
                transcendentals=0,
            ),
            name="down",
        )(own, sibling, *pieces, *tagged, *extra)

    def base(pieces, weight, after, start, ready, length):
        columns = weight.shape[1]
        stream = length - ready.shape[0]
        return pl.pallas_call(
            functools.partial(base_kernel, len(pieces), start, length - stream),
            out_shape=jax.ShapeDtypeStruct((total, columns), f32),
            in_specs=[spec()] * (len(pieces) + 1) + [spec(pltpu.HBM), spec(pl.ANY)],
            out_specs=spec(),
            scratch_shapes=[
                VMEM((stream, columns), bf16),
                pltpu.SemaphoreType.DMA((stream // 1024 + 1,)),
            ],
            compiler_params=params,
            cost_estimate=pl.CostEstimate(
                flops=2 * total * length * columns,
                bytes_accessed=4 * length * columns,
                transcendentals=0,
            ),
            name="base",
        )(*pieces, ready, hbm(weight), after)

    def lift(down, tagged, up, base_terms, bounds, ranks):
        columns = up.shape[2]
        whole = lambda x: pl.BlockSpec(x.shape, lambda i: (0,) * x.ndim)
        operands = [down, up] + base_terms
        return pl.pallas_call(
            functools.partial(lift_kernel, count, rows, len(tagged), bounds, ranks),
            grid=(1,),
            out_shape=jax.ShapeDtypeStruct((count, rows, columns), bf16),
            in_specs=tag_specs(tagged) + [whole(x) for x in operands],
            out_specs=pl.BlockSpec((count, rows, columns), lambda i: (0, 0, 0)),
            scratch_shapes=[VMEM((total, columns), f32)],
            compiler_params=params,
            name="lift",
        )(*tagged, *operands)

    def project(column, pieces, tagged, own, sibling, ready, low, high, weight, up, bounds):
        half = width // 2
        down, *rest = downs(own, sibling, column, tagged[: len(column)], low, high, weight)
        ready = ready + rest[1:]

        def term(turn, after):
            if turn > 1:
                return None
            return base(pieces, weight, after, turn * half, ready[turn], half)

        down, base_terms = sum_over(down, count, term)
        columns = lift(down, tagged, up, base_terms, bounds, high - low)
        mine = exchange(columns)
        return jnp.swapaxes(mine, 0, 1).reshape(rows, -1), rest

    bounds = (0, width, width + kv_width, width + 2 * kv_width)
    sibling_maps = jnp.swapaxes(swap(adapter_down, count, 1), 1, 2)
    column, tagged = gather_rows(normed, count)
    qkv_mine, rest = project(
        column,
        tagged,
        tagged,
        first_maps,
        sibling_maps,
        [first_rows],
        0,
        3 * rank,
        projection_weight,
        projection_up_adapter,
        bounds,
    )
    columns = output_weight.shape[1]
    ahead = min(2048, width // 2 - 1024)
    attended, *ready = pl.pallas_call(
        attend_kernel,
        out_shape=[jax.ShapeDtypeStruct((rows, width), bf16)] + [VMEM((ahead, columns), bf16)] * 2,
        in_specs=[spec(SMEM)] + [spec()] * 3 + [spec(pltpu.HBM)],
        out_specs=[spec()] * 3,
        scratch_shapes=[pltpu.SemaphoreType.DMA((2,))],
        compiler_params=params,
        cost_estimate=pl.CostEstimate(
            flops=4 * rows * width * context,
            bytes_accessed=4 * cache_keys.size,
            transcendentals=rows * width // head_dim * context,
        ),
        name="attend",
    )(lengths, qkv_mine, cache_keys, cache_values, hbm(output_weight))
    column, pieces = gather_rows(attended, count)
    output, _ = project(
        column,
        pieces,
        tagged,
        own_maps,
        rest[0],
        ready,
        3 * rank,
        4 * rank,
        output_weight,
        output_up_adapter,
        (0, width),
    )
    return output


def solution(mesh):
    count = mesh.shape[AXIS]

    def body(*arrays):
        return local(*arrays, count=count)

    return jax.shard_map(
        body,
        mesh=mesh,
        in_specs=(
            P(("groups", "tensor"), None),
            P(),
            P(("groups", "tensor"), None),
            P(),
            P(("groups", "tensor")),
            P(None, "tensor"),
            P(None, "tensor"),
            P("tensor", None, None),
            P(None, None, "tensor"),
            P(None, None, "tensor"),
            P(("groups", "tensor"), None, None, None),
            P(("groups", "tensor"), None, None, None),
        ),
        out_specs=P(("groups", "tensor"), None),
        check_vma=False,
    )
```

```python
import functools

import jax
import jax.numpy as jnp
from jax import lax
from jax.experimental import pallas as pl
from jax.experimental.pallas import tpu as pltpu
from jax.sharding import PartitionSpec as P

eps = 1e-05
AXIS = "tensor"
LANES = 128
VMEM = pltpu.VMEM
SMEM = pltpu.SMEM


def swap(x, count, offset):
    return lax.ppermute(x, AXIS, [(i, i ^ offset) for i in range(count)])


def exchange(x, groups=None):
    return lax.all_to_all(
        x, AXIS, split_axis=0, concat_axis=0, axis_index_groups=groups, tiled=True
    )


def sum_over(x, count, beside):
    step, turn, terms = count, 0, []
    while step > 1:
        radix = 4 if step % 4 == 0 else 2
        step //= radix
        others = [swap(x, count, k * step) for k in range(1, radix)]
        term = beside(turn, x)
        if term is not None:
            *others, term = lax.optimization_barrier((*others, term))
        terms.append(term)
        for other in others:
            x = x + other
        turn += 1
    return x, [t for t in terms if t is not None]


def pack_kernel(*refs):
    in_refs, out_ref = refs[-2::-1], refs[-1]
    rows, width = in_refs[0].shape
    per = 16 // rows
    for first in range(0, len(in_refs), per):
        parts = [r[...].astype(jnp.float32) for r in in_refs[first : first + per]]
        at = slice(first * rows, (first + per) * rows)
        out_ref[at] = jnp.concatenate(parts, axis=0).astype(jnp.bfloat16)


def pack(parts):
    rows, width = parts[0].shape
    return pl.pallas_call(
        pack_kernel,
        out_shape=jax.ShapeDtypeStruct((rows * len(parts), width), jnp.bfloat16),
        in_specs=[spec()] * len(parts),
        out_specs=spec(),
        compiler_params=pltpu.CompilerParams(vmem_limit_bytes=16 * 1024 * 1024),
        name="pack",
    )(*parts[::-1])


def gather_rows(x, count):
    step = count // 4
    near, middle, far = (swap(x, count, k * step) for k in (1, 2, 3))
    step //= 2
    across = [swap(p, count, step) for p in (x, near, middle, far)]
    held = [pack([x, near, middle, far] + across)]
    step //= 2
    while step > 1:
        held = held + [swap(h, count, step) for h in held]
        step //= 2
    return held, held + [swap(h, count, 1) for h in held]


def place_of(row, me, count, rows):
    block = row // rows
    source = (block % 4) * (count // 4)
    piece, step = block // 4, count // 8
    while step:
        source = source + (piece % 2) * step
        piece, step = piece // 2, step // 2
    return (source ^ me) * rows + row % rows


def spec(space=VMEM):
    return pl.BlockSpec(memory_space=space)


def hbm(x):
    return pltpu.with_memory_space_constraint(x, pltpu.HBM)


def iota(shape, dim):
    return lax.broadcasted_iota(jnp.int32, shape, dim)


def one_hot(condition):
    return jnp.where(condition, 1.0, 0.0).astype(jnp.bfloat16)


def norm_kernel(
    hidden_hbm,
    gain_hbm,
    names_hbm,
    slots_hbm,
    maps_hbm,
    weight_hbm,
    out_ref,
    maps_ref,
    weight_ref,
    hidden_ref,
    gain_ref,
    names_ref,
    slots_ref,
    sems,
    row_sems,
):
    ranks = maps_ref.shape[1]
    copies = [
        pltpu.make_async_copy(source, target, sems.at[i])
        for i, (source, target) in enumerate(
            (
                (hidden_hbm, hidden_ref),
                (gain_hbm, gain_ref),
                (names_hbm, names_ref),
                (slots_hbm, slots_ref),
                (maps_hbm.at[:, :ranks], maps_ref),
            )
        )
    ] + rows_copies(weight_hbm, 0, weight_ref, row_sems)
    for copy in copies:
        copy.start()
    for copy in copies[:4]:
        copy.wait()
    rows, width = hidden_ref.shape
    hidden = hidden_ref[...].astype(jnp.float32)
    power = jnp.sum(hidden * hidden, axis=1, keepdims=True) / width
    gain = gain_ref[...].reshape(1, width).astype(jnp.float32)
    out_ref[:, :width] = (hidden * lax.rsqrt(power + eps) * gain).astype(jnp.bfloat16)
    row, lane = iota((rows, LANES), 0), iota((rows, LANES), 1)
    tags = jnp.zeros((rows, LANES), jnp.float32)
    for r in range(rows):
        name = names_ref[r]
        tag = jnp.where(lane < LANES // 2, name, slots_ref[name]).astype(jnp.float32)
        tags = jnp.where(row == r, tag, tags)
    out_ref[:, width:] = tags.astype(jnp.bfloat16)
    for copy in copies[4:]:
        copy.wait()


NT = (((1,), (1,)), ((), ()))


def rows_copies(weight_hbm, start, rows_ref, sems):
    length = rows_ref.shape[0] // sems.shape[0]
    return [
        pltpu.make_async_copy(
            weight_hbm.at[start + i * length : start + (i + 1) * length],
            rows_ref.at[i * length : (i + 1) * length],
            sems.at[i],
        )
        for i in range(sems.shape[0])
    ]


def down_kernel(count, rows, pieces, ranks, *refs):
    map_refs, piece_refs = refs[:2], refs[2 : 2 + pieces]
    tag_refs, refs = refs[2 + pieces : 2 + 2 * pieces], refs[2 + 2 * pieces :]
    if len(refs) > 1:
        weight_hbm, out_ref, rest_ref, rows_ref, sems = refs
        copies = rows_copies(weight_hbm, weight_hbm.shape[0] // 2, rows_ref, sems)
        for copy in copies:
            copy.start()
    else:
        (out_ref,) = refs
    me = lax.axis_index(AXIS)
    held, _, width = map_refs[0].shape
    rank = ranks[1] - ranks[0]
    total, half = count * rows, count * rows // 2
    chunk = 4096
    sums = jnp.zeros((2 * held * rank, half), jnp.float32)
    for k in range(0, width, chunk):
        x = jnp.concatenate([p[:, k : k + chunk] for p in piece_refs], axis=0)
        maps = jnp.concatenate(
            [m[:, :rank, k : k + chunk].reshape(held * rank, chunk) for m in map_refs], axis=0
        )
        sums = sums + lax.dot_general(maps, x, NT, preferred_element_type=jnp.float32)
    if len(refs) > 1:
        rest_ref[...] = map_refs[1][:, rank:]
    tags = jnp.concatenate([t[...] for t in tag_refs], axis=0)
    pick = one_hot(iota((16, LANES), 1) == LANES // 2)
    slots = lax.dot_general(pick, tags, NT, preferred_element_type=jnp.float32)[:1]
    chosen = jnp.zeros((rank, half), jnp.float32)
    for m in range(2):
        for s in range(held):
            slot = ((me ^ m) * held + s).astype(jnp.float32)
            at = (m * held + s) * rank
            chosen = jnp.where(slots == slot, sums[at : at + rank], chosen)
    row, column = iota((half, total), 0), iota((half, total), 1)
    back = one_hot(place_of(row, me, count, rows) == column)
    placed = jnp.dot(chosen.astype(jnp.bfloat16), back, preferred_element_type=jnp.float32)
    folds = out_ref.shape[1] // total
    part = rank // folds
    folded = [placed[f * part : (f + 1) * part] for f in range(folds)]
    value = jnp.concatenate(folded, axis=1).astype(jnp.bfloat16)
    out_ref[...] = value
    if len(refs) > 1:
        for copy in copies:
            copy.wait()


def base_kernel(pieces, start, ready, *refs):
    ready_ref = refs[pieces]
    weight_hbm, _, out_ref, weight_ref, sems, side_ref = refs[pieces + 1 :]
    total, columns = out_ref.shape
    whole = columns // 256 * 256
    narrow = columns - whole == 128
    stream = weight_ref.shape[0]
    copies = rows_copies(weight_hbm, start + ready, weight_ref, sems)
    for copy in copies:
        copy.start()
    each = stream // len(copies)

    def rows_of(at, length):
        return jnp.concatenate([p[:, at : at + length] for p in refs[:pieces]], axis=0)

    def dot(x, weight):
        return jnp.dot(x, weight, preferred_element_type=jnp.float32)

    def wide(from_ref, k, length, offset):
        if whole:
            x = rows_of(start + offset, length)
            term = dot(x, from_ref[k : k + length, :whole])
            out_ref[:, :whole] = term if offset == 0 else out_ref[:, :whole] + term

    def rest(weight, offset):
        length = weight.shape[0]
        if narrow:
            half = length // 2
            left = [rows_of(start + offset + h, half) for h in (0, half)]
            right = [weight[:half], weight[half:]]
            term = dot(jnp.concatenate(left, axis=0), jnp.concatenate(right, axis=1))
        else:
            term = dot(rows_of(start + offset, length), weight)
        side_ref[...] = term if offset == 0 else side_ref[...] + term

    wide(ready_ref, 0, ready, 0)
    early = stream - 1024
    for i, copy in enumerate(copies):
        copy.wait()
        at = (i + 1) * each
        if at % 1024 == 0 and at <= early:
            wide(weight_ref, at - 1024, 1024, ready + at - 1024)
        if at == early and columns > whole:
            parts = [ready_ref[:, whole:], weight_ref[:early, whole:]]
            rest(jnp.concatenate(parts, axis=0), 0)
    wide(weight_ref, early, 1024, ready + early)
    if columns > whole:
        rest(weight_ref[early:, whole:], ready + early)
        if narrow:
            out_ref[:, whole:] = side_ref[:total, :128] + side_ref[total:, 128:]
        else:
            out_ref[:, whole:] = side_ref[...]


def lift_kernel(count, rows, pieces, bounds, rank, *refs):
    tag_refs, refs = refs[:pieces], refs[pieces:]
    (down_ref, up_ref), base_refs, (out_ref, sum_ref) = refs[:2], refs[2:-2], refs[-2:]
    total = count * rows
    me = lax.axis_index(AXIS)
    adapters, per, columns = up_ref.shape
    wide = adapters * per
    row, column = iota((total, total), 0), iota((total, total), 1)
    order = one_hot(place_of(column, me, count, rows) == row)
    back = one_hot(place_of(row, me, count, rows) == column)
    folded = down_ref[...].astype(jnp.float32)
    folds = folded.shape[1] // total
    down = jnp.concatenate([folded[:, f * total : (f + 1) * total] for f in range(folds)], axis=0)
    down = lax.dot_general(
        back, down.astype(jnp.bfloat16), NT, preferred_element_type=jnp.float32
    ).astype(jnp.bfloat16)
    names = jnp.concatenate([t[...] for t in tag_refs], axis=0).astype(jnp.float32)[:, :1]
    named = (iota((total, wide), 1) // per).astype(jnp.float32) == names
    start = me * columns
    value = base_refs[0][...]
    for b in base_refs[1:]:
        value = value + b[...]
    sum_ref[...] = value
    for g in range(rank // per):
        low, high = bounds[g], bounds[g + 1]

        @pl.when((start < high) & (start + columns > low))
        def _():
            at = iota((rank, wide), 1) % per + g * per
            spread = one_hot(at == iota((rank, wide), 0))
            copies = jnp.dot(down, spread, preferred_element_type=jnp.float32)
            chosen = jnp.where(named, copies, 0.0).astype(jnp.bfloat16)
            up = up_ref[...].reshape(wide, columns)
            lifted = jnp.dot(chosen, up, preferred_element_type=jnp.float32)
            at = iota((total, columns), 1) + start
            sum_ref[...] += jnp.where((at >= low) & (at < high), lifted, 0.0)

    placed = jnp.dot(
        order, sum_ref[...].astype(jnp.bfloat16), preferred_element_type=jnp.float32
    ).astype(jnp.bfloat16)
    for d in range(count):
        out_ref[d] = placed[d * rows : (d + 1) * rows]


def attend_kernel(
    lengths_ref, qkv_ref, keys_ref, values_ref, weight_hbm, out_ref, low_ref, high_ref, sems
):
    copies = rows_copies(weight_hbm, 0, low_ref, sems.at[0])
    copies += rows_copies(weight_hbm, weight_hbm.shape[0] // 2, high_ref, sems.at[1])
    for copy in copies:
        copy.start()
    rows, kv_heads, context, dim = keys_ref.shape
    width = out_ref.shape[1]
    groups = width // dim // kv_heads
    per_head = groups * rows
    together = max(1, LANES // per_head)
    lanes = together * per_head
    lane = iota((1, lanes), 1)
    length = jnp.zeros((1, lanes), jnp.int32)
    for b in range(rows):
        length = jnp.where(lane % rows == b, lengths_ref[b], length)
    live = iota((context, lanes), 0) < length
    request = iota((per_head, 1), 0) % rows
    scale = dim ** (-0.5)

    def columns(at):
        return qkv_ref[:, at : at + dim].astype(jnp.float32)

    for first in range(0, kv_heads, together):
        heads = range(first, first + together)
        query = jnp.concatenate(
            [columns((h * groups + g) * dim) for h in heads for g in range(groups)], axis=0
        )
        key = jnp.concatenate([columns(width + h * dim) for h in heads for _ in range(groups)], axis=0)
        at = width + kv_heads * dim
        value = jnp.concatenate([columns(at + h * dim) for h in heads for _ in range(groups)], axis=0)
        half = query.astype(jnp.bfloat16)
        scores = jnp.zeros((context, lanes), jnp.float32)
        for n, h in enumerate(heads):
            cached = keys_ref[:, h].reshape(rows * context, dim)
            every = lax.dot_general(cached, half, NT, preferred_element_type=jnp.float32)
            for b in range(rows):
                mine = (lane // per_head == n) & (lane % rows == b)
                scores = jnp.where(mine, every[b * context : (b + 1) * context], scores)
        scores = jnp.where(live, scores * scale, -1e30)
        own = jnp.sum((query * key).T, axis=0, keepdims=True) * scale
        peak = jnp.maximum(jnp.max(scores, axis=0, keepdims=True), own)
        weights = jnp.exp(scores - peak)
        own_weight = jnp.exp(own - peak)
        denominator = jnp.sum(weights, axis=0, keepdims=True) + own_weight
        probs = (weights / denominator).T.astype(jnp.bfloat16)
        own_prob = (own_weight / denominator).astype(jnp.bfloat16).astype(jnp.float32)
        own_term = jnp.broadcast_to(own_prob, (dim, lanes)).T * value
        for n, h in enumerate(heads):
            span = slice(n * per_head, (n + 1) * per_head)
            mixed = jnp.zeros((per_head, dim), jnp.float32)
            for b in range(rows):
                one = jnp.dot(probs[span], values_ref[b, h], preferred_element_type=jnp.float32)
                mixed = jnp.where(request == b, one, mixed)
            mixed = (mixed + own_term[span]).astype(jnp.bfloat16)
            for g in range(groups):
                at = (h * groups + g) * dim
                out_ref[:, at : at + dim] = mixed[g * rows : (g + 1) * rows]
    for copy in copies:
        copy.wait()


def local(
    input_hidden,
    input_norm_gain,
    request_adapter,
    adapter_storage,
    lengths,
    projection_weight,
    output_weight,
    adapter_down,
    projection_up_adapter,
    output_up_adapter,
    cache_keys,
    cache_values,
    *,
    count,
):
    rows, width = input_hidden.shape
    rank = projection_up_adapter.shape[1]
    held = adapter_down.shape[0]
    kv_heads, context, head_dim = cache_keys.shape[1:]
    kv_width = kv_heads * head_dim
    total = rows * count
    bf16, f32 = jnp.bfloat16, jnp.float32
    params = pltpu.CompilerParams(vmem_limit_bytes=(16 if total <= 64 else 60) * 1024 * 1024)
    own_maps = jnp.swapaxes(adapter_down, 1, 2)

    normed, first_maps, first_rows = pl.pallas_call(
        norm_kernel,
        out_shape=[
            VMEM((rows, width + LANES), bf16),
            VMEM((held, 3 * rank, width), bf16),
            VMEM((1024, projection_weight.shape[1]), bf16),
        ],
        in_specs=[spec(pltpu.HBM)] * 6,
        out_specs=[spec()] * 3,
        scratch_shapes=[
            VMEM((rows, width), bf16),
            VMEM((width,), bf16),
            SMEM((rows,), jnp.int32),
            SMEM(adapter_storage.shape, jnp.int32),
            pltpu.SemaphoreType.DMA((5,)),
            pltpu.SemaphoreType.DMA((4,)),
        ],
        compiler_params=params,
        name="norm",
    )(
        hbm(input_hidden),
        hbm(input_norm_gain),
        hbm(request_adapter.reshape(rows)),
        hbm(adapter_storage),
        hbm(own_maps),
        hbm(projection_weight),
    )

    def tag_specs(pieces):
        return [pl.BlockSpec((p.shape[0], LANES), lambda i: (0, width // LANES)) for p in pieces]

    def downs(own, sibling, pieces, tagged, low, high, weight):
        ranks = high - low
        lanes = max(LANES, total)
        whole = lambda x: pl.BlockSpec(x.shape, lambda i: (0,) * len(x.shape))
        own_spec = pl.BlockSpec((held, ranks, width), lambda i: (0, low // ranks, 0))
        outs = [jax.ShapeDtypeStruct((ranks * total // lanes, lanes), bf16)]
        extra = []
        if low == 0:
            rest = sibling.shape[1] - ranks
            outs.append(jax.ShapeDtypeStruct((held, rest, width), bf16))
            extra = [hbm(weight)]
        out_specs = [whole(x) for x in outs]
        if extra:
            outs.append(VMEM((1024, weight.shape[1]), bf16))
            out_specs.append(spec(pl.ANY))
        return pl.pallas_call(
            functools.partial(down_kernel, count, rows, len(pieces), (low, high)),
            grid=(1,),
            out_shape=outs,
            in_specs=[own_spec, whole(sibling)]
            + [pl.BlockSpec((p.shape[0], width), lambda i: (0, 0)) for p in pieces]
            + tag_specs(tagged)
            + [spec(pltpu.HBM)] * len(extra),
            out_specs=out_specs,
            scratch_shapes=[pltpu.SemaphoreType.DMA((4,))] * len(extra),
            compiler_params=params,
            cost_estimate=pl.CostEstimate(
                flops=2 * total * width * held * ranks,
                bytes_accessed=2 * width * (2 * held * ranks + total),
                transcendentals=0,
            ),
            name="down",
        )(own, sibling, *pieces, *tagged, *extra)

    def base(pieces, weight, after, start, ready, length):
        columns = weight.shape[1]
        stream = length - ready.shape[0]
        rest = columns % 256
        side = (2 * total, 256) if rest == 128 else (total, max(rest, 1))
        return pl.pallas_call(
            functools.partial(base_kernel, len(pieces), start, length - stream),
            out_shape=jax.ShapeDtypeStruct((total, columns), f32),
            in_specs=[spec()] * (len(pieces) + 1) + [spec(pltpu.HBM), spec(pl.ANY)],
            out_specs=spec(),
            scratch_shapes=[
                VMEM((stream, columns), bf16),
                pltpu.SemaphoreType.DMA((stream // 512,)),
                VMEM(side, f32),
            ],
            compiler_params=params,
            cost_estimate=pl.CostEstimate(
                flops=2 * total * length * columns,
                bytes_accessed=4 * length * columns,
                transcendentals=0,
            ),
            name="base",
        )(*pieces, ready, hbm(weight), after)

    def lift(down, tagged, up, base_terms, bounds, ranks):
        columns = up.shape[2]
        whole = lambda x: pl.BlockSpec(x.shape, lambda i: (0,) * x.ndim)
        operands = [down, up] + base_terms
        return pl.pallas_call(
            functools.partial(lift_kernel, count, rows, len(tagged), bounds, ranks),
            grid=(1,),
            out_shape=jax.ShapeDtypeStruct((count, rows, columns), bf16),
            in_specs=tag_specs(tagged) + [whole(x) for x in operands],
            out_specs=pl.BlockSpec((count, rows, columns), lambda i: (0, 0, 0)),
            scratch_shapes=[VMEM((total, columns), f32)],
            compiler_params=params,
            name="lift",
        )(*tagged, *operands)

    def project(column, pieces, tagged, own, sibling, ready, low, high, weight, up, bounds):
        half = width // 2
        down, *rest = downs(own, sibling, column, tagged[: len(column)], low, high, weight)
        ready = ready + rest[1:]

        def term(turn, after):
            if turn > 1:
                return None
            return base(pieces, weight, after, turn * half, ready[turn], half)

        down, base_terms = sum_over(down, count, term)
        columns = lift(down, tagged, up, base_terms, bounds, high - low)
        mine = exchange(columns)
        return jnp.swapaxes(mine, 0, 1).reshape(rows, -1), rest

    bounds = (0, width, width + kv_width, width + 2 * kv_width)
    sibling_maps = jnp.swapaxes(swap(adapter_down, count, 1), 1, 2)
    column, tagged = gather_rows(normed, count)
    qkv_mine, rest = project(
        column,
        tagged,
        tagged,
        first_maps,
        sibling_maps,
        [first_rows],
        0,
        3 * rank,
        projection_weight,
        projection_up_adapter,
        bounds,
    )
    columns = output_weight.shape[1]
    ahead = min(2048, width // 2 - 1024)
    attended, *ready = pl.pallas_call(
        attend_kernel,
        out_shape=[jax.ShapeDtypeStruct((rows, width), bf16)] + [VMEM((ahead, columns), bf16)] * 2,
        in_specs=[spec(SMEM)] + [spec()] * 3 + [spec(pltpu.HBM)],
        out_specs=[spec()] * 3,
        scratch_shapes=[pltpu.SemaphoreType.DMA((2, 4))],
        compiler_params=params,
        cost_estimate=pl.CostEstimate(
            flops=4 * rows * width * context,
            bytes_accessed=4 * cache_keys.size,
            transcendentals=rows * width // head_dim * context,
        ),
        name="attend",
    )(lengths, qkv_mine, cache_keys, cache_values, hbm(output_weight))
    column, pieces = gather_rows(attended, count)
    output, _ = project(
        column,
        pieces,
        tagged,
        own_maps,
        rest[0],
        ready,
        3 * rank,
        4 * rank,
        output_weight,
        output_up_adapter,
        (0, width),
    )
    return output


def solution(mesh):
    count = mesh.shape[AXIS]

    def body(*arrays):
        return local(*arrays, count=count)

    return jax.shard_map(
        body,
        mesh=mesh,
        in_specs=(
            P(("groups", "tensor"), None),
            P(),
            P(("groups", "tensor"), None),
            P(),
            P(("groups", "tensor")),
            P(None, "tensor"),
            P(None, "tensor"),
            P("tensor", None, None),
            P(None, None, "tensor"),
            P(None, None, "tensor"),
            P(("groups", "tensor"), None, None, None),
            P(("groups", "tensor"), None, None, None),
        ),
        out_specs=P(("groups", "tensor"), None),
        check_vma=False,
    )
```

```python
import functools

import jax
import jax.numpy as jnp
from jax import lax
from jax.experimental import pallas as pl
from jax.experimental.pallas import tpu as pltpu
from jax.sharding import PartitionSpec as P

eps = 1e-05
AXIS = "tensor"
LANES = 128
VMEM = pltpu.VMEM
SMEM = pltpu.SMEM


def swap(x, count, offset):
    return lax.ppermute(x, AXIS, [(i, i ^ offset) for i in range(count)])


def exchange(x, groups=None):
    return lax.all_to_all(
        x, AXIS, split_axis=0, concat_axis=0, axis_index_groups=groups, tiled=True
    )


def sum_over(x, count, beside):
    step, turn, terms = count, 0, []
    while step > 1:
        radix = 4 if step % 4 == 0 else 2
        step //= radix
        others = [swap(x, count, k * step) for k in range(1, radix)]
        term = beside(turn, x)
        if term is not None:
            *others, term = lax.optimization_barrier((*others, term))
        terms.append(term)
        for other in others:
            x = x + other
        turn += 1
    return x, [t for t in terms if t is not None]


def pack_kernel(*refs):
    in_refs, out_ref = refs[-2::-1], refs[-1]
    rows, width = in_refs[0].shape
    per = 16 // rows
    for first in range(0, len(in_refs), per):
        parts = [r[...].astype(jnp.float32) for r in in_refs[first : first + per]]
        at = slice(first * rows, (first + per) * rows)
        out_ref[at] = jnp.concatenate(parts, axis=0).astype(jnp.bfloat16)


def pack(parts):
    rows, width = parts[0].shape
    return pl.pallas_call(
        pack_kernel,
        out_shape=jax.ShapeDtypeStruct((rows * len(parts), width), jnp.bfloat16),
        in_specs=[spec()] * len(parts),
        out_specs=spec(),
        compiler_params=pltpu.CompilerParams(vmem_limit_bytes=16 * 1024 * 1024),
        name="pack",
    )(*parts[::-1])


def gather_rows(x, count):
    step = count // 4
    near, middle, far = (swap(x, count, k * step) for k in (1, 2, 3))
    step //= 2
    across = [swap(p, count, step) for p in (x, near, middle, far)]
    held = [pack([x, near, middle, far] + across)]
    step //= 2
    while step > 1:
        held = held + [swap(h, count, step) for h in held]
        step //= 2
    return held, held + [swap(h, count, 1) for h in held]


def place_of(row, me, count, rows):
    block = row // rows
    source = (block % 4) * (count // 4)
    piece, step = block // 4, count // 8
    while step:
        source = source + (piece % 2) * step
        piece, step = piece // 2, step // 2
    return (source ^ me) * rows + row % rows


def spec(space=VMEM):
    return pl.BlockSpec(memory_space=space)


def hbm(x):
    return pltpu.with_memory_space_constraint(x, pltpu.HBM)


def iota(shape, dim):
    return lax.broadcasted_iota(jnp.int32, shape, dim)


def one_hot(condition):
    return jnp.where(condition, 1.0, 0.0).astype(jnp.bfloat16)


def norm_kernel(
    hidden_hbm,
    gain_hbm,
    names_hbm,
    slots_hbm,
    maps_hbm,
    weight_hbm,
    out_ref,
    maps_ref,
    weight_ref,
    hidden_ref,
    gain_ref,
    names_ref,
    slots_ref,
    sems,
    row_sems,
):
    ranks = maps_ref.shape[1]
    copies = [
        pltpu.make_async_copy(source, target, sems.at[i])
        for i, (source, target) in enumerate(
            (
                (hidden_hbm, hidden_ref),
                (gain_hbm, gain_ref),
                (names_hbm, names_ref),
                (slots_hbm, slots_ref),
                (maps_hbm.at[:, :ranks], maps_ref),
            )
        )
    ] + rows_copies(weight_hbm, 0, weight_ref, row_sems)
    for copy in copies:
        copy.start()
    for copy in copies[:4]:
        copy.wait()
    rows, width = hidden_ref.shape
    hidden = hidden_ref[...].astype(jnp.float32)
    power = jnp.sum(hidden * hidden, axis=1, keepdims=True) / width
    gain = gain_ref[...].reshape(1, width).astype(jnp.float32)
    out_ref[:, :width] = (hidden * lax.rsqrt(power + eps) * gain).astype(jnp.bfloat16)
    row, lane = iota((rows, LANES), 0), iota((rows, LANES), 1)
    tags = jnp.zeros((rows, LANES), jnp.float32)
    for r in range(rows):
        name = names_ref[r]
        tag = jnp.where(lane < LANES // 2, name, slots_ref[name]).astype(jnp.float32)
        tags = jnp.where(row == r, tag, tags)
    out_ref[:, width:] = tags.astype(jnp.bfloat16)
    for copy in copies[4:]:
        copy.wait()


NT = (((1,), (1,)), ((), ()))


def rows_copies(weight_hbm, start, rows_ref, sems):
    length = rows_ref.shape[0] // sems.shape[0]
    return [
        pltpu.make_async_copy(
            weight_hbm.at[start + i * length : start + (i + 1) * length],
            rows_ref.at[i * length : (i + 1) * length],
            sems.at[i],
        )
        for i in range(sems.shape[0])
    ]


def down_kernel(count, rows, pieces, ranks, *refs):
    map_refs, piece_refs = refs[:2], refs[2 : 2 + pieces]
    tag_refs, refs = refs[2 + pieces : 2 + 2 * pieces], refs[2 + 2 * pieces :]
    if len(refs) > 1:
        weight_hbm, out_ref, rest_ref, rows_ref, sems = refs
        copies = rows_copies(weight_hbm, weight_hbm.shape[0] // 2, rows_ref, sems)
        for copy in copies:
            copy.start()
    else:
        (out_ref,) = refs
    me = lax.axis_index(AXIS)
    held, _, width = map_refs[0].shape
    rank = ranks[1] - ranks[0]
    total, half = count * rows, count * rows // 2
    chunk = 4096
    sums = jnp.zeros((2 * held * rank, half), jnp.float32)
    for k in range(0, width, chunk):
        x = jnp.concatenate([p[:, k : k + chunk] for p in piece_refs], axis=0)
        maps = jnp.concatenate(
            [m[:, :rank, k : k + chunk].reshape(held * rank, chunk) for m in map_refs], axis=0
        )
        sums = sums + lax.dot_general(maps, x, NT, preferred_element_type=jnp.float32)
    if len(refs) > 1:
        rest_ref[...] = map_refs[1][:, rank:]
    tags = jnp.concatenate([t[...] for t in tag_refs], axis=0)
    pick = one_hot(iota((16, LANES), 1) == LANES // 2)
    slots = lax.dot_general(pick, tags, NT, preferred_element_type=jnp.float32)[:1]
    chosen = jnp.zeros((rank, half), jnp.float32)
    for m in range(2):
        for s in range(held):
            slot = ((me ^ m) * held + s).astype(jnp.float32)
            at = (m * held + s) * rank
            chosen = jnp.where(slots == slot, sums[at : at + rank], chosen)
    row, column = iota((half, total), 0), iota((half, total), 1)
    back = one_hot(place_of(row, me, count, rows) == column)
    placed = jnp.dot(chosen.astype(jnp.bfloat16), back, preferred_element_type=jnp.float32)
    folds = out_ref.shape[1] // total
    part = rank // folds
    folded = [placed[f * part : (f + 1) * part] for f in range(folds)]
    value = jnp.concatenate(folded, axis=1).astype(jnp.bfloat16)
    out_ref[...] = value
    if len(refs) > 1:
        for copy in copies:
            copy.wait()


def base_kernel(pieces, start, ready, *refs):
    ready_ref = refs[pieces] if ready else None
    weight_hbm, _, out_ref, weight_ref, sems, side_ref = refs[-6:]
    total, columns = out_ref.shape
    whole = columns // 256 * 256
    narrow = columns - whole == 128
    stream = weight_ref.shape[0]
    copies = rows_copies(weight_hbm, start + ready, weight_ref, sems)
    for copy in copies:
        copy.start()
    each = stream // len(copies)

    def rows_of(at, length):
        return jnp.concatenate([p[:, at : at + length] for p in refs[:pieces]], axis=0)

    def dot(x, weight):
        return jnp.dot(x, weight, preferred_element_type=jnp.float32)

    def wide(from_ref, k, length, offset):
        if whole:
            x = rows_of(start + offset, length)
            term = dot(x, from_ref[k : k + length, :whole])
            out_ref[:, :whole] = term if offset == 0 else out_ref[:, :whole] + term

    def rest(weight, offset):
        length = weight.shape[0]
        if narrow:
            half = length // 2
            left = [rows_of(start + offset + h, half) for h in (0, half)]
            right = [weight[:half], weight[half:]]
            term = dot(jnp.concatenate(left, axis=0), jnp.concatenate(right, axis=1))
        else:
            term = dot(rows_of(start + offset, length), weight)
        side_ref[...] = term if offset == 0 else side_ref[...] + term

    if ready:
        wide(ready_ref, 0, ready, 0)
    early = stream - 1024
    for i, copy in enumerate(copies):
        copy.wait()
        at = (i + 1) * each
        if at % 1024 == 0 and at <= early:
            wide(weight_ref, at - 1024, 1024, ready + at - 1024)
        if at == early and columns > whole:
            weight = weight_ref[:early, whole:]
            if ready:
                weight = jnp.concatenate([ready_ref[:, whole:], weight], axis=0)
            rest(weight, 0)
    wide(weight_ref, early, 1024, ready + early)
    if columns > whole:
        rest(weight_ref[early:, whole:], ready + early)
        if narrow:
            out_ref[:, whole:] = side_ref[:total, :128] + side_ref[total:, 128:]
        else:
            out_ref[:, whole:] = side_ref[...]


def lift_kernel(count, rows, pieces, bounds, rank, *refs):
    tag_refs, refs = refs[:pieces], refs[pieces:]
    (down_ref, up_ref), base_refs, (out_ref, sum_ref) = refs[:2], refs[2:-2], refs[-2:]
    total = count * rows
    me = lax.axis_index(AXIS)
    adapters, per, columns = up_ref.shape
    wide = adapters * per
    row, column = iota((total, total), 0), iota((total, total), 1)
    order = one_hot(place_of(column, me, count, rows) == row)
    back = one_hot(place_of(row, me, count, rows) == column)
    folded = down_ref[...].astype(jnp.float32)
    folds = folded.shape[1] // total
    down = jnp.concatenate([folded[:, f * total : (f + 1) * total] for f in range(folds)], axis=0)
    down = lax.dot_general(
        back, down.astype(jnp.bfloat16), NT, preferred_element_type=jnp.float32
    ).astype(jnp.bfloat16)
    names = jnp.concatenate([t[...] for t in tag_refs], axis=0).astype(jnp.float32)[:, :1]
    named = (iota((total, wide), 1) // per).astype(jnp.float32) == names
    start = me * columns
    value = base_refs[0][...]
    for b in base_refs[1:]:
        value = value + b[...]
    sum_ref[...] = value
    for g in range(rank // per):
        low, high = bounds[g], bounds[g + 1]

        @pl.when((start < high) & (start + columns > low))
        def _():
            at = iota((rank, wide), 1) % per + g * per
            spread = one_hot(at == iota((rank, wide), 0))
            copies = jnp.dot(down, spread, preferred_element_type=jnp.float32)
            chosen = jnp.where(named, copies, 0.0).astype(jnp.bfloat16)
            up = up_ref[...].reshape(wide, columns)
            lifted = jnp.dot(chosen, up, preferred_element_type=jnp.float32)
            at = iota((total, columns), 1) + start
            sum_ref[...] += jnp.where((at >= low) & (at < high), lifted, 0.0)

    placed = jnp.dot(
        order, sum_ref[...].astype(jnp.bfloat16), preferred_element_type=jnp.float32
    ).astype(jnp.bfloat16)
    for d in range(count):
        out_ref[d] = placed[d * rows : (d + 1) * rows]


def attend_kernel(lengths_ref, qkv_ref, keys_ref, values_ref, out_ref):
    rows, kv_heads, context, dim = keys_ref.shape
    width = out_ref.shape[1]
    groups = width // dim // kv_heads
    per_head = groups * rows
    together = max(2, LANES // per_head)
    lanes = together * per_head
    lane = iota((1, lanes), 1)
    length = jnp.zeros((1, lanes), jnp.int32)
    for b in range(rows):
        length = jnp.where(lane % rows == b, lengths_ref[b], length)
    live = iota((context, lanes), 0) < length
    odd = iota((lanes, 1), 0) // per_head % 2 == 1
    pair_row = iota((2 * per_head, 1), 0)
    scale = dim ** (-0.5)

    def columns(at):
        return qkv_ref[:, at : at + dim].astype(jnp.float32)

    for first in range(0, kv_heads, together):
        heads = range(first, first + together)
        query = jnp.concatenate(
            [columns((h * groups + g) * dim) for h in heads for g in range(groups)], axis=0
        )
        key = jnp.concatenate([columns(width + h * dim) for h in heads for _ in range(groups)], axis=0)
        at = width + kv_heads * dim
        value = jnp.concatenate([columns(at + h * dim) for h in heads for _ in range(groups)], axis=0)
        half = jnp.concatenate([jnp.where(odd, 0.0, query), jnp.where(odd, query, 0.0)], axis=1)
        half = half.astype(jnp.bfloat16)
        scores = jnp.zeros((context, lanes), jnp.float32)
        for n in range(0, together, 2):
            cached = [keys_ref[:, first + n + m].reshape(rows * context, dim) for m in range(2)]
            every = lax.dot_general(
                jnp.concatenate(cached, axis=1), half, NT, preferred_element_type=jnp.float32
            )
            for b in range(rows):
                mine = (lane // (2 * per_head) == n // 2) & (lane % rows == b)
                scores = jnp.where(mine, every[b * context : (b + 1) * context], scores)
        scores = jnp.where(live, scores * scale, -1e30)
        own = jnp.sum((query * key).T, axis=0, keepdims=True) * scale
        peak = jnp.maximum(jnp.max(scores, axis=0, keepdims=True), own)
        weights = jnp.exp(scores - peak)
        own_weight = jnp.exp(own - peak)
        denominator = jnp.sum(weights, axis=0, keepdims=True) + own_weight
        probs = (weights / denominator).T.astype(jnp.bfloat16)
        own_prob = (own_weight / denominator).astype(jnp.bfloat16).astype(jnp.float32)
        own_term = jnp.broadcast_to(own_prob, (dim, lanes)).T * value
        for n in range(0, together, 2):
            span = slice(n * per_head, (n + 2) * per_head)
            mixed = jnp.zeros((2 * per_head, dim), jnp.float32)
            for b in range(rows):
                both = jnp.concatenate([values_ref[b, first + n + m] for m in range(2)], axis=1)
                one = jnp.dot(probs[span], both, preferred_element_type=jnp.float32)
                one = jnp.where(pair_row < per_head, one[:, :dim], one[:, dim:])
                mixed = jnp.where(pair_row % rows == b, one, mixed)
            mixed = (mixed + own_term[span]).astype(jnp.bfloat16)
            for g in range(2 * groups):
                at = ((first + n) * groups + g) * dim
                out_ref[:, at : at + dim] = mixed[g * rows : (g + 1) * rows]


def local(
    input_hidden,
    input_norm_gain,
    request_adapter,
    adapter_storage,
    lengths,
    projection_weight,
    output_weight,
    adapter_down,
    projection_up_adapter,
    output_up_adapter,
    cache_keys,
    cache_values,
    *,
    count,
):
    rows, width = input_hidden.shape
    rank = projection_up_adapter.shape[1]
    held = adapter_down.shape[0]
    kv_heads, context, head_dim = cache_keys.shape[1:]
    kv_width = kv_heads * head_dim
    total = rows * count
    bf16, f32 = jnp.bfloat16, jnp.float32
    params = pltpu.CompilerParams(vmem_limit_bytes=(16 if total <= 64 else 60) * 1024 * 1024)
    own_maps = jnp.swapaxes(adapter_down, 1, 2)

    normed, first_maps, first_rows = pl.pallas_call(
        norm_kernel,
        out_shape=[
            VMEM((rows, width + LANES), bf16),
            VMEM((held, 3 * rank, width), bf16),
            VMEM((1024, projection_weight.shape[1]), bf16),
        ],
        in_specs=[spec(pltpu.HBM)] * 6,
        out_specs=[spec()] * 3,
        scratch_shapes=[
            VMEM((rows, width), bf16),
            VMEM((width,), bf16),
            SMEM((rows,), jnp.int32),
            SMEM(adapter_storage.shape, jnp.int32),
            pltpu.SemaphoreType.DMA((5,)),
            pltpu.SemaphoreType.DMA((1,)),
        ],
        compiler_params=params,
        name="norm",
    )(
        hbm(input_hidden),
        hbm(input_norm_gain),
        hbm(request_adapter.reshape(rows)),
        hbm(adapter_storage),
        hbm(own_maps),
        hbm(projection_weight),
    )

    def tag_specs(pieces):
        return [pl.BlockSpec((p.shape[0], LANES), lambda i: (0, width // LANES)) for p in pieces]

    def downs(own, sibling, pieces, tagged, low, high, weight):
        ranks = high - low
        lanes = max(LANES, total)
        whole = lambda x: pl.BlockSpec(x.shape, lambda i: (0,) * len(x.shape))
        own_spec = pl.BlockSpec((held, ranks, width), lambda i: (0, low // ranks, 0))
        outs = [jax.ShapeDtypeStruct((ranks * total // lanes, lanes), bf16)]
        extra = []
        if low == 0:
            rest = sibling.shape[1] - ranks
            outs.append(jax.ShapeDtypeStruct((held, rest, width), bf16))
            extra = [hbm(weight)]
        out_specs = [whole(x) for x in outs]
        if extra:
            outs.append(VMEM((1024, weight.shape[1]), bf16))
            out_specs.append(spec(pl.ANY))
        return pl.pallas_call(
            functools.partial(down_kernel, count, rows, len(pieces), (low, high)),
            grid=(1,),
            out_shape=outs,
            in_specs=[own_spec, whole(sibling)]
            + [pl.BlockSpec((p.shape[0], width), lambda i: (0, 0)) for p in pieces]
            + tag_specs(tagged)
            + [spec(pltpu.HBM)] * len(extra),
            out_specs=out_specs,
            scratch_shapes=[pltpu.SemaphoreType.DMA((1,))] * len(extra),
            compiler_params=params,
            cost_estimate=pl.CostEstimate(
                flops=2 * total * width * held * ranks,
                bytes_accessed=2 * width * (2 * held * ranks + total),
                transcendentals=0,
            ),
            name="down",
        )(own, sibling, *pieces, *tagged, *extra)

    def base(pieces, weight, after, start, ready, length):
        columns = weight.shape[1]
        first = [] if ready is None else [ready]
        stream = length - sum(r.shape[0] for r in first)
        rest = columns % 256
        side = (2 * total, 256) if rest == 128 else (total, max(rest, 1))
        return pl.pallas_call(
            functools.partial(base_kernel, len(pieces), start, length - stream),
            out_shape=jax.ShapeDtypeStruct((total, columns), f32),
            in_specs=[spec()] * (len(pieces) + len(first)) + [spec(pltpu.HBM), spec(pl.ANY)],
            out_specs=spec(),
            scratch_shapes=[
                VMEM((stream, columns), bf16),
                pltpu.SemaphoreType.DMA((stream // 1024,)),
                VMEM(side, f32),
            ],
            compiler_params=params,
            cost_estimate=pl.CostEstimate(
                flops=2 * total * length * columns,
                bytes_accessed=4 * length * columns,
                transcendentals=0,
            ),
            name="base",
        )(*pieces, *first, hbm(weight), after)

    def lift(down, tagged, up, base_terms, bounds, ranks):
        columns = up.shape[2]
        whole = lambda x: pl.BlockSpec(x.shape, lambda i: (0,) * x.ndim)
        operands = [down, up] + base_terms
        return pl.pallas_call(
            functools.partial(lift_kernel, count, rows, len(tagged), bounds, ranks),
            grid=(1,),
            out_shape=jax.ShapeDtypeStruct((count, rows, columns), bf16),
            in_specs=tag_specs(tagged) + [whole(x) for x in operands],
            out_specs=pl.BlockSpec((count, rows, columns), lambda i: (0, 0, 0)),
            scratch_shapes=[VMEM((total, columns), f32)],
            compiler_params=params,
            name="lift",
        )(*tagged, *operands)

    def project(column, pieces, tagged, own, sibling, ready, low, high, weight, up, bounds):
        half = width // 2
        down, *rest = downs(own, sibling, column, tagged[: len(column)], low, high, weight)
        ready = ready + rest[1:]

        def term(turn, after):
            if turn > 1:
                return None
            return base(pieces, weight, after, turn * half, ready[turn], half)

        down, base_terms = sum_over(down, count, term)
        columns = lift(down, tagged, up, base_terms, bounds, high - low)
        mine = exchange(columns)
        return jnp.swapaxes(mine, 0, 1).reshape(rows, -1), rest

    bounds = (0, width, width + kv_width, width + 2 * kv_width)
    sibling_maps = jnp.swapaxes(swap(adapter_down, count, 1), 1, 2)
    column, tagged = gather_rows(normed, count)
    qkv_mine, rest = project(
        column,
        tagged,
        tagged,
        first_maps,
        sibling_maps,
        [first_rows],
        0,
        3 * rank,
        projection_weight,
        projection_up_adapter,
        bounds,
    )
    attended = pl.pallas_call(
        attend_kernel,
        out_shape=jax.ShapeDtypeStruct((rows, width), bf16),
        in_specs=[spec(SMEM)] + [spec()] * 3,
        out_specs=spec(),
        compiler_params=params,
        cost_estimate=pl.CostEstimate(
            flops=4 * rows * width * context,
            bytes_accessed=4 * cache_keys.size,
            transcendentals=rows * width // head_dim * context,
        ),
        name="attend",
    )(lengths, qkv_mine, cache_keys, cache_values)
    column, pieces = gather_rows(attended, count)
    output, _ = project(
        column,
        pieces,
        tagged,
        own_maps,
        rest[0],
        [None, None],
        3 * rank,
        4 * rank,
        output_weight,
        output_up_adapter,
        (0, width),
    )
    return output


def solution(mesh):
    count = mesh.shape[AXIS]

    def body(*arrays):
        return local(*arrays, count=count)

    return jax.shard_map(
        body,
        mesh=mesh,
        in_specs=(
            P(("groups", "tensor"), None),
            P(),
            P(("groups", "tensor"), None),
            P(),
            P(("groups", "tensor")),
            P(None, "tensor"),
            P(None, "tensor"),
            P("tensor", None, None),
            P(None, None, "tensor"),
            P(None, None, "tensor"),
            P(("groups", "tensor"), None, None, None),
            P(("groups", "tensor"), None, None, None),
        ),
        out_specs=P(("groups", "tensor"), None),
        check_vma=False,
    )
```

```python
import functools

import jax
import jax.numpy as jnp
from jax import lax
from jax.experimental import pallas as pl
from jax.experimental.pallas import tpu as pltpu
from jax.sharding import PartitionSpec as P

eps = 1e-05
AXIS = "tensor"
LANES = 128
VMEM = pltpu.VMEM
SMEM = pltpu.SMEM


def swap(x, count, offset):
    return lax.ppermute(x, AXIS, [(i, i ^ offset) for i in range(count)])


def exchange(x, groups=None):
    return lax.all_to_all(
        x, AXIS, split_axis=0, concat_axis=0, axis_index_groups=groups, tiled=True
    )


def sum_over(x, count, beside):
    step, turn, terms = count, 0, []
    while step > 1:
        radix = 4 if turn > 1 and step % 4 == 0 else 2
        step //= radix
        others = [swap(x, count, k * step) for k in range(1, radix)]
        term = beside(turn, x)
        if term is not None:
            *others, term = lax.optimization_barrier((*others, term))
            terms.append(term)
        for other in others:
            x = x + other
        turn += 1
    return x, terms


def pack_kernel(*refs):
    in_refs, out_ref = refs[-2::-1], refs[-1]
    rows, width = in_refs[0].shape
    per = 16 // rows
    for first in range(0, len(in_refs), per):
        parts = [r[...].astype(jnp.float32) for r in in_refs[first : first + per]]
        at = slice(first * rows, (first + per) * rows)
        out_ref[at] = jnp.concatenate(parts, axis=0).astype(jnp.bfloat16)


def pack(parts):
    rows, width = parts[0].shape
    return pl.pallas_call(
        pack_kernel,
        out_shape=jax.ShapeDtypeStruct((rows * len(parts), width), jnp.bfloat16),
        in_specs=[spec()] * len(parts),
        out_specs=spec(),
        compiler_params=pltpu.CompilerParams(vmem_limit_bytes=16 * 1024 * 1024),
        name="pack",
    )(*parts[::-1])


def gather_rows(x, count):
    step = count // 4
    near, middle, far = (swap(x, count, k * step) for k in (1, 2, 3))
    step //= 2
    across = [swap(p, count, step) for p in (x, near, middle, far)]
    held = [pack([x, near, middle, far] + across)]
    step //= 2
    while step > 1:
        held = held + [swap(h, count, step) for h in held]
        step //= 2
    return held, held + [swap(h, count, 1) for h in held]


def place_of(row, me, count, rows):
    block = row // rows
    source = (block % 4) * (count // 4)
    piece, step = block // 4, count // 8
    while step:
        source = source + (piece % 2) * step
        piece, step = piece // 2, step // 2
    return (source ^ me) * rows + row % rows


def spec(space=VMEM):
    return pl.BlockSpec(memory_space=space)


def hbm(x):
    return pltpu.with_memory_space_constraint(x, pltpu.HBM)


def iota(shape, dim):
    return lax.broadcasted_iota(jnp.int32, shape, dim)


def one_hot(condition):
    return jnp.where(condition, 1.0, 0.0).astype(jnp.bfloat16)


def norm_kernel(
    hidden_hbm,
    gain_hbm,
    names_hbm,
    slots_hbm,
    maps_hbm,
    weight_hbm,
    out_ref,
    maps_ref,
    weight_ref,
    hidden_ref,
    gain_ref,
    names_ref,
    slots_ref,
    sems,
    row_sems,
):
    ranks = maps_ref.shape[1]
    copies = [
        pltpu.make_async_copy(source, target, sems.at[i])
        for i, (source, target) in enumerate(
            (
                (hidden_hbm, hidden_ref),
                (gain_hbm, gain_ref),
                (names_hbm, names_ref),
                (slots_hbm, slots_ref),
                (maps_hbm.at[:, :ranks], maps_ref),
            )
        )
    ] + rows_copies(weight_hbm, 0, weight_ref, row_sems)
    for copy in copies:
        copy.start()
    for copy in copies[:4]:
        copy.wait()
    rows, width = hidden_ref.shape
    hidden = hidden_ref[...].astype(jnp.float32)
    power = jnp.sum(hidden * hidden, axis=1, keepdims=True) / width
    gain = gain_ref[...].reshape(1, width).astype(jnp.float32)
    out_ref[:, :width] = (hidden * lax.rsqrt(power + eps) * gain).astype(jnp.bfloat16)
    row, lane = iota((rows, LANES), 0), iota((rows, LANES), 1)
    tags = jnp.zeros((rows, LANES), jnp.float32)
    for r in range(rows):
        name = names_ref[r]
        tag = jnp.where(lane < LANES // 2, name, slots_ref[name]).astype(jnp.float32)
        tags = jnp.where(row == r, tag, tags)
    out_ref[:, width:] = tags.astype(jnp.bfloat16)
    for copy in copies[4:]:
        copy.wait()


NT = (((1,), (1,)), ((), ()))


def rows_copies(weight_hbm, start, rows_ref, sems):
    length = rows_ref.shape[0] // sems.shape[0]
    return [
        pltpu.make_async_copy(
            weight_hbm.at[start + i * length : start + (i + 1) * length],
            rows_ref.at[i * length : (i + 1) * length],
            sems.at[i],
        )
        for i in range(sems.shape[0])
    ]


def down_kernel(count, rows, pieces, ranks, start, *refs):
    map_refs, piece_refs = refs[:2], refs[2 : 2 + pieces]
    tag_refs, refs = refs[2 + pieces : 2 + 2 * pieces], refs[2 + 2 * pieces :]
    if len(refs) > 1:
        weight_hbm, out_ref, rest_ref, rows_ref, sems = refs
        copies = rows_copies(weight_hbm, start, rows_ref, sems)
        for copy in copies:
            copy.start()
    else:
        (out_ref,) = refs
    me = lax.axis_index(AXIS)
    held, _, width = map_refs[0].shape
    rank = ranks[1] - ranks[0]
    total, half = count * rows, count * rows // 2
    chunk = 4096
    sums = jnp.zeros((2 * held * rank, half), jnp.float32)
    for k in range(0, width, chunk):
        x = jnp.concatenate([p[:, k : k + chunk] for p in piece_refs], axis=0)
        maps = jnp.concatenate(
            [m[:, :rank, k : k + chunk].reshape(held * rank, chunk) for m in map_refs], axis=0
        )
        sums = sums + lax.dot_general(maps, x, NT, preferred_element_type=jnp.float32)
    if len(refs) > 1:
        rest_ref[...] = map_refs[1][:, rank:]
    tags = jnp.concatenate([t[...] for t in tag_refs], axis=0)
    pick = one_hot(iota((16, LANES), 1) == LANES // 2)
    slots = lax.dot_general(pick, tags, NT, preferred_element_type=jnp.float32)[:1]
    chosen = jnp.zeros((rank, half), jnp.float32)
    for m in range(2):
        for s in range(held):
            slot = ((me ^ m) * held + s).astype(jnp.float32)
            at = (m * held + s) * rank
            chosen = jnp.where(slots == slot, sums[at : at + rank], chosen)
    row, column = iota((half, total), 0), iota((half, total), 1)
    back = one_hot(place_of(row, me, count, rows) == column)
    placed = jnp.dot(chosen.astype(jnp.bfloat16), back, preferred_element_type=jnp.float32)
    folds = out_ref.shape[1] // total
    part = rank // folds
    folded = [placed[f * part : (f + 1) * part] for f in range(folds)]
    value = jnp.concatenate(folded, axis=1).astype(jnp.bfloat16)
    out_ref[...] = value
    if len(refs) > 1:
        for copy in copies:
            copy.wait()


def spans_of(length):
    spans, at = [], 0
    while at < length:
        left = length - at
        size = 1024 if left > 1024 else min(left, 512)
        spans.append((at, size))
        at += size
    return spans


def base_kernel(pieces, start, ready, *refs):
    ready_ref = refs[pieces] if ready else None
    weight_hbm, _, out_ref, weight_ref, sems, side_ref = refs[-6:]
    total, columns = out_ref.shape
    whole = columns // 256 * 256
    narrow = columns - whole == 128
    spans = spans_of(weight_ref.shape[0])
    copies = [
        pltpu.make_async_copy(
            weight_hbm.at[start + ready + k : start + ready + k + length],
            weight_ref.at[k : k + length],
            sems.at[i],
        )
        for i, (k, length) in enumerate(spans)
    ]
    for copy in copies:
        copy.start()

    def rows_of(at, length):
        return jnp.concatenate([p[:, at : at + length] for p in refs[:pieces]], axis=0)

    def dot(x, weight):
        return jnp.dot(x, weight, preferred_element_type=jnp.float32)

    def wide(from_ref, k, length, offset):
        if whole:
            x = rows_of(start + offset, length)
            term = dot(x, from_ref[k : k + length, :whole])
            out_ref[:, :whole] = term if offset == 0 else out_ref[:, :whole] + term

    def rest(weight, offset):
        length = weight.shape[0]
        if narrow:
            half = length // 2
            left = [rows_of(start + offset + h, half) for h in (0, half)]
            right = [weight[:half], weight[half:]]
            term = dot(jnp.concatenate(left, axis=0), jnp.concatenate(right, axis=1))
        else:
            term = dot(rows_of(start + offset, length), weight)
        side_ref[...] = term if offset == 0 else side_ref[...] + term

    if ready:
        wide(ready_ref, 0, ready, 0)
    for (k, length), copy in zip(spans, copies):
        if (k, length) == spans[-1] and columns > whole:
            weight = weight_ref[:k, whole:]
            if ready:
                weight = jnp.concatenate([ready_ref[:, whole:], weight], axis=0)
            rest(weight, 0)
        copy.wait()
        wide(weight_ref, k, length, ready + k)
    if columns > whole:
        rest(weight_ref[k:, whole:], ready + k)
        side = side_ref[...]
        out_ref[:, whole:] = side[:total, :128] + side[total:, 128:] if narrow else side


def lift_kernel(count, rows, pieces, bounds, rank, *refs):
    tag_refs, refs = refs[:pieces], refs[pieces:]
    (down_ref, up_ref), base_refs, (out_ref, sum_ref) = refs[:2], refs[2:-2], refs[-2:]
    total = count * rows
    me = lax.axis_index(AXIS)
    adapters, per, columns = up_ref.shape
    wide = adapters * per
    row, column = iota((total, total), 0), iota((total, total), 1)
    order = one_hot(place_of(column, me, count, rows) == row)
    back = one_hot(place_of(row, me, count, rows) == column)
    folded = down_ref[...].astype(jnp.float32)
    folds = folded.shape[1] // total
    down = jnp.concatenate([folded[:, f * total : (f + 1) * total] for f in range(folds)], axis=0)
    down = lax.dot_general(
        back, down.astype(jnp.bfloat16), NT, preferred_element_type=jnp.float32
    ).astype(jnp.bfloat16)
    names = jnp.concatenate([t[...] for t in tag_refs], axis=0).astype(jnp.float32)[:, :1]
    named = (iota((total, wide), 1) // per).astype(jnp.float32) == names
    start = me * columns
    value = base_refs[0][...]
    for b in base_refs[1:]:
        value = value + b[...]
    sum_ref[...] = value
    for g in range(rank // per):
        low, high = bounds[g], bounds[g + 1]

        @pl.when((start < high) & (start + columns > low))
        def _():
            at = iota((rank, wide), 1) % per + g * per
            spread = one_hot(at == iota((rank, wide), 0))
            copies = jnp.dot(down, spread, preferred_element_type=jnp.float32)
            chosen = jnp.where(named, copies, 0.0).astype(jnp.bfloat16)
            up = up_ref[...].reshape(wide, columns)
            lifted = jnp.dot(chosen, up, preferred_element_type=jnp.float32)
            at = iota((total, columns), 1) + start
            sum_ref[...] += jnp.where((at >= low) & (at < high), lifted, 0.0)

    placed = jnp.dot(
        order, sum_ref[...].astype(jnp.bfloat16), preferred_element_type=jnp.float32
    ).astype(jnp.bfloat16)
    for d in range(count):
        out_ref[d] = placed[d * rows : (d + 1) * rows]


def attend_kernel(lengths_ref, qkv_ref, keys_ref, values_ref, out_ref):
    rows, kv_heads, context, dim = keys_ref.shape
    width = out_ref.shape[1]
    groups = width // dim // kv_heads
    per_head = groups * rows
    together = max(2, LANES // per_head)
    lanes = together * per_head
    lane = iota((1, lanes), 1)
    length = jnp.zeros((1, lanes), jnp.int32)
    for b in range(rows):
        length = jnp.where(lane % rows == b, lengths_ref[b], length)
    live = iota((context, lanes), 0) < length
    odd = iota((lanes, 1), 0) // per_head % 2 == 1
    pair_row = iota((2 * per_head, 1), 0)
    scale = dim ** (-0.5)

    def columns(at):
        return qkv_ref[:, at : at + dim].astype(jnp.float32)

    steps = []
    for first in range(0, kv_heads, together):
        heads = range(first, first + together)
        query = jnp.concatenate(
            [columns((h * groups + g) * dim) for h in heads for g in range(groups)], axis=0
        )
        half = jnp.concatenate([jnp.where(odd, 0.0, query), jnp.where(odd, query, 0.0)], axis=1)
        half = half.astype(jnp.bfloat16)
        scores = jnp.zeros((context, lanes), jnp.float32)
        for n in range(0, together, 2):
            cached = [keys_ref[:, first + n + m].reshape(rows * context, dim) for m in range(2)]
            every = lax.dot_general(
                jnp.concatenate(cached, axis=1), half, NT, preferred_element_type=jnp.float32
            )
            for b in range(rows):
                mine = (lane // (2 * per_head) == n // 2) & (lane % rows == b)
                scores = jnp.where(mine, every[b * context : (b + 1) * context], scores)
        steps.append((first, heads, query, scores))

    for i, (first, heads, query, scores) in enumerate(steps):
        key = jnp.concatenate([columns(width + h * dim) for h in heads for _ in range(groups)], axis=0)
        at = width + kv_heads * dim
        value = jnp.concatenate([columns(at + h * dim) for h in heads for _ in range(groups)], axis=0)
        scores = jnp.where(live, scores * scale, -1e30)
        own = jnp.sum((query * key).T, axis=0, keepdims=True) * scale
        peak = jnp.maximum(jnp.max(scores, axis=0, keepdims=True), own)
        weights = jnp.exp(scores - peak)
        own_weight = jnp.exp(own - peak)
        denominator = jnp.sum(weights, axis=0, keepdims=True) + own_weight
        probs = (weights / denominator).T.astype(jnp.bfloat16)
        own_prob = (own_weight / denominator).astype(jnp.bfloat16).astype(jnp.float32)
        steps[i] = (first, probs, jnp.broadcast_to(own_prob, (dim, lanes)).T * value)

    for first, probs, own_term in steps:
        for n in range(0, together, 2):
            span = slice(n * per_head, (n + 2) * per_head)
            mixed = jnp.zeros((2 * per_head, dim), jnp.float32)
            for b in range(rows):
                both = jnp.concatenate([values_ref[b, first + n + m] for m in range(2)], axis=1)
                one = jnp.dot(probs[span], both, preferred_element_type=jnp.float32)
                one = jnp.where(pair_row < per_head, one[:, :dim], one[:, dim:])
                mixed = jnp.where(pair_row % rows == b, one, mixed)
            mixed = (mixed + own_term[span]).astype(jnp.bfloat16)
            for g in range(2 * groups):
                at = ((first + n) * groups + g) * dim
                out_ref[:, at : at + dim] = mixed[g * rows : (g + 1) * rows]


def local(
    input_hidden,
    input_norm_gain,
    request_adapter,
    adapter_storage,
    lengths,
    projection_weight,
    output_weight,
    adapter_down,
    projection_up_adapter,
    output_up_adapter,
    cache_keys,
    cache_values,
    *,
    count,
):
    rows, width = input_hidden.shape
    rank = projection_up_adapter.shape[1]
    held = adapter_down.shape[0]
    kv_heads, context, head_dim = cache_keys.shape[1:]
    kv_width = kv_heads * head_dim
    total = rows * count
    bf16, f32 = jnp.bfloat16, jnp.float32
    params = pltpu.CompilerParams(vmem_limit_bytes=(16 if total <= 64 else 60) * 1024 * 1024)
    own_maps = jnp.swapaxes(adapter_down, 1, 2)

    normed, first_maps, first_rows = pl.pallas_call(
        norm_kernel,
        out_shape=[
            VMEM((rows, width + LANES), bf16),
            VMEM((held, 3 * rank, width), bf16),
            VMEM((1024, projection_weight.shape[1]), bf16),
        ],
        in_specs=[spec(pltpu.HBM)] * 6,
        out_specs=[spec()] * 3,
        scratch_shapes=[
            VMEM((rows, width), bf16),
            VMEM((width,), bf16),
            SMEM((rows,), jnp.int32),
            SMEM(adapter_storage.shape, jnp.int32),
            pltpu.SemaphoreType.DMA((5,)),
            pltpu.SemaphoreType.DMA((1,)),
        ],
        compiler_params=params,
        name="norm",
    )(
        hbm(input_hidden),
        hbm(input_norm_gain),
        hbm(request_adapter.reshape(rows)),
        hbm(adapter_storage),
        hbm(own_maps),
        hbm(projection_weight),
    )

    def tag_specs(pieces):
        return [pl.BlockSpec((p.shape[0], LANES), lambda i: (0, width // LANES)) for p in pieces]

    def downs(own, sibling, pieces, tagged, low, high, weight, start):
        ranks = high - low
        lanes = max(LANES, total)
        whole = lambda x: pl.BlockSpec(x.shape, lambda i: (0,) * len(x.shape))
        own_spec = pl.BlockSpec((held, ranks, width), lambda i: (0, low // ranks, 0))
        outs = [jax.ShapeDtypeStruct((ranks * total // lanes, lanes), bf16)]
        extra = []
        if low == 0:
            rest = sibling.shape[1] - ranks
            outs.append(jax.ShapeDtypeStruct((held, rest, width), bf16))
            extra = [hbm(weight)]
        out_specs = [whole(x) for x in outs]
        if extra:
            outs.append(VMEM((1024, weight.shape[1]), bf16))
            out_specs.append(spec(pl.ANY))
        return pl.pallas_call(
            functools.partial(down_kernel, count, rows, len(pieces), (low, high), start),
            grid=(1,),
            out_shape=outs,
            in_specs=[own_spec, whole(sibling)]
            + [pl.BlockSpec((p.shape[0], width), lambda i: (0, 0)) for p in pieces]
            + tag_specs(tagged)
            + [spec(pltpu.HBM)] * len(extra),
            out_specs=out_specs,
            scratch_shapes=[pltpu.SemaphoreType.DMA((1,))] * len(extra),
            compiler_params=params,
            cost_estimate=pl.CostEstimate(
                flops=2 * total * width * held * ranks,
                bytes_accessed=2 * width * (2 * held * ranks + total),
                transcendentals=0,
            ),
            name="down",
        )(own, sibling, *pieces, *tagged, *extra)

    def base(pieces, weight, after, start, ready, length):
        columns = weight.shape[1]
        first = [] if ready is None else [ready]
        stream = length - sum(r.shape[0] for r in first)
        rest = columns % 256
        side = (2 * total, 256) if rest == 128 else (total, max(rest, 1))
        return pl.pallas_call(
            functools.partial(base_kernel, len(pieces), start, length - stream),
            out_shape=jax.ShapeDtypeStruct((total, columns), f32),
            in_specs=[spec()] * (len(pieces) + len(first)) + [spec(pltpu.HBM), spec(pl.ANY)],
            out_specs=spec(),
            scratch_shapes=[
                VMEM((stream, columns), bf16),
                pltpu.SemaphoreType.DMA((len(spans_of(stream)),)),
                VMEM(side, f32),
            ],
            compiler_params=params,
            cost_estimate=pl.CostEstimate(
                flops=2 * total * length * columns,
                bytes_accessed=4 * length * columns,
                transcendentals=0,
            ),
            name="base",
        )(*pieces, *first, hbm(weight), after)

    def lift(down, tagged, up, base_terms, bounds, ranks):
        columns = up.shape[2]
        whole = lambda x: pl.BlockSpec(x.shape, lambda i: (0,) * x.ndim)
        operands = [down, up] + base_terms
        return pl.pallas_call(
            functools.partial(lift_kernel, count, rows, len(tagged), bounds, ranks),
            grid=(1,),
            out_shape=jax.ShapeDtypeStruct((count, rows, columns), bf16),
            in_specs=tag_specs(tagged) + [whole(x) for x in operands],
            out_specs=pl.BlockSpec((count, rows, columns), lambda i: (0, 0, 0)),
            scratch_shapes=[VMEM((total, columns), f32)],
            compiler_params=params,
            name="lift",
        )(*tagged, *operands)

    def project(column, pieces, tagged, own, sibling, first_rows, low, high, weight, up, bounds):
        eighth = width // 8
        cuts = (0, 3 * eighth, 11 * eighth // 2 if first_rows is not None else 6 * eighth, width)
        down, *rest = downs(
            own, sibling, column, tagged[: len(column)], low, high, weight, cuts[2]
        )
        ready = [first_rows, None, rest[1] if rest[1:] else None]

        def term(turn, after):
            if turn > 2:
                return None
            return base(pieces, weight, after, cuts[turn], ready[turn], cuts[turn + 1] - cuts[turn])

        down, base_terms = sum_over(down, count, term)
        columns = lift(down, tagged, up, base_terms, bounds, high - low)
        mine = exchange(columns)
        return jnp.swapaxes(mine, 0, 1).reshape(rows, -1), rest

    bounds = (0, width, width + kv_width, width + 2 * kv_width)
    sibling_maps = jnp.swapaxes(swap(adapter_down, count, 1), 1, 2)
    column, tagged = gather_rows(normed, count)
    qkv_mine, rest = project(
        column,
        tagged,
        tagged,
        first_maps,
        sibling_maps,
        first_rows,
        0,
        3 * rank,
        projection_weight,
        projection_up_adapter,
        bounds,
    )
    attended = pl.pallas_call(
        attend_kernel,
        out_shape=jax.ShapeDtypeStruct((rows, width), bf16),
        in_specs=[spec(SMEM)] + [spec()] * 3,
        out_specs=spec(),
        compiler_params=params,
        cost_estimate=pl.CostEstimate(
            flops=4 * rows * width * context,
            bytes_accessed=4 * cache_keys.size,
            transcendentals=rows * width // head_dim * context,
        ),
        name="attend",
    )(lengths, qkv_mine, cache_keys, cache_values)
    column, pieces = gather_rows(attended, count)
    output, _ = project(
        column,
        pieces,
        tagged,
        own_maps,
        rest[0],
        None,
        3 * rank,
        4 * rank,
        output_weight,
        output_up_adapter,
        (0, width),
    )
    return output


def solution(mesh):
    count = mesh.shape[AXIS]

    def body(*arrays):
        return local(*arrays, count=count)

    return jax.shard_map(
        body,
        mesh=mesh,
        in_specs=(
            P(("groups", "tensor"), None),
            P(),
            P(("groups", "tensor"), None),
            P(),
            P(("groups", "tensor")),
            P(None, "tensor"),
            P(None, "tensor"),
            P("tensor", None, None),
            P(None, None, "tensor"),
            P(None, None, "tensor"),
            P(("groups", "tensor"), None, None, None),
            P(("groups", "tensor"), None, None, None),
        ),
        out_specs=P(("groups", "tensor"), None),
        check_vma=False,
    )
```

```python
import functools

import jax
import jax.numpy as jnp
from jax import lax
from jax.experimental import pallas as pl
from jax.experimental.pallas import tpu as pltpu
from jax.sharding import PartitionSpec as P

eps = 1e-05
AXIS = "tensor"
LANES = 128
VMEM = pltpu.VMEM
SMEM = pltpu.SMEM


def swap(x, count, offset):
    return lax.ppermute(x, AXIS, [(i, i ^ offset) for i in range(count)])


def exchange(x, groups=None):
    return lax.all_to_all(
        x, AXIS, split_axis=0, concat_axis=0, axis_index_groups=groups, tiled=True
    )


def sum_over(x, count, beside):
    step, turn, terms = count, 0, []
    while step > 1:
        radix = 4 if step % 4 == 0 else 2
        step //= radix
        others = [swap(x, count, k * step) for k in range(1, radix)]
        term = beside(turn, x)
        if term is not None:
            *others, term = lax.optimization_barrier((*others, term))
            terms.append(term)
        for other in others:
            x = x + other
        turn += 1
    return x, terms


def pack_kernel(*refs):
    in_refs, out_ref = refs[-2::-1], refs[-1]
    rows, width = in_refs[0].shape
    per = 16 // rows
    for first in range(0, len(in_refs), per):
        parts = [r[...].astype(jnp.float32) for r in in_refs[first : first + per]]
        at = slice(first * rows, (first + per) * rows)
        out_ref[at] = jnp.concatenate(parts, axis=0).astype(jnp.bfloat16)


def pack(parts):
    rows, width = parts[0].shape
    return pl.pallas_call(
        pack_kernel,
        out_shape=jax.ShapeDtypeStruct((rows * len(parts), width), jnp.bfloat16),
        in_specs=[spec()] * len(parts),
        out_specs=spec(),
        compiler_params=pltpu.CompilerParams(vmem_limit_bytes=16 * 1024 * 1024),
        name="pack",
    )(*parts[::-1])


def gather_rows(x, count, beside):
    step = count // 4
    near, middle, far = (swap(x, count, k * step) for k in (1, 2, 3))
    step //= 2
    across = [swap(p, count, step) for p in (x, near, middle, far)]
    *across, loaded = lax.optimization_barrier((*across[::-1], beside(far)))
    held = [pack([x, near, middle, far] + across[::-1])]
    step //= 2
    while step > 1:
        held = held + [swap(h, count, step) for h in held]
        step //= 2
    return held, held + [swap(h, count, 1) for h in held], loaded


def place_of(row, me, count, rows):
    block = row // rows
    source = (block % 4) * (count // 4)
    piece, step = block // 4, count // 8
    while step:
        source = source + (piece % 2) * step
        piece, step = piece // 2, step // 2
    return (source ^ me) * rows + row % rows


def spec(space=VMEM):
    return pl.BlockSpec(memory_space=space)


def hbm(x):
    return pltpu.with_memory_space_constraint(x, pltpu.HBM)


def iota(shape, dim):
    return lax.broadcasted_iota(jnp.int32, shape, dim)


def one_hot(condition):
    return jnp.where(condition, 1.0, 0.0).astype(jnp.bfloat16)


def norm_kernel(
    hidden_hbm, gain_hbm, names_hbm, slots_hbm, out_ref, hidden_ref, gain_ref, names_ref, slots_ref, sems
):
    copies = [
        pltpu.make_async_copy(source, target, sems.at[i])
        for i, (source, target) in enumerate(
            (
                (hidden_hbm, hidden_ref),
                (gain_hbm, gain_ref),
                (names_hbm, names_ref),
                (slots_hbm, slots_ref),
            )
        )
    ]
    for copy in copies:
        copy.start()
    for copy in copies:
        copy.wait()
    rows, width = hidden_ref.shape
    hidden = hidden_ref[...].astype(jnp.float32)
    power = jnp.sum(hidden * hidden, axis=1, keepdims=True) / width
    gain = gain_ref[...].reshape(1, width).astype(jnp.float32)
    out_ref[:, :width] = (hidden * lax.rsqrt(power + eps) * gain).astype(jnp.bfloat16)
    row, lane = iota((rows, LANES), 0), iota((rows, LANES), 1)
    tags = jnp.zeros((rows, LANES), jnp.float32)
    for r in range(rows):
        name = names_ref[r]
        tag = jnp.where(lane < LANES // 2, name, slots_ref[name]).astype(jnp.float32)
        tags = jnp.where(row == r, tag, tags)
    out_ref[:, width:] = tags.astype(jnp.bfloat16)


NT = (((1,), (1,)), ((), ()))


def load_kernel(starts, *refs):
    _, weight_hbm, *refs = refs
    *refs, sems = refs
    rows_refs, refs = refs[-len(starts) :], refs[: -len(starts)]
    copies = []
    if refs:
        maps_hbm, maps_ref = refs
        for s in range(maps_ref.shape[0]):
            copies.append((maps_hbm.at[s, : maps_ref.shape[1]], maps_ref.at[s]))
    for start, rows_ref in zip(starts, rows_refs):
        for k in range(0, rows_ref.shape[0], 1024):
            copies.append((weight_hbm.at[start + k : start + k + 1024], rows_ref.at[k : k + 1024]))
    copies = [pltpu.make_async_copy(*ends, sems.at[i]) for i, ends in enumerate(copies)]
    for copy in copies:
        copy.start()
    for copy in copies:
        copy.wait()


def down_kernel(count, rows, pieces, ranks, *refs):
    map_refs, piece_refs = refs[:2], refs[2 : 2 + pieces]
    tag_refs, refs = refs[2 + pieces : 2 + 2 * pieces], refs[2 + 2 * pieces :]
    out_ref = refs[0]
    me = lax.axis_index(AXIS)
    held, _, width = map_refs[0].shape
    rank = ranks[1] - ranks[0]
    total, half = count * rows, count * rows // 2
    chunk = 4096
    sums = jnp.zeros((2 * held * rank, half), jnp.float32)
    for k in range(0, width, chunk):
        x = jnp.concatenate([p[:, k : k + chunk] for p in piece_refs], axis=0)
        maps = jnp.concatenate(
            [m[:, :rank, k : k + chunk].reshape(held * rank, chunk) for m in map_refs], axis=0
        )
        sums = sums + lax.dot_general(maps, x, NT, preferred_element_type=jnp.float32)
    if len(refs) > 1:
        refs[1][...] = map_refs[1][:, rank:]
    tags = jnp.concatenate([t[...] for t in tag_refs], axis=0)
    pick = one_hot(iota((16, LANES), 1) == LANES // 2)
    slots = lax.dot_general(pick, tags, NT, preferred_element_type=jnp.float32)[:1]
    chosen = jnp.zeros((rank, half), jnp.float32)
    for m in range(2):
        for s in range(held):
            slot = ((me ^ m) * held + s).astype(jnp.float32)
            at = (m * held + s) * rank
            chosen = jnp.where(slots == slot, sums[at : at + rank], chosen)
    row, column = iota((half, total), 0), iota((half, total), 1)
    back = one_hot(place_of(row, me, count, rows) == column)
    placed = jnp.dot(chosen.astype(jnp.bfloat16), back, preferred_element_type=jnp.float32)
    folds = out_ref.shape[1] // total
    part = rank // folds
    folded = [placed[f * part : (f + 1) * part] for f in range(folds)]
    value = jnp.concatenate(folded, axis=1).astype(jnp.bfloat16)
    out_ref[...] = value


def spans_of(length):
    spans, at = [], 0
    while at < length:
        left = length - at
        size = 1024 if left > 1024 else min(left, 512)
        spans.append((at, size))
        at += size
    return spans


def base_kernel(pieces, start, ready, *refs):
    ready_ref = refs[pieces] if ready else None
    weight_hbm, _, out_ref, weight_ref, sems, side_ref = refs[-6:]
    total, columns = out_ref.shape
    whole = columns // 256 * 256
    narrow = columns - whole == 128
    spans = spans_of(weight_ref.shape[0])
    copies = [
        pltpu.make_async_copy(
            weight_hbm.at[start + ready + k : start + ready + k + length],
            weight_ref.at[k : k + length],
            sems.at[i],
        )
        for i, (k, length) in enumerate(spans)
    ]
    for copy in copies:
        copy.start()

    def rows_of(at, length):
        return jnp.concatenate([p[:, at : at + length] for p in refs[:pieces]], axis=0)

    def dot(x, weight):
        return jnp.dot(x, weight, preferred_element_type=jnp.float32)

    def wide(from_ref, k, length, offset):
        if whole:
            x = rows_of(start + offset, length)
            term = dot(x, from_ref[k : k + length, :whole])
            out_ref[:, :whole] = term if offset == 0 else out_ref[:, :whole] + term

    def rest(weight, offset):
        length = weight.shape[0]
        if narrow:
            half = length // 2
            left = [rows_of(start + offset + h, half) for h in (0, half)]
            right = [weight[:half], weight[half:]]
            term = dot(jnp.concatenate(left, axis=0), jnp.concatenate(right, axis=1))
        else:
            term = dot(rows_of(start + offset, length), weight)
        side_ref[...] = term if offset == 0 else side_ref[...] + term

    if ready:
        wide(ready_ref, 0, ready, 0)
    for (k, length), copy in zip(spans, copies):
        if (k, length) == spans[-1] and columns > whole:
            weight = weight_ref[:k, whole:]
            if ready:
                weight = jnp.concatenate([ready_ref[:, whole:], weight], axis=0)
            rest(weight, 0)
        copy.wait()
        wide(weight_ref, k, length, ready + k)
    if columns > whole:
        rest(weight_ref[k:, whole:], ready + k)
        side = side_ref[...]
        out_ref[:, whole:] = side[:total, :128] + side[total:, 128:] if narrow else side


def lift_kernel(count, rows, pieces, bounds, rank, *refs):
    tag_refs, refs = refs[:pieces], refs[pieces:]
    (down_ref, up_ref), base_refs, (out_ref, sum_ref) = refs[:2], refs[2:-2], refs[-2:]
    total = count * rows
    me = lax.axis_index(AXIS)
    adapters, per, columns = up_ref.shape
    wide = adapters * per
    row, column = iota((total, total), 0), iota((total, total), 1)
    order = one_hot(place_of(column, me, count, rows) == row)
    back = one_hot(place_of(row, me, count, rows) == column)
    folded = down_ref[...].astype(jnp.float32)
    folds = folded.shape[1] // total
    down = jnp.concatenate([folded[:, f * total : (f + 1) * total] for f in range(folds)], axis=0)
    down = lax.dot_general(
        back, down.astype(jnp.bfloat16), NT, preferred_element_type=jnp.float32
    ).astype(jnp.bfloat16)
    names = jnp.concatenate([t[...] for t in tag_refs], axis=0).astype(jnp.float32)[:, :1]
    named = (iota((total, wide), 1) // per).astype(jnp.float32) == names
    start = me * columns
    value = base_refs[0][...]
    for b in base_refs[1:]:
        value = value + b[...]
    sum_ref[...] = value
    for g in range(rank // per):
        low, high = bounds[g], bounds[g + 1]

        @pl.when((start < high) & (start + columns > low))
        def _():
            at = iota((rank, wide), 1) % per + g * per
            spread = one_hot(at == iota((rank, wide), 0))
            copies = jnp.dot(down, spread, preferred_element_type=jnp.float32)
            chosen = jnp.where(named, copies, 0.0).astype(jnp.bfloat16)
            up = up_ref[...].reshape(wide, columns)
            lifted = jnp.dot(chosen, up, preferred_element_type=jnp.float32)
            at = iota((total, columns), 1) + start
            sum_ref[...] += jnp.where((at >= low) & (at < high), lifted, 0.0)

    placed = jnp.dot(
        order, sum_ref[...].astype(jnp.bfloat16), preferred_element_type=jnp.float32
    ).astype(jnp.bfloat16)
    for d in range(count):
        out_ref[d] = placed[d * rows : (d + 1) * rows]


def attend_kernel(lengths_ref, qkv_ref, keys_ref, values_ref, out_ref):
    rows, kv_heads, context, dim = keys_ref.shape
    width = out_ref.shape[1]
    groups = width // dim // kv_heads
    per_head = groups * rows
    together = max(2, LANES // per_head)
    lanes = together * per_head
    lane = iota((1, lanes), 1)
    length = jnp.zeros((1, lanes), jnp.int32)
    for b in range(rows):
        length = jnp.where(lane % rows == b, lengths_ref[b], length)
    live = iota((context, lanes), 0) < length
    odd = iota((lanes, 1), 0) // per_head % 2 == 1
    pair_row = iota((2 * per_head, 1), 0)
    scale = dim ** (-0.5)

    def columns(at):
        return qkv_ref[:, at : at + dim].astype(jnp.float32)

    steps = []
    for first in range(0, kv_heads, together):
        heads = range(first, first + together)
        query = jnp.concatenate(
            [columns((h * groups + g) * dim) for h in heads for g in range(groups)], axis=0
        )
        half = jnp.concatenate([jnp.where(odd, 0.0, query), jnp.where(odd, query, 0.0)], axis=1)
        half = half.astype(jnp.bfloat16)
        scores = jnp.zeros((context, lanes), jnp.float32)
        for n in range(0, together, 2):
            cached = [keys_ref[:, first + n + m].reshape(rows * context, dim) for m in range(2)]
            every = lax.dot_general(
                jnp.concatenate(cached, axis=1), half, NT, preferred_element_type=jnp.float32
            )
            for b in range(rows):
                mine = (lane // (2 * per_head) == n // 2) & (lane % rows == b)
                scores = jnp.where(mine, every[b * context : (b + 1) * context], scores)
        steps.append((first, heads, query, scores))

    for i, (first, heads, query, scores) in enumerate(steps):
        key = jnp.concatenate([columns(width + h * dim) for h in heads for _ in range(groups)], axis=0)
        at = width + kv_heads * dim
        value = jnp.concatenate([columns(at + h * dim) for h in heads for _ in range(groups)], axis=0)
        scores = jnp.where(live, scores * scale, -1e30)
        own = jnp.sum((query * key).T, axis=0, keepdims=True) * scale
        peak = jnp.maximum(jnp.max(scores, axis=0, keepdims=True), own)
        weights = jnp.exp(scores - peak)
        own_weight = jnp.exp(own - peak)
        denominator = jnp.sum(weights, axis=0, keepdims=True) + own_weight
        probs = (weights / denominator).T.astype(jnp.bfloat16)
        own_prob = (own_weight / denominator).astype(jnp.bfloat16).astype(jnp.float32)
        steps[i] = (first, probs, jnp.broadcast_to(own_prob, (dim, lanes)).T * value)

    for first, probs, own_term in steps:
        for n in range(0, together, 2):
            span = slice(n * per_head, (n + 2) * per_head)
            mixed = jnp.zeros((2 * per_head, dim), jnp.float32)
            for b in range(rows):
                both = jnp.concatenate([values_ref[b, first + n + m] for m in range(2)], axis=1)
                one = jnp.dot(probs[span], both, preferred_element_type=jnp.float32)
                one = jnp.where(pair_row < per_head, one[:, :dim], one[:, dim:])
                mixed = jnp.where(pair_row % rows == b, one, mixed)
            mixed = (mixed + own_term[span]).astype(jnp.bfloat16)
            for g in range(2 * groups):
                at = ((first + n) * groups + g) * dim
                out_ref[:, at : at + dim] = mixed[g * rows : (g + 1) * rows]


def local(
    input_hidden,
    input_norm_gain,
    request_adapter,
    adapter_storage,
    lengths,
    projection_weight,
    output_weight,
    adapter_down,
    projection_up_adapter,
    output_up_adapter,
    cache_keys,
    cache_values,
    *,
    count,
):
    rows, width = input_hidden.shape
    rank = projection_up_adapter.shape[1]
    held = adapter_down.shape[0]
    kv_heads, context, head_dim = cache_keys.shape[1:]
    kv_width = kv_heads * head_dim
    total = rows * count
    bf16, f32 = jnp.bfloat16, jnp.float32
    params = pltpu.CompilerParams(vmem_limit_bytes=(16 if total <= 64 else 60) * 1024 * 1024)
    own_maps = jnp.swapaxes(adapter_down, 1, 2)

    normed = pl.pallas_call(
        norm_kernel,
        out_shape=VMEM((rows, width + LANES), bf16),
        in_specs=[spec(pltpu.HBM)] * 4,
        out_specs=spec(),
        scratch_shapes=[
            VMEM((rows, width), bf16),
            VMEM((width,), bf16),
            SMEM((rows,), jnp.int32),
            SMEM(adapter_storage.shape, jnp.int32),
            pltpu.SemaphoreType.DMA((4,)),
        ],
        compiler_params=params,
        name="norm",
    )(
        hbm(input_hidden),
        hbm(input_norm_gain),
        hbm(request_adapter.reshape(rows)),
        hbm(adapter_storage),
    )

    def load(after, weight, parts, maps=None):
        columns = weight.shape[1]
        outs = [VMEM((length, columns), bf16) for _, length in parts]
        sources, copies = [], sum(length // 1024 for _, length in parts)
        if maps is not None:
            outs = [VMEM((held, 3 * rank, width), bf16)] + outs
            sources, copies = [hbm(maps)], copies + held
        return pl.pallas_call(
            functools.partial(load_kernel, [start for start, _ in parts]),
            out_shape=outs,
            in_specs=[spec(pl.ANY)] + [spec(pltpu.HBM)] * (1 + len(sources)),
            out_specs=[spec()] * len(outs),
            scratch_shapes=[pltpu.SemaphoreType.DMA((copies,))],
            compiler_params=params,
            cost_estimate=pl.CostEstimate(
                flops=0,
                bytes_accessed=4 * columns * sum(length for _, length in parts),
                transcendentals=0,
            ),
            name="load",
        )(after, hbm(weight), *sources)

    def tag_specs(pieces):
        return [pl.BlockSpec((p.shape[0], LANES), lambda i: (0, width // LANES)) for p in pieces]

    def downs(own, sibling, pieces, tagged, low, high):
        ranks = high - low
        lanes = max(LANES, total)
        whole = lambda x: pl.BlockSpec(x.shape, lambda i: (0,) * len(x.shape))
        own_spec = pl.BlockSpec((held, ranks, width), lambda i: (0, low // ranks, 0))
        outs = [jax.ShapeDtypeStruct((ranks * total // lanes, lanes), bf16)]
        if low == 0:
            rest = sibling.shape[1] - ranks
            outs.append(jax.ShapeDtypeStruct((held, rest, width), bf16))
        return pl.pallas_call(
            functools.partial(down_kernel, count, rows, len(pieces), (low, high)),
            grid=(1,),
            out_shape=outs,
            in_specs=[own_spec, whole(sibling)]
            + [pl.BlockSpec((p.shape[0], width), lambda i: (0, 0)) for p in pieces]
            + tag_specs(tagged),
            out_specs=[whole(x) for x in outs],
            compiler_params=params,
            cost_estimate=pl.CostEstimate(
                flops=2 * total * width * held * ranks,
                bytes_accessed=2 * width * (2 * held * ranks + total),
                transcendentals=0,
            ),
            name="down",
        )(own, sibling, *pieces, *tagged)

    def base(pieces, weight, after, start, ready, length):
        columns = weight.shape[1]
        first = [] if ready is None else [ready]
        stream = length - sum(r.shape[0] for r in first)
        rest = columns % 256
        side = (2 * total, 256) if rest == 128 else (total, max(rest, 1))
        return pl.pallas_call(
            functools.partial(base_kernel, len(pieces), start, length - stream),
            out_shape=jax.ShapeDtypeStruct((total, columns), f32),
            in_specs=[spec()] * (len(pieces) + len(first)) + [spec(pltpu.HBM), spec(pl.ANY)],
            out_specs=spec(),
            scratch_shapes=[
                VMEM((stream, columns), bf16),
                pltpu.SemaphoreType.DMA((len(spans_of(stream)),)),
                VMEM(side, f32),
            ],
            compiler_params=params,
            cost_estimate=pl.CostEstimate(
                flops=2 * total * length * columns,
                bytes_accessed=4 * length * columns,
                transcendentals=0,
            ),
            name="base",
        )(*pieces, *first, hbm(weight), after)

    def lift(down, tagged, up, base_terms, bounds, ranks):
        columns = up.shape[2]
        whole = lambda x: pl.BlockSpec(x.shape, lambda i: (0,) * x.ndim)
        operands = [down, up] + base_terms
        return pl.pallas_call(
            functools.partial(lift_kernel, count, rows, len(tagged), bounds, ranks),
            grid=(1,),
            out_shape=jax.ShapeDtypeStruct((count, rows, columns), bf16),
            in_specs=tag_specs(tagged) + [whole(x) for x in operands],
            out_specs=pl.BlockSpec((count, rows, columns), lambda i: (0, 0, 0)),
            scratch_shapes=[VMEM((total, columns), f32)],
            compiler_params=params,
            name="lift",
        )(*tagged, *operands)

    def project(column, pieces, tagged, own, sibling, ready, low, high, weight, up, bounds):
        half = width // 2
        down, *rest = downs(own, sibling, column, tagged[: len(column)], low, high)

        def term(turn, after):
            if turn > 1:
                return None
            return base(pieces, weight, after, turn * half, ready[turn], half)

        down, base_terms = sum_over(down, count, term)
        columns = lift(down, tagged, up, base_terms, bounds, high - low)
        mine = exchange(columns)
        return jnp.swapaxes(mine, 0, 1).reshape(rows, -1), rest

    bounds = (0, width, width + kv_width, width + 2 * kv_width)
    sibling_maps = jnp.swapaxes(swap(adapter_down, count, 1), 1, 2)
    parts = ((0, 1024), (width // 2, 1024))
    column, tagged, (first_maps, *ready) = gather_rows(
        normed, count, lambda piece: load(piece, projection_weight, parts, own_maps)
    )
    qkv_mine, rest = project(
        column,
        tagged,
        tagged,
        first_maps,
        sibling_maps,
        ready,
        0,
        3 * rank,
        projection_weight,
        projection_up_adapter,
        bounds,
    )
    attended = pl.pallas_call(
        attend_kernel,
        out_shape=jax.ShapeDtypeStruct((rows, width), bf16),
        in_specs=[spec(SMEM)] + [spec()] * 3,
        out_specs=spec(),
        compiler_params=params,
        cost_estimate=pl.CostEstimate(
            flops=4 * rows * width * context,
            bytes_accessed=4 * cache_keys.size,
            transcendentals=rows * width // head_dim * context,
        ),
        name="attend",
    )(lengths, qkv_mine, cache_keys, cache_values)
    parts = ((0, 1024), (width // 2, 2048))
    column, pieces, ready = gather_rows(
        attended, count, lambda piece: load(piece, output_weight, parts)
    )
    output, _ = project(
        column,
        pieces,
        tagged,
        own_maps,
        rest[0],
        ready,
        3 * rank,
        4 * rank,
        output_weight,
        output_up_adapter,
        (0, width),
    )
    return output


def solution(mesh):
    count = mesh.shape[AXIS]

    def body(*arrays):
        return local(*arrays, count=count)

    return jax.shard_map(
        body,
        mesh=mesh,
        in_specs=(
            P(("groups", "tensor"), None),
            P(),
            P(("groups", "tensor"), None),
            P(),
            P(("groups", "tensor")),
            P(None, "tensor"),
            P(None, "tensor"),
            P("tensor", None, None),
            P(None, None, "tensor"),
            P(None, None, "tensor"),
            P(("groups", "tensor"), None, None, None),
            P(("groups", "tensor"), None, None, None),
        ),
        out_specs=P(("groups", "tensor"), None),
        check_vma=False,
    )
```

```python
import functools

import jax
import jax.numpy as jnp
from jax import lax
from jax.experimental import pallas as pl
from jax.experimental.pallas import tpu as pltpu
from jax.sharding import PartitionSpec as P

eps = 1e-05
AXIS = "tensor"
LANES = 128
VMEM = pltpu.VMEM
SMEM = pltpu.SMEM


def swap(x, count, offset):
    return lax.ppermute(x, AXIS, [(i, i ^ offset) for i in range(count)])


def exchange(x, groups=None):
    return lax.all_to_all(
        x, AXIS, split_axis=0, concat_axis=0, axis_index_groups=groups, tiled=True
    )


def sum_over(x, count, beside):
    step, turn, terms = count, 0, []
    while step > 1:
        radix = 4 if step % 4 == 0 else 2
        step //= radix
        others = [swap(x, count, k * step) for k in range(1, radix)]
        term = beside(turn, x)
        if term is not None:
            *others, term = lax.optimization_barrier((*others, term))
            terms.append(term)
        for other in others:
            x = x + other
        turn += 1
    return x, terms


def pack_kernel(*refs):
    in_refs, out_ref = refs[-2::-1], refs[-1]
    rows, width = in_refs[0].shape
    per = 16 // rows
    for first in range(0, len(in_refs), per):
        parts = [r[...].astype(jnp.float32) for r in in_refs[first : first + per]]
        at = slice(first * rows, (first + per) * rows)
        out_ref[at] = jnp.concatenate(parts, axis=0).astype(jnp.bfloat16)


def pack(parts):
    rows, width = parts[0].shape
    return pl.pallas_call(
        pack_kernel,
        out_shape=jax.ShapeDtypeStruct((rows * len(parts), width), jnp.bfloat16),
        in_specs=[spec()] * len(parts),
        out_specs=spec(),
        compiler_params=pltpu.CompilerParams(vmem_limit_bytes=16 * 1024 * 1024),
        name="pack",
    )(*parts[::-1])


def gather_rows(x, count, beside):
    step = count // 4
    near, middle, far = (swap(x, count, k * step) for k in (1, 2, 3))
    step //= 2
    across = [swap(p, count, step) for p in (far, near, middle, x)]
    *across, loaded = lax.optimization_barrier((*across, beside(far)))
    held = [pack([x, near, middle, far] + [across[i] for i in (3, 1, 2, 0)])]
    step //= 2
    while step > 1:
        held = held + [swap(h, count, step) for h in held]
        step //= 2
    return held, held + [swap(h, count, 1) for h in held], loaded


def place_of(row, me, count, rows):
    block = row // rows
    source = (block % 4) * (count // 4)
    piece, step = block // 4, count // 8
    while step:
        source = source + (piece % 2) * step
        piece, step = piece // 2, step // 2
    return (source ^ me) * rows + row % rows


def spec(space=VMEM):
    return pl.BlockSpec(memory_space=space)


def hbm(x):
    return pltpu.with_memory_space_constraint(x, pltpu.HBM)


def iota(shape, dim):
    return lax.broadcasted_iota(jnp.int32, shape, dim)


def one_hot(condition):
    return jnp.where(condition, 1.0, 0.0).astype(jnp.bfloat16)


def norm_kernel(
    hidden_hbm, gain_hbm, names_hbm, slots_hbm, out_ref, hidden_ref, gain_ref, names_ref, slots_ref, sems
):
    copies = [
        pltpu.make_async_copy(source, target, sems.at[i])
        for i, (source, target) in enumerate(
            (
                (hidden_hbm, hidden_ref),
                (gain_hbm, gain_ref),
                (names_hbm, names_ref),
                (slots_hbm, slots_ref),
            )
        )
    ]
    for copy in copies:
        copy.start()
    for copy in copies:
        copy.wait()
    rows, width = hidden_ref.shape
    hidden = hidden_ref[...].astype(jnp.float32)
    power = jnp.sum(hidden * hidden, axis=1, keepdims=True) / width
    gain = gain_ref[...].reshape(1, width).astype(jnp.float32)
    out_ref[:, :width] = (hidden * lax.rsqrt(power + eps) * gain).astype(jnp.bfloat16)
    row, lane = iota((rows, LANES), 0), iota((rows, LANES), 1)
    tags = jnp.zeros((rows, LANES), jnp.float32)
    for r in range(rows):
        name = names_ref[r]
        tag = jnp.where(lane < LANES // 2, name, slots_ref[name]).astype(jnp.float32)
        tags = jnp.where(row == r, tag, tags)
    out_ref[:, width:] = tags.astype(jnp.bfloat16)


NT = (((1,), (1,)), ((), ()))


def load_kernel(starts, *refs):
    _, weight_hbm, *refs = refs
    *refs, sems = refs
    rows_refs, refs = refs[-len(starts) :], refs[: -len(starts)]
    copies = []
    if refs:
        maps_hbm, maps_ref = refs
        for s in range(maps_ref.shape[0]):
            copies.append((maps_hbm.at[s, : maps_ref.shape[1]], maps_ref.at[s]))
    for start, rows_ref in zip(starts, rows_refs):
        for k in range(0, rows_ref.shape[0], 1024):
            copies.append((weight_hbm.at[start + k : start + k + 1024], rows_ref.at[k : k + 1024]))
    copies = [pltpu.make_async_copy(*ends, sems.at[i]) for i, ends in enumerate(copies)]
    for copy in copies:
        copy.start()
    for copy in copies:
        copy.wait()


def down_kernel(count, rows, pieces, ranks, *refs):
    map_refs, piece_refs = refs[:2], refs[2 : 2 + pieces]
    tag_refs, refs = refs[2 + pieces : 2 + 2 * pieces], refs[2 + 2 * pieces :]
    out_ref = refs[0]
    me = lax.axis_index(AXIS)
    held, _, width = map_refs[0].shape
    rank = ranks[1] - ranks[0]
    total, half = count * rows, count * rows // 2
    chunk = 4096
    sums = jnp.zeros((2 * held * rank, half), jnp.float32)
    for k in range(0, width, chunk):
        x = jnp.concatenate([p[:, k : k + chunk] for p in piece_refs], axis=0)
        maps = jnp.concatenate(
            [m[:, :rank, k : k + chunk].reshape(held * rank, chunk) for m in map_refs], axis=0
        )
        sums = sums + lax.dot_general(maps, x, NT, preferred_element_type=jnp.float32)
    if len(refs) > 1:
        refs[1][...] = map_refs[1][:, rank:]
    tags = jnp.concatenate([t[...] for t in tag_refs], axis=0)
    pick = one_hot(iota((16, LANES), 1) == LANES // 2)
    slots = lax.dot_general(pick, tags, NT, preferred_element_type=jnp.float32)[:1]
    chosen = jnp.zeros((rank, half), jnp.float32)
    for m in range(2):
        for s in range(held):
            slot = ((me ^ m) * held + s).astype(jnp.float32)
            at = (m * held + s) * rank
            chosen = jnp.where(slots == slot, sums[at : at + rank], chosen)
    row, column = iota((half, total), 0), iota((half, total), 1)
    back = one_hot(place_of(row, me, count, rows) == column)
    placed = jnp.dot(chosen.astype(jnp.bfloat16), back, preferred_element_type=jnp.float32)
    folds = out_ref.shape[1] // total
    part = rank // folds
    folded = [placed[f * part : (f + 1) * part] for f in range(folds)]
    value = jnp.concatenate(folded, axis=1).astype(jnp.bfloat16)
    out_ref[...] = value


def spans_of(length):
    spans, at = [], 0
    while at < length:
        left = length - at
        size = 1024 if left > 1024 else min(left, 512)
        spans.append((at, size))
        at += size
    return spans


def base_kernel(pieces, start, ready, *refs):
    ready_ref = refs[pieces] if ready else None
    weight_hbm, _, out_ref, weight_ref, sems, side_ref = refs[-6:]
    total, columns = out_ref.shape
    whole = columns // 256 * 256
    narrow = columns - whole == 128
    spans = spans_of(weight_ref.shape[0])
    copies = [
        pltpu.make_async_copy(
            weight_hbm.at[start + ready + k : start + ready + k + length],
            weight_ref.at[k : k + length],
            sems.at[i],
        )
        for i, (k, length) in enumerate(spans)
    ]
    for copy in copies:
        copy.start()

    def rows_of(at, length):
        return jnp.concatenate([p[:, at : at + length] for p in refs[:pieces]], axis=0)

    def dot(x, weight):
        return jnp.dot(x, weight, preferred_element_type=jnp.float32)

    def wide(from_ref, k, length, offset):
        if whole:
            x = rows_of(start + offset, length)
            term = dot(x, from_ref[k : k + length, :whole])
            out_ref[:, :whole] = term if offset == 0 else out_ref[:, :whole] + term

    def rest(weight, offset):
        length = weight.shape[0]
        if narrow:
            half = length // 2
            left = [rows_of(start + offset + h, half) for h in (0, half)]
            right = [weight[:half], weight[half:]]
            term = dot(jnp.concatenate(left, axis=0), jnp.concatenate(right, axis=1))
        else:
            term = dot(rows_of(start + offset, length), weight)
        side_ref[...] = term if offset == 0 else side_ref[...] + term

    if ready:
        wide(ready_ref, 0, ready, 0)
    for (k, length), copy in zip(spans, copies):
        if (k, length) == spans[-1] and columns > whole:
            weight = weight_ref[:k, whole:]
            if ready:
                weight = jnp.concatenate([ready_ref[:, whole:], weight], axis=0)
            rest(weight, 0)
        copy.wait()
        wide(weight_ref, k, length, ready + k)
    if columns > whole:
        rest(weight_ref[k:, whole:], ready + k)
        side = side_ref[...]
        out_ref[:, whole:] = side[:total, :128] + side[total:, 128:] if narrow else side


def lift_kernel(count, rows, pieces, bounds, rank, *refs):
    tag_refs, refs = refs[:pieces], refs[pieces:]
    (down_ref, up_ref), base_refs, (out_ref, sum_ref) = refs[:2], refs[2:-2], refs[-2:]
    total = count * rows
    me = lax.axis_index(AXIS)
    adapters, per, columns = up_ref.shape
    wide = adapters * per
    row, column = iota((total, total), 0), iota((total, total), 1)
    order = one_hot(place_of(column, me, count, rows) == row)
    back = one_hot(place_of(row, me, count, rows) == column)
    folded = down_ref[...].astype(jnp.float32)
    folds = folded.shape[1] // total
    down = jnp.concatenate([folded[:, f * total : (f + 1) * total] for f in range(folds)], axis=0)
    down = lax.dot_general(
        back, down.astype(jnp.bfloat16), NT, preferred_element_type=jnp.float32
    ).astype(jnp.bfloat16)
    names = jnp.concatenate([t[...] for t in tag_refs], axis=0).astype(jnp.float32)[:, :1]
    named = (iota((total, wide), 1) // per).astype(jnp.float32) == names
    start = me * columns
    value = base_refs[0][...]
    for b in base_refs[1:]:
        value = value + b[...]
    sum_ref[...] = value
    for g in range(rank // per):
        low, high = bounds[g], bounds[g + 1]

        @pl.when((start < high) & (start + columns > low))
        def _():
            at = iota((rank, wide), 1) % per + g * per
            spread = one_hot(at == iota((rank, wide), 0))
            copies = jnp.dot(down, spread, preferred_element_type=jnp.float32)
            chosen = jnp.where(named, copies, 0.0).astype(jnp.bfloat16)
            up = up_ref[...].reshape(wide, columns)
            lifted = jnp.dot(chosen, up, preferred_element_type=jnp.float32)
            at = iota((total, columns), 1) + start
            sum_ref[...] += jnp.where((at >= low) & (at < high), lifted, 0.0)

    placed = jnp.dot(
        order, sum_ref[...].astype(jnp.bfloat16), preferred_element_type=jnp.float32
    ).astype(jnp.bfloat16)
    for d in range(count):
        out_ref[d] = placed[d * rows : (d + 1) * rows]


def attend_kernel(lengths_ref, qkv_ref, keys_ref, values_ref, out_ref):
    rows, kv_heads, context, dim = keys_ref.shape
    width = out_ref.shape[1]
    groups = width // dim // kv_heads
    per_head = groups * rows
    together = max(2, LANES // per_head)
    lanes = together * per_head
    lane = iota((1, lanes), 1)
    length = jnp.zeros((1, lanes), jnp.int32)
    for b in range(rows):
        length = jnp.where(lane % rows == b, lengths_ref[b], length)
    live = iota((context, lanes), 0) < length
    odd = iota((lanes, 1), 0) // per_head % 2 == 1
    pair_row = iota((2 * per_head, 1), 0)
    scale = dim ** (-0.5)

    def columns(at):
        return qkv_ref[:, at : at + dim].astype(jnp.float32)

    steps = []
    for first in range(0, kv_heads, together):
        heads = range(first, first + together)
        query = jnp.concatenate(
            [columns((h * groups + g) * dim) for h in heads for g in range(groups)], axis=0
        )
        half = jnp.concatenate([jnp.where(odd, 0.0, query), jnp.where(odd, query, 0.0)], axis=1)
        half = half.astype(jnp.bfloat16)
        scores = jnp.zeros((context, lanes), jnp.float32)
        for n in range(0, together, 2):
            cached = [keys_ref[:, first + n + m].reshape(rows * context, dim) for m in range(2)]
            every = lax.dot_general(
                jnp.concatenate(cached, axis=1), half, NT, preferred_element_type=jnp.float32
            )
            for b in range(rows):
                mine = (lane // (2 * per_head) == n // 2) & (lane % rows == b)
                scores = jnp.where(mine, every[b * context : (b + 1) * context], scores)
        steps.append((first, heads, query, scores))

    for i, (first, heads, query, scores) in enumerate(steps):
        key = jnp.concatenate([columns(width + h * dim) for h in heads for _ in range(groups)], axis=0)
        at = width + kv_heads * dim
        value = jnp.concatenate([columns(at + h * dim) for h in heads for _ in range(groups)], axis=0)
        scores = jnp.where(live, scores * scale, -1e30)
        own = jnp.sum((query * key).T, axis=0, keepdims=True) * scale
        peak = jnp.maximum(jnp.max(scores, axis=0, keepdims=True), own)
        weights = jnp.exp(scores - peak)
        own_weight = jnp.exp(own - peak)
        denominator = jnp.sum(weights, axis=0, keepdims=True) + own_weight
        probs = (weights / denominator).T.astype(jnp.bfloat16)
        own_prob = (own_weight / denominator).astype(jnp.bfloat16).astype(jnp.float32)
        steps[i] = (first, probs, jnp.broadcast_to(own_prob, (dim, lanes)).T * value)

    for first, probs, own_term in steps:
        for n in range(0, together, 2):
            span = slice(n * per_head, (n + 2) * per_head)
            mixed = jnp.zeros((2 * per_head, dim), jnp.float32)
            for b in range(rows):
                both = jnp.concatenate([values_ref[b, first + n + m] for m in range(2)], axis=1)
                one = jnp.dot(probs[span], both, preferred_element_type=jnp.float32)
                one = jnp.where(pair_row < per_head, one[:, :dim], one[:, dim:])
                mixed = jnp.where(pair_row % rows == b, one, mixed)
            mixed = (mixed + own_term[span]).astype(jnp.bfloat16)
            for g in range(2 * groups):
                at = ((first + n) * groups + g) * dim
                out_ref[:, at : at + dim] = mixed[g * rows : (g + 1) * rows]


def local(
    input_hidden,
    input_norm_gain,
    request_adapter,
    adapter_storage,
    lengths,
    projection_weight,
    output_weight,
    adapter_down,
    projection_up_adapter,
    output_up_adapter,
    cache_keys,
    cache_values,
    *,
    count,
):
    rows, width = input_hidden.shape
    rank = projection_up_adapter.shape[1]
    held = adapter_down.shape[0]
    kv_heads, context, head_dim = cache_keys.shape[1:]
    kv_width = kv_heads * head_dim
    total = rows * count
    bf16, f32 = jnp.bfloat16, jnp.float32
    params = pltpu.CompilerParams(vmem_limit_bytes=(16 if total <= 64 else 60) * 1024 * 1024)
    own_maps = jnp.swapaxes(adapter_down, 1, 2)

    normed = pl.pallas_call(
        norm_kernel,
        out_shape=VMEM((rows, width + LANES), bf16),
        in_specs=[spec(pltpu.HBM)] * 4,
        out_specs=spec(),
        scratch_shapes=[
            VMEM((rows, width), bf16),
            VMEM((width,), bf16),
            SMEM((rows,), jnp.int32),
            SMEM(adapter_storage.shape, jnp.int32),
            pltpu.SemaphoreType.DMA((4,)),
        ],
        compiler_params=params,
        name="norm",
    )(
        hbm(input_hidden),
        hbm(input_norm_gain),
        hbm(request_adapter.reshape(rows)),
        hbm(adapter_storage),
    )

    def load(after, weight, parts, maps=None):
        columns = weight.shape[1]
        outs = [VMEM((length, columns), bf16) for _, length in parts]
        sources, copies = [], sum(length // 1024 for _, length in parts)
        if maps is not None:
            outs = [VMEM((held, 3 * rank, width), bf16)] + outs
            sources, copies = [hbm(maps)], copies + held
        return pl.pallas_call(
            functools.partial(load_kernel, [start for start, _ in parts]),
            out_shape=outs,
            in_specs=[spec(pl.ANY)] + [spec(pltpu.HBM)] * (1 + len(sources)),
            out_specs=[spec()] * len(outs),
            scratch_shapes=[pltpu.SemaphoreType.DMA((copies,))],
            compiler_params=params,
            cost_estimate=pl.CostEstimate(
                flops=0,
                bytes_accessed=4 * columns * sum(length for _, length in parts),
                transcendentals=0,
            ),
            name="load",
        )(after, hbm(weight), *sources)

    def tag_specs(pieces):
        return [pl.BlockSpec((p.shape[0], LANES), lambda i: (0, width // LANES)) for p in pieces]

    def downs(own, sibling, pieces, tagged, low, high):
        ranks = high - low
        lanes = max(LANES, total)
        whole = lambda x: pl.BlockSpec(x.shape, lambda i: (0,) * len(x.shape))
        own_spec = pl.BlockSpec((held, ranks, width), lambda i: (0, low // ranks, 0))
        outs = [jax.ShapeDtypeStruct((ranks * total // lanes, lanes), bf16)]
        if low == 0:
            rest = sibling.shape[1] - ranks
            outs.append(jax.ShapeDtypeStruct((held, rest, width), bf16))
        return pl.pallas_call(
            functools.partial(down_kernel, count, rows, len(pieces), (low, high)),
            grid=(1,),
            out_shape=outs,
            in_specs=[own_spec, whole(sibling)]
            + [pl.BlockSpec((p.shape[0], width), lambda i: (0, 0)) for p in pieces]
            + tag_specs(tagged),
            out_specs=[whole(x) for x in outs],
            compiler_params=params,
            cost_estimate=pl.CostEstimate(
                flops=2 * total * width * held * ranks,
                bytes_accessed=2 * width * (2 * held * ranks + total),
                transcendentals=0,
            ),
            name="down",
        )(own, sibling, *pieces, *tagged)

    def base(pieces, weight, after, start, ready, length):
        columns = weight.shape[1]
        first = [] if ready is None else [ready]
        stream = length - sum(r.shape[0] for r in first)
        rest = columns % 256
        side = (2 * total, 256) if rest == 128 else (total, max(rest, 1))
        return pl.pallas_call(
            functools.partial(base_kernel, len(pieces), start, length - stream),
            out_shape=jax.ShapeDtypeStruct((total, columns), f32),
            in_specs=[spec()] * (len(pieces) + len(first)) + [spec(pltpu.HBM), spec(pl.ANY)],
            out_specs=spec(),
            scratch_shapes=[
                VMEM((stream, columns), bf16),
                pltpu.SemaphoreType.DMA((len(spans_of(stream)),)),
                VMEM(side, f32),
            ],
            compiler_params=params,
            cost_estimate=pl.CostEstimate(
                flops=2 * total * length * columns,
                bytes_accessed=4 * length * columns,
                transcendentals=0,
            ),
            name="base",
        )(*pieces, *first, hbm(weight), after)

    def lift(down, tagged, up, base_terms, bounds, ranks):
        columns = up.shape[2]
        whole = lambda x: pl.BlockSpec(x.shape, lambda i: (0,) * x.ndim)
        operands = [down, up] + base_terms
        return pl.pallas_call(
            functools.partial(lift_kernel, count, rows, len(tagged), bounds, ranks),
            grid=(1,),
            out_shape=jax.ShapeDtypeStruct((count, rows, columns), bf16),
            in_specs=tag_specs(tagged) + [whole(x) for x in operands],
            out_specs=pl.BlockSpec((count, rows, columns), lambda i: (0, 0, 0)),
            scratch_shapes=[VMEM((total, columns), f32)],
            compiler_params=params,
            name="lift",
        )(*tagged, *operands)

    def project(column, pieces, tagged, own, sibling, ready, low, high, weight, up, bounds):
        half = width // 2
        down, *rest = downs(own, sibling, column, tagged[: len(column)], low, high)

        def term(turn, after):
            if turn > 1:
                return None
            return base(pieces, weight, after, turn * half, ready[turn], half)

        down, base_terms = sum_over(down, count, term)
        columns = lift(down, tagged, up, base_terms, bounds, high - low)
        mine = exchange(columns)
        return jnp.swapaxes(mine, 0, 1).reshape(rows, -1), rest

    bounds = (0, width, width + kv_width, width + 2 * kv_width)
    sibling_maps = jnp.swapaxes(swap(adapter_down, count, 1), 1, 2)
    parts = ((0, 1024), (width // 2, 2048))
    column, tagged, (first_maps, *ready) = gather_rows(
        normed, count, lambda piece: load(piece, projection_weight, parts, own_maps)
    )
    qkv_mine, rest = project(
        column,
        tagged,
        tagged,
        first_maps,
        sibling_maps,
        ready,
        0,
        3 * rank,
        projection_weight,
        projection_up_adapter,
        bounds,
    )
    attended = pl.pallas_call(
        attend_kernel,
        out_shape=jax.ShapeDtypeStruct((rows, width), bf16),
        in_specs=[spec(SMEM)] + [spec()] * 3,
        out_specs=spec(),
        compiler_params=params,
        cost_estimate=pl.CostEstimate(
            flops=4 * rows * width * context,
            bytes_accessed=4 * cache_keys.size,
            transcendentals=rows * width // head_dim * context,
        ),
        name="attend",
    )(lengths, qkv_mine, cache_keys, cache_values)
    parts = ((0, 1024), (width // 2, 2048))
    column, pieces, ready = gather_rows(
        attended, count, lambda piece: load(piece, output_weight, parts)
    )
    output, _ = project(
        column,
        pieces,
        tagged,
        own_maps,
        rest[0],
        ready,
        3 * rank,
        4 * rank,
        output_weight,
        output_up_adapter,
        (0, width),
    )
    return output


def solution(mesh):
    count = mesh.shape[AXIS]

    def body(*arrays):
        return local(*arrays, count=count)

    return jax.shard_map(
        body,
        mesh=mesh,
        in_specs=(
            P(("groups", "tensor"), None),
            P(),
            P(("groups", "tensor"), None),
            P(),
            P(("groups", "tensor")),
            P(None, "tensor"),
            P(None, "tensor"),
            P("tensor", None, None),
            P(None, None, "tensor"),
            P(None, None, "tensor"),
            P(("groups", "tensor"), None, None, None),
            P(("groups", "tensor"), None, None, None),
        ),
        out_specs=P(("groups", "tensor"), None),
        check_vma=False,
    )
```

```python
import functools

import jax
import jax.numpy as jnp
from jax import lax
from jax.experimental import pallas as pl
from jax.experimental.pallas import tpu as pltpu
from jax.sharding import PartitionSpec as P

eps = 1e-05
AXIS = "tensor"
LANES = 128
VMEM = pltpu.VMEM
SMEM = pltpu.SMEM


def swap(x, count, offset):
    return lax.ppermute(x, AXIS, [(i, i ^ offset) for i in range(count)])


def exchange(x, groups=None):
    return lax.all_to_all(
        x, AXIS, split_axis=0, concat_axis=0, axis_index_groups=groups, tiled=True
    )


def sum_over(x, count, beside):
    step, turn, terms = count, 0, []
    while step > 1:
        radix = 4 if step % 4 == 0 else 2
        step //= radix
        others = [swap(x, count, k * step) for k in range(1, radix)]
        term = beside(turn, x)
        if term is not None:
            *others, term = lax.optimization_barrier((*others, term))
            terms.append(term)
        for other in others:
            x = x + other
        turn += 1
    return x, terms


def pack_kernel(*refs):
    in_refs, out_ref = refs[-2::-1], refs[-1]
    rows, width = in_refs[0].shape
    per = 16 // rows
    for first in range(0, len(in_refs), per):
        parts = [r[...].astype(jnp.float32) for r in in_refs[first : first + per]]
        at = slice(first * rows, (first + per) * rows)
        out_ref[at] = jnp.concatenate(parts, axis=0).astype(jnp.bfloat16)


def pack(parts):
    rows, width = parts[0].shape
    return pl.pallas_call(
        pack_kernel,
        out_shape=jax.ShapeDtypeStruct((rows * len(parts), width), jnp.bfloat16),
        in_specs=[spec()] * len(parts),
        out_specs=spec(),
        compiler_params=pltpu.CompilerParams(vmem_limit_bytes=16 * 1024 * 1024),
        name="pack",
    )(*parts[::-1])


def gather_rows(x, count, beside):
    step = count // 4
    near, middle, far = (swap(x, count, k * step) for k in (1, 2, 3))
    step //= 2
    across = [swap(p, count, step) for p in (far, near, middle, x)]
    *across, loaded = lax.optimization_barrier((*across, beside(far)))
    held = [pack([x, near, middle, far] + [across[i] for i in (3, 1, 2, 0)])]
    step //= 2
    while step > 1:
        held = held + [swap(h, count, step) for h in held]
        step //= 2
    return held, held + [swap(h, count, 1) for h in held], loaded


def place_of(row, me, count, rows):
    block = row // rows
    source = (block % 4) * (count // 4)
    piece, step = block // 4, count // 8
    while step:
        source = source + (piece % 2) * step
        piece, step = piece // 2, step // 2
    return (source ^ me) * rows + row % rows


def spec(space=VMEM):
    return pl.BlockSpec(memory_space=space)


def hbm(x):
    return pltpu.with_memory_space_constraint(x, pltpu.HBM)


def iota(shape, dim):
    return lax.broadcasted_iota(jnp.int32, shape, dim)


def one_hot(condition):
    return jnp.where(condition, 1.0, 0.0).astype(jnp.bfloat16)


def norm_kernel(
    hidden_hbm, gain_hbm, names_hbm, slots_hbm, out_ref, hidden_ref, gain_ref, names_ref, slots_ref, sems
):
    copies = [
        pltpu.make_async_copy(source, target, sems.at[i])
        for i, (source, target) in enumerate(
            (
                (hidden_hbm, hidden_ref),
                (gain_hbm, gain_ref),
                (names_hbm, names_ref),
                (slots_hbm, slots_ref),
            )
        )
    ]
    for copy in copies:
        copy.start()
    for copy in copies:
        copy.wait()
    rows, width = hidden_ref.shape
    hidden = hidden_ref[...].astype(jnp.float32)
    power = jnp.sum(hidden * hidden, axis=1, keepdims=True) / width
    gain = gain_ref[...].reshape(1, width).astype(jnp.float32)
    out_ref[:, :width] = (hidden * lax.rsqrt(power + eps) * gain).astype(jnp.bfloat16)
    row, lane = iota((rows, LANES), 0), iota((rows, LANES), 1)
    tags = jnp.zeros((rows, LANES), jnp.float32)
    for r in range(rows):
        name = names_ref[r]
        tag = jnp.where(lane < LANES // 2, name, slots_ref[name]).astype(jnp.float32)
        tags = jnp.where(row == r, tag, tags)
    out_ref[:, width:] = tags.astype(jnp.bfloat16)


NT = (((1,), (1,)), ((), ()))


def load_kernel(starts, *refs):
    _, weight_hbm, *refs = refs
    *refs, sems = refs
    rows_refs, refs = refs[-len(starts) :], refs[: -len(starts)]
    copies = []
    if refs:
        maps_hbm, maps_ref = refs
        for s in range(maps_ref.shape[0]):
            copies.append((maps_hbm.at[s, : maps_ref.shape[1]], maps_ref.at[s]))
    for start, rows_ref in zip(starts, rows_refs):
        for k in range(0, rows_ref.shape[0], 1024):
            copies.append((weight_hbm.at[start + k : start + k + 1024], rows_ref.at[k : k + 1024]))
    copies = [pltpu.make_async_copy(*ends, sems.at[i]) for i, ends in enumerate(copies)]
    for copy in copies:
        copy.start()
    for copy in copies:
        copy.wait()


def down_kernel(count, rows, pieces, ranks, *refs):
    map_refs, piece_refs = refs[:2], refs[2 : 2 + pieces]
    tag_refs, refs = refs[2 + pieces : 2 + 2 * pieces], refs[2 + 2 * pieces :]
    out_ref = refs[0]
    me = lax.axis_index(AXIS)
    held, _, width = map_refs[0].shape
    rank = ranks[1] - ranks[0]
    total, half = count * rows, count * rows // 2
    chunk = 4096
    sums = jnp.zeros((2 * held * rank, half), jnp.float32)
    for k in range(0, width, chunk):
        x = jnp.concatenate([p[:, k : k + chunk] for p in piece_refs], axis=0)
        maps = jnp.concatenate(
            [m[:, :rank, k : k + chunk].reshape(held * rank, chunk) for m in map_refs], axis=0
        )
        sums = sums + lax.dot_general(maps, x, NT, preferred_element_type=jnp.float32)
    if len(refs) > 1:
        refs[1][...] = map_refs[1][:, rank:]
    tags = jnp.concatenate([t[...] for t in tag_refs], axis=0)
    pick = one_hot(iota((16, LANES), 1) == LANES // 2)
    slots = lax.dot_general(pick, tags, NT, preferred_element_type=jnp.float32)[:1]
    chosen = jnp.zeros((rank, half), jnp.float32)
    for m in range(2):
        for s in range(held):
            slot = ((me ^ m) * held + s).astype(jnp.float32)
            at = (m * held + s) * rank
            chosen = jnp.where(slots == slot, sums[at : at + rank], chosen)
    row, column = iota((half, total), 0), iota((half, total), 1)
    back = one_hot(place_of(row, me, count, rows) == column)
    placed = jnp.dot(chosen.astype(jnp.bfloat16), back, preferred_element_type=jnp.float32)
    folds = out_ref.shape[1] // total
    part = rank // folds
    folded = [placed[f * part : (f + 1) * part] for f in range(folds)]
    value = jnp.concatenate(folded, axis=1).astype(jnp.bfloat16)
    out_ref[...] = value


def spans_of(length):
    spans, at = [], 0
    while at < length:
        left = length - at
        size = 1024 if left > 1024 else min(left, 512)
        spans.append((at, size))
        at += size
    return spans


def base_kernel(pieces, start, ready, *refs):
    ready_ref = refs[pieces] if ready else None
    weight_hbm, _, out_ref, weight_ref, sems, side_ref = refs[-6:]
    total, columns = out_ref.shape
    whole = columns // 256 * 256
    narrow = columns - whole == 128
    spans = spans_of(weight_ref.shape[0])
    copies = [
        pltpu.make_async_copy(
            weight_hbm.at[start + ready + k : start + ready + k + length],
            weight_ref.at[k : k + length],
            sems.at[i],
        )
        for i, (k, length) in enumerate(spans)
    ]
    for copy in copies:
        copy.start()

    def rows_of(at, length):
        return jnp.concatenate([p[:, at : at + length] for p in refs[:pieces]], axis=0)

    def dot(x, weight):
        return jnp.dot(x, weight, preferred_element_type=jnp.float32)

    def wide(from_ref, k, length, offset):
        if whole:
            x = rows_of(start + offset, length)
            term = dot(x, from_ref[k : k + length, :whole])
            out_ref[:, :whole] = term if offset == 0 else out_ref[:, :whole] + term

    def rest(weight, offset):
        length = weight.shape[0]
        if narrow:
            half = length // 2
            left = [rows_of(start + offset + h, half) for h in (0, half)]
            right = [weight[:half], weight[half:]]
            term = dot(jnp.concatenate(left, axis=0), jnp.concatenate(right, axis=1))
        else:
            term = dot(rows_of(start + offset, length), weight)
        side_ref[...] = term if offset == 0 else side_ref[...] + term

    if ready:
        wide(ready_ref, 0, ready, 0)
    for (k, length), copy in zip(spans, copies):
        if (k, length) == spans[-1] and columns > whole:
            weight = weight_ref[:k, whole:]
            if ready:
                weight = jnp.concatenate([ready_ref[:, whole:], weight], axis=0)
            rest(weight, 0)
        copy.wait()
        wide(weight_ref, k, length, ready + k)
    if columns > whole:
        rest(weight_ref[k:, whole:], ready + k)
        side = side_ref[...]
        out_ref[:, whole:] = side[:total, :128] + side[total:, 128:] if narrow else side


def lift_kernel(count, rows, pieces, bounds, rank, *refs):
    tag_refs, refs = refs[:pieces], refs[pieces:]
    (down_ref, up_ref), base_refs, (out_ref, sum_ref) = refs[:2], refs[2:-2], refs[-2:]
    total = count * rows
    me = lax.axis_index(AXIS)
    adapters, per, columns = up_ref.shape
    wide = adapters * per
    row, column = iota((total, total), 0), iota((total, total), 1)
    order = one_hot(place_of(column, me, count, rows) == row)
    back = one_hot(place_of(row, me, count, rows) == column)
    folded = down_ref[...].astype(jnp.float32)
    folds = folded.shape[1] // total
    down = jnp.concatenate([folded[:, f * total : (f + 1) * total] for f in range(folds)], axis=0)
    down = lax.dot_general(
        back, down.astype(jnp.bfloat16), NT, preferred_element_type=jnp.float32
    ).astype(jnp.bfloat16)
    names = jnp.concatenate([t[...] for t in tag_refs], axis=0).astype(jnp.float32)[:, :1]
    named = (iota((total, wide), 1) // per).astype(jnp.float32) == names
    start = me * columns
    value = base_refs[0][...]
    for b in base_refs[1:]:
        value = value + b[...]
    sum_ref[...] = value
    for g in range(rank // per):
        low, high = bounds[g], bounds[g + 1]

        @pl.when((start < high) & (start + columns > low))
        def _():
            at = iota((rank, wide), 1) % per + g * per
            spread = one_hot(at == iota((rank, wide), 0))
            copies = jnp.dot(down, spread, preferred_element_type=jnp.float32)
            chosen = jnp.where(named, copies, 0.0).astype(jnp.bfloat16)
            up = up_ref[...].reshape(wide, columns)
            lifted = jnp.dot(chosen, up, preferred_element_type=jnp.float32)
            at = iota((total, columns), 1) + start
            sum_ref[...] += jnp.where((at >= low) & (at < high), lifted, 0.0)

    placed = jnp.dot(
        order, sum_ref[...].astype(jnp.bfloat16), preferred_element_type=jnp.float32
    ).astype(jnp.bfloat16)
    for d in range(count):
        out_ref[d] = placed[d * rows : (d + 1) * rows]


def attend_kernel(lengths_ref, qkv_ref, keys_ref, values_ref, out_ref):
    rows, kv_heads, context, dim = keys_ref.shape
    width = out_ref.shape[1]
    groups = width // dim // kv_heads
    per_head = groups * rows
    together = max(2, LANES // per_head)
    lanes = together * per_head
    lane = iota((1, lanes), 1)
    length = jnp.zeros((1, lanes), jnp.int32)
    for b in range(rows):
        length = jnp.where(lane % rows == b, lengths_ref[b], length)
    live = iota((context, lanes), 0) < length
    odd = iota((lanes, 1), 0) // per_head % 2 == 1
    pair_row = iota((2 * per_head, 1), 0)
    scale = dim ** (-0.5)

    def columns(at):
        return qkv_ref[:, at : at + dim].astype(jnp.float32)

    steps = []
    for first in range(0, kv_heads, together):
        heads = range(first, first + together)
        query = jnp.concatenate(
            [columns((h * groups + g) * dim) for h in heads for g in range(groups)], axis=0
        )
        half = jnp.concatenate([jnp.where(odd, 0.0, query), jnp.where(odd, query, 0.0)], axis=1)
        half = half.astype(jnp.bfloat16)
        scores = jnp.zeros((context, lanes), jnp.float32)
        for n in range(0, together, 2):
            cached = [keys_ref[:, first + n + m].reshape(rows * context, dim) for m in range(2)]
            every = lax.dot_general(
                jnp.concatenate(cached, axis=1), half, NT, preferred_element_type=jnp.float32
            )
            for b in range(rows):
                mine = (lane // (2 * per_head) == n // 2) & (lane % rows == b)
                scores = jnp.where(mine, every[b * context : (b + 1) * context], scores)
        steps.append((first, heads, query, scores))

    for i, (first, heads, query, scores) in enumerate(steps):
        key = jnp.concatenate([columns(width + h * dim) for h in heads for _ in range(groups)], axis=0)
        at = width + kv_heads * dim
        value = jnp.concatenate([columns(at + h * dim) for h in heads for _ in range(groups)], axis=0)
        scores = jnp.where(live, scores * scale, -1e30)
        own = jnp.sum((query * key).T, axis=0, keepdims=True) * scale
        peak = jnp.maximum(jnp.max(scores, axis=0, keepdims=True), own)
        weights = jnp.exp(scores - peak)
        own_weight = jnp.exp(own - peak)
        denominator = jnp.sum(weights, axis=0, keepdims=True) + own_weight
        share = 1.0 / denominator
        probs = (weights * share).T.astype(jnp.bfloat16)
        own_prob = (own_weight * share).astype(jnp.bfloat16).astype(jnp.float32)
        steps[i] = (first, probs, jnp.broadcast_to(own_prob, (dim, lanes)).T * value)

    for first, probs, own_term in steps:
        for n in range(0, together, 2):
            span = slice(n * per_head, (n + 2) * per_head)
            mixed = jnp.zeros((2 * per_head, dim), jnp.float32)
            for b in range(rows):
                both = jnp.concatenate([values_ref[b, first + n + m] for m in range(2)], axis=1)
                one = jnp.dot(probs[span], both, preferred_element_type=jnp.float32)
                one = jnp.where(pair_row < per_head, one[:, :dim], one[:, dim:])
                mixed = jnp.where(pair_row % rows == b, one, mixed)
            mixed = (mixed + own_term[span]).astype(jnp.bfloat16)
            for g in range(2 * groups):
                at = ((first + n) * groups + g) * dim
                out_ref[:, at : at + dim] = mixed[g * rows : (g + 1) * rows]


def local(
    input_hidden,
    input_norm_gain,
    request_adapter,
    adapter_storage,
    lengths,
    projection_weight,
    output_weight,
    adapter_down,
    projection_up_adapter,
    output_up_adapter,
    cache_keys,
    cache_values,
    *,
    count,
):
    rows, width = input_hidden.shape
    rank = projection_up_adapter.shape[1]
    held = adapter_down.shape[0]
    kv_heads, context, head_dim = cache_keys.shape[1:]
    kv_width = kv_heads * head_dim
    total = rows * count
    bf16, f32 = jnp.bfloat16, jnp.float32
    params = pltpu.CompilerParams(vmem_limit_bytes=(16 if total <= 64 else 60) * 1024 * 1024)
    own_maps = jnp.swapaxes(adapter_down, 1, 2)

    normed = pl.pallas_call(
        norm_kernel,
        out_shape=VMEM((rows, width + LANES), bf16),
        in_specs=[spec(pltpu.HBM)] * 4,
        out_specs=spec(),
        scratch_shapes=[
            VMEM((rows, width), bf16),
            VMEM((width,), bf16),
            SMEM((rows,), jnp.int32),
            SMEM(adapter_storage.shape, jnp.int32),
            pltpu.SemaphoreType.DMA((4,)),
        ],
        compiler_params=params,
        name="norm",
    )(
        hbm(input_hidden),
        hbm(input_norm_gain),
        hbm(request_adapter.reshape(rows)),
        hbm(adapter_storage),
    )

    def load(after, weight, parts, maps=None):
        columns = weight.shape[1]
        outs = [VMEM((length, columns), bf16) for _, length in parts]
        sources, copies = [], sum(length // 1024 for _, length in parts)
        if maps is not None:
            outs = [VMEM((held, 3 * rank, width), bf16)] + outs
            sources, copies = [hbm(maps)], copies + held
        return pl.pallas_call(
            functools.partial(load_kernel, [start for start, _ in parts]),
            out_shape=outs,
            in_specs=[spec(pl.ANY)] + [spec(pltpu.HBM)] * (1 + len(sources)),
            out_specs=[spec()] * len(outs),
            scratch_shapes=[pltpu.SemaphoreType.DMA((copies,))],
            compiler_params=params,
            cost_estimate=pl.CostEstimate(
                flops=0,
                bytes_accessed=4 * columns * sum(length for _, length in parts),
                transcendentals=0,
            ),
            name="load",
        )(after, hbm(weight), *sources)

    def tag_specs(pieces):
        return [pl.BlockSpec((p.shape[0], LANES), lambda i: (0, width // LANES)) for p in pieces]

    def downs(own, sibling, pieces, tagged, low, high):
        ranks = high - low
        lanes = max(LANES, total)
        whole = lambda x: pl.BlockSpec(x.shape, lambda i: (0,) * len(x.shape))
        own_spec = pl.BlockSpec((held, ranks, width), lambda i: (0, low // ranks, 0))
        outs = [jax.ShapeDtypeStruct((ranks * total // lanes, lanes), bf16)]
        if low == 0:
            rest = sibling.shape[1] - ranks
            outs.append(jax.ShapeDtypeStruct((held, rest, width), bf16))
        return pl.pallas_call(
            functools.partial(down_kernel, count, rows, len(pieces), (low, high)),
            grid=(1,),
            out_shape=outs,
            in_specs=[own_spec, whole(sibling)]
            + [pl.BlockSpec((p.shape[0], width), lambda i: (0, 0)) for p in pieces]
            + tag_specs(tagged),
            out_specs=[whole(x) for x in outs],
            compiler_params=params,
            cost_estimate=pl.CostEstimate(
                flops=2 * total * width * held * ranks,
                bytes_accessed=2 * width * (2 * held * ranks + total),
                transcendentals=0,
            ),
            name="down",
        )(own, sibling, *pieces, *tagged)

    def base(pieces, weight, after, start, ready, length):
        columns = weight.shape[1]
        first = [] if ready is None else [ready]
        stream = length - sum(r.shape[0] for r in first)
        rest = columns % 256
        side = (2 * total, 256) if rest == 128 else (total, max(rest, 1))
        return pl.pallas_call(
            functools.partial(base_kernel, len(pieces), start, length - stream),
            out_shape=jax.ShapeDtypeStruct((total, columns), f32),
            in_specs=[spec()] * (len(pieces) + len(first)) + [spec(pltpu.HBM), spec(pl.ANY)],
            out_specs=spec(),
            scratch_shapes=[
                VMEM((stream, columns), bf16),
                pltpu.SemaphoreType.DMA((len(spans_of(stream)),)),
                VMEM(side, f32),
            ],
            compiler_params=params,
            cost_estimate=pl.CostEstimate(
                flops=2 * total * length * columns,
                bytes_accessed=4 * length * columns,
                transcendentals=0,
            ),
            name="base",
        )(*pieces, *first, hbm(weight), after)

    def lift(down, tagged, up, base_terms, bounds, ranks):
        columns = up.shape[2]
        whole = lambda x: pl.BlockSpec(x.shape, lambda i: (0,) * x.ndim)
        operands = [down, up] + base_terms
        return pl.pallas_call(
            functools.partial(lift_kernel, count, rows, len(tagged), bounds, ranks),
            grid=(1,),
            out_shape=jax.ShapeDtypeStruct((count, rows, columns), bf16),
            in_specs=tag_specs(tagged) + [whole(x) for x in operands],
            out_specs=pl.BlockSpec((count, rows, columns), lambda i: (0, 0, 0)),
            scratch_shapes=[VMEM((total, columns), f32)],
            compiler_params=params,
            name="lift",
        )(*tagged, *operands)

    def project(column, pieces, tagged, own, sibling, ready, low, high, weight, up, bounds):
        half = width // 2
        down, *rest = downs(own, sibling, column, tagged[: len(column)], low, high)

        def term(turn, after):
            if turn > 1:
                return None
            return base(pieces, weight, after, turn * half, ready[turn], half)

        down, base_terms = sum_over(down, count, term)
        columns = lift(down, tagged, up, base_terms, bounds, high - low)
        mine = exchange(columns)
        return jnp.swapaxes(mine, 0, 1).reshape(rows, -1), rest

    bounds = (0, width, width + kv_width, width + 2 * kv_width)
    sibling_maps = jnp.swapaxes(swap(adapter_down, count, 1), 1, 2)
    parts = ((0, 2048), (width // 2, 2048))
    column, tagged, (first_maps, *ready) = gather_rows(
        normed, count, lambda piece: load(piece, projection_weight, parts, own_maps)
    )
    qkv_mine, rest = project(
        column,
        tagged,
        tagged,
        first_maps,
        sibling_maps,
        ready,
        0,
        3 * rank,
        projection_weight,
        projection_up_adapter,
        bounds,
    )
    attended = pl.pallas_call(
        attend_kernel,
        out_shape=jax.ShapeDtypeStruct((rows, width), bf16),
        in_specs=[spec(SMEM)] + [spec()] * 3,
        out_specs=spec(),
        compiler_params=params,
        cost_estimate=pl.CostEstimate(
            flops=4 * rows * width * context,
            bytes_accessed=4 * cache_keys.size,
            transcendentals=rows * width // head_dim * context,
        ),
        name="attend",
    )(lengths, qkv_mine, cache_keys, cache_values)
    parts = ((0, 1024), (width // 2, 2048))
    column, pieces, ready = gather_rows(
        attended, count, lambda piece: load(piece, output_weight, parts)
    )
    output, _ = project(
        column,
        pieces,
        tagged,
        own_maps,
        rest[0],
        ready,
        3 * rank,
        4 * rank,
        output_weight,
        output_up_adapter,
        (0, width),
    )
    return output


def solution(mesh):
    count = mesh.shape[AXIS]

    def body(*arrays):
        return local(*arrays, count=count)

    return jax.shard_map(
        body,
        mesh=mesh,
        in_specs=(
            P(("groups", "tensor"), None),
            P(),
            P(("groups", "tensor"), None),
            P(),
            P(("groups", "tensor")),
            P(None, "tensor"),
            P(None, "tensor"),
            P("tensor", None, None),
            P(None, None, "tensor"),
            P(None, None, "tensor"),
            P(("groups", "tensor"), None, None, None),
            P(("groups", "tensor"), None, None, None),
        ),
        out_specs=P(("groups", "tensor"), None),
        check_vma=False,
    )
```

```python
import functools

import jax
import jax.numpy as jnp
from jax import lax
from jax.experimental import pallas as pl
from jax.experimental.pallas import tpu as pltpu
from jax.sharding import PartitionSpec as P

eps = 1e-05
AXIS = "tensor"
LANES = 128
VMEM = pltpu.VMEM
SMEM = pltpu.SMEM


def swap(x, count, offset):
    return lax.ppermute(x, AXIS, [(i, i ^ offset) for i in range(count)])


def exchange(x, groups=None):
    return lax.all_to_all(
        x, AXIS, split_axis=0, concat_axis=0, axis_index_groups=groups, tiled=True
    )


def sum_over(x, count, beside):
    step, turn, terms = count, 0, []
    while step > 1:
        radix = 4 if step % 4 == 0 else 2
        step //= radix
        others = [swap(x, count, k * step) for k in range(1, radix)]
        term = beside(turn, x)
        if term is not None:
            *others, term = lax.optimization_barrier((*others, term))
            terms.append(term)
        for other in others:
            x = x + other
        turn += 1
    return x, terms


def pack_kernel(*refs):
    in_refs, out_ref = refs[-2::-1], refs[-1]
    rows, width = in_refs[0].shape
    per = 16 // rows
    for first in range(0, len(in_refs), per):
        parts = [r[...].astype(jnp.float32) for r in in_refs[first : first + per]]
        at = slice(first * rows, (first + per) * rows)
        out_ref[at] = jnp.concatenate(parts, axis=0).astype(jnp.bfloat16)


def pack(parts):
    rows, width = parts[0].shape
    return pl.pallas_call(
        pack_kernel,
        out_shape=jax.ShapeDtypeStruct((rows * len(parts), width), jnp.bfloat16),
        in_specs=[spec()] * len(parts),
        out_specs=spec(),
        compiler_params=pltpu.CompilerParams(vmem_limit_bytes=16 * 1024 * 1024),
        name="pack",
    )(*parts[::-1])


def gather_rows(x, count, beside):
    step = count // 4
    near, middle, far = (swap(x, count, k * step) for k in (1, 2, 3))
    step //= 2
    across = [swap(p, count, step) for p in (middle, near, far, x)]
    *across, loaded = lax.optimization_barrier((*across, beside(middle)))
    held = [pack([x, near, middle, far] + [across[i] for i in (3, 1, 0, 2)])]
    step //= 2
    while step > 1:
        held = held + [swap(h, count, step) for h in held]
        step //= 2
    return held, held + [swap(h, count, 1) for h in held], loaded


def place_of(row, me, count, rows):
    block = row // rows
    source = (block % 4) * (count // 4)
    piece, step = block // 4, count // 8
    while step:
        source = source + (piece % 2) * step
        piece, step = piece // 2, step // 2
    return (source ^ me) * rows + row % rows


def spec(space=VMEM):
    return pl.BlockSpec(memory_space=space)


def hbm(x):
    return pltpu.with_memory_space_constraint(x, pltpu.HBM)


def iota(shape, dim):
    return lax.broadcasted_iota(jnp.int32, shape, dim)


def one_hot(condition):
    return jnp.where(condition, 1.0, 0.0).astype(jnp.bfloat16)


def norm_kernel(
    hidden_hbm, gain_hbm, names_hbm, slots_hbm, out_ref, hidden_ref, gain_ref, names_ref, slots_ref, sems
):
    copies = [
        pltpu.make_async_copy(source, target, sems.at[i])
        for i, (source, target) in enumerate(
            (
                (hidden_hbm, hidden_ref),
                (gain_hbm, gain_ref),
                (names_hbm, names_ref),
                (slots_hbm, slots_ref),
            )
        )
    ]
    for copy in copies:
        copy.start()
    for copy in copies:
        copy.wait()
    rows, width = hidden_ref.shape
    hidden = hidden_ref[...].astype(jnp.float32)
    power = jnp.sum(hidden * hidden, axis=1, keepdims=True) / width
    gain = gain_ref[...].reshape(1, width).astype(jnp.float32)
    out_ref[:, :width] = (hidden * lax.rsqrt(power + eps) * gain).astype(jnp.bfloat16)
    row, lane = iota((rows, LANES), 0), iota((rows, LANES), 1)
    tags = jnp.zeros((rows, LANES), jnp.float32)
    for r in range(rows):
        name = names_ref[r]
        tag = jnp.where(lane < LANES // 2, name, slots_ref[name]).astype(jnp.float32)
        tags = jnp.where(row == r, tag, tags)
    out_ref[:, width:] = tags.astype(jnp.bfloat16)


NT = (((1,), (1,)), ((), ()))


def load_kernel(starts, *refs):
    _, weight_hbm, *refs = refs
    *refs, sems = refs
    rows_refs, refs = refs[-len(starts) :], refs[: -len(starts)]
    copies = []
    if refs:
        maps_hbm, maps_ref = refs
        for s in range(maps_ref.shape[0]):
            copies.append((maps_hbm.at[s, : maps_ref.shape[1]], maps_ref.at[s]))
    for start, rows_ref in zip(starts, rows_refs):
        for k in range(0, rows_ref.shape[0], 1024):
            copies.append((weight_hbm.at[start + k : start + k + 1024], rows_ref.at[k : k + 1024]))
    copies = [pltpu.make_async_copy(*ends, sems.at[i]) for i, ends in enumerate(copies)]
    for copy in copies:
        copy.start()
    for copy in copies:
        copy.wait()


def down_kernel(count, rows, pieces, ranks, *refs):
    map_refs, piece_refs = refs[:2], refs[2 : 2 + pieces]
    tag_refs, refs = refs[2 + pieces : 2 + 2 * pieces], refs[2 + 2 * pieces :]
    out_ref = refs[0]
    me = lax.axis_index(AXIS)
    held, _, width = map_refs[0].shape
    rank = ranks[1] - ranks[0]
    total, half = count * rows, count * rows // 2
    chunk = 4096
    sums = jnp.zeros((2 * held * rank, half), jnp.float32)
    for k in range(0, width, chunk):
        x = jnp.concatenate([p[:, k : k + chunk] for p in piece_refs], axis=0)
        maps = jnp.concatenate(
            [m[:, :rank, k : k + chunk].reshape(held * rank, chunk) for m in map_refs], axis=0
        )
        sums = sums + lax.dot_general(maps, x, NT, preferred_element_type=jnp.float32)
    if len(refs) > 1:
        refs[1][...] = map_refs[1][:, rank:]
    tags = jnp.concatenate([t[...] for t in tag_refs], axis=0)
    pick = one_hot(iota((16, LANES), 1) == LANES // 2)
    slots = lax.dot_general(pick, tags, NT, preferred_element_type=jnp.float32)[:1]
    chosen = jnp.zeros((rank, half), jnp.float32)
    for m in range(2):
        for s in range(held):
            slot = ((me ^ m) * held + s).astype(jnp.float32)
            at = (m * held + s) * rank
            chosen = jnp.where(slots == slot, sums[at : at + rank], chosen)
    row, column = iota((half, total), 0), iota((half, total), 1)
    back = one_hot(place_of(row, me, count, rows) == column)
    placed = jnp.dot(chosen.astype(jnp.bfloat16), back, preferred_element_type=jnp.float32)
    folds = out_ref.shape[1] // total
    part = rank // folds
    folded = [placed[f * part : (f + 1) * part] for f in range(folds)]
    value = jnp.concatenate(folded, axis=1).astype(jnp.bfloat16)
    out_ref[...] = value


def spans_of(length):
    spans, at = [], 0
    while at < length:
        left = length - at
        size = 1024 if left > 1024 else min(left, 512)
        spans.append((at, size))
        at += size
    return spans


def base_kernel(pieces, start, ready, *refs):
    ready_ref = refs[pieces] if ready else None
    weight_hbm, _, out_ref, weight_ref, sems, side_ref = refs[-6:]
    total, columns = out_ref.shape
    whole = columns // 256 * 256
    narrow = columns - whole == 128
    spans = spans_of(weight_ref.shape[0])
    copies = [
        pltpu.make_async_copy(
            weight_hbm.at[start + ready + k : start + ready + k + length],
            weight_ref.at[k : k + length],
            sems.at[i],
        )
        for i, (k, length) in enumerate(spans)
    ]
    for copy in copies:
        copy.start()

    def rows_of(at, length):
        return jnp.concatenate([p[:, at : at + length] for p in refs[:pieces]], axis=0)

    def dot(x, weight):
        return jnp.dot(x, weight, preferred_element_type=jnp.float32)

    def wide(from_ref, k, length, offset):
        if whole:
            x = rows_of(start + offset, length)
            term = dot(x, from_ref[k : k + length, :whole])
            out_ref[:, :whole] = term if offset == 0 else out_ref[:, :whole] + term

    def rest(weight, offset):
        length = weight.shape[0]
        if narrow:
            half = length // 2
            left = [rows_of(start + offset + h, half) for h in (0, half)]
            right = [weight[:half], weight[half:]]
            term = dot(jnp.concatenate(left, axis=0), jnp.concatenate(right, axis=1))
        else:
            term = dot(rows_of(start + offset, length), weight)
        side_ref[...] = term if offset == 0 else side_ref[...] + term

    if ready:
        wide(ready_ref, 0, ready, 0)
    for (k, length), copy in zip(spans, copies):
        if (k, length) == spans[-1] and columns > whole:
            weight = weight_ref[:k, whole:]
            if ready:
                weight = jnp.concatenate([ready_ref[:, whole:], weight], axis=0)
            rest(weight, 0)
        copy.wait()
        wide(weight_ref, k, length, ready + k)
    if columns > whole:
        rest(weight_ref[k:, whole:], ready + k)
        side = side_ref[...]
        out_ref[:, whole:] = side[:total, :128] + side[total:, 128:] if narrow else side


def lift_kernel(count, rows, pieces, bounds, rank, *refs):
    tag_refs, refs = refs[:pieces], refs[pieces:]
    (down_ref, up_ref), base_refs, (out_ref, sum_ref) = refs[:2], refs[2:-2], refs[-2:]
    total = count * rows
    me = lax.axis_index(AXIS)
    adapters, per, columns = up_ref.shape
    wide = adapters * per
    row, column = iota((total, total), 0), iota((total, total), 1)
    order = one_hot(place_of(column, me, count, rows) == row)
    back = one_hot(place_of(row, me, count, rows) == column)
    folded = down_ref[...].astype(jnp.float32)
    folds = folded.shape[1] // total
    down = jnp.concatenate([folded[:, f * total : (f + 1) * total] for f in range(folds)], axis=0)
    down = lax.dot_general(
        back, down.astype(jnp.bfloat16), NT, preferred_element_type=jnp.float32
    ).astype(jnp.bfloat16)
    names = jnp.concatenate([t[...] for t in tag_refs], axis=0).astype(jnp.float32)[:, :1]
    named = (iota((total, wide), 1) // per).astype(jnp.float32) == names
    start = me * columns
    value = base_refs[0][...]
    for b in base_refs[1:]:
        value = value + b[...]
    sum_ref[...] = value
    for g in range(rank // per):
        low, high = bounds[g], bounds[g + 1]

        @pl.when((start < high) & (start + columns > low))
        def _():
            at = iota((rank, wide), 1) % per + g * per
            spread = one_hot(at == iota((rank, wide), 0))
            copies = jnp.dot(down, spread, preferred_element_type=jnp.float32)
            chosen = jnp.where(named, copies, 0.0).astype(jnp.bfloat16)
            up = up_ref[...].reshape(wide, columns)
            lifted = jnp.dot(chosen, up, preferred_element_type=jnp.float32)
            at = iota((total, columns), 1) + start
            sum_ref[...] += jnp.where((at >= low) & (at < high), lifted, 0.0)

    placed = jnp.dot(
        order, sum_ref[...].astype(jnp.bfloat16), preferred_element_type=jnp.float32
    ).astype(jnp.bfloat16)
    for d in range(count):
        out_ref[d] = placed[d * rows : (d + 1) * rows]


def attend_kernel(lengths_ref, qkv_ref, keys_ref, values_ref, out_ref):
    rows, kv_heads, context, dim = keys_ref.shape
    width = out_ref.shape[1]
    groups = width // dim // kv_heads
    per_head = groups * rows
    together = max(2, LANES // per_head)
    lanes = together * per_head
    lane = iota((1, lanes), 1)
    length = jnp.zeros((1, lanes), jnp.int32)
    for b in range(rows):
        length = jnp.where(lane % rows == b, lengths_ref[b], length)
    live = iota((context, lanes), 0) < length
    odd = iota((lanes, 1), 0) // per_head % 2 == 1
    pair_row = iota((2 * per_head, 1), 0)
    scale = dim ** (-0.5)

    def columns(at):
        return qkv_ref[:, at : at + dim].astype(jnp.float32)

    steps = []
    for first in range(0, kv_heads, together):
        heads = range(first, first + together)
        query = jnp.concatenate(
            [columns((h * groups + g) * dim) for h in heads for g in range(groups)], axis=0
        )
        half = jnp.concatenate([jnp.where(odd, 0.0, query), jnp.where(odd, query, 0.0)], axis=1)
        half = half.astype(jnp.bfloat16)
        scores = jnp.zeros((context, lanes), jnp.float32)
        for n in range(0, together, 2):
            cached = [keys_ref[:, first + n + m].reshape(rows * context, dim) for m in range(2)]
            every = lax.dot_general(
                jnp.concatenate(cached, axis=1), half, NT, preferred_element_type=jnp.float32
            )
            for b in range(rows):
                mine = (lane // (2 * per_head) == n // 2) & (lane % rows == b)
                scores = jnp.where(mine, every[b * context : (b + 1) * context], scores)
        steps.append((first, heads, query, scores))

    for i, (first, heads, query, scores) in enumerate(steps):
        key = jnp.concatenate([columns(width + h * dim) for h in heads for _ in range(groups)], axis=0)
        at = width + kv_heads * dim
        value = jnp.concatenate([columns(at + h * dim) for h in heads for _ in range(groups)], axis=0)
        scores = jnp.where(live, scores * scale, -1e30)
        own = jnp.sum((query * key).T, axis=0, keepdims=True) * scale
        peak = jnp.maximum(jnp.max(scores, axis=0, keepdims=True), own)
        weights = jnp.exp(scores - peak)
        own_weight = jnp.exp(own - peak)
        denominator = jnp.sum(weights, axis=0, keepdims=True) + own_weight
        share = 1.0 / denominator
        probs = (weights * share).T.astype(jnp.bfloat16)
        own_prob = (own_weight * share).astype(jnp.bfloat16).astype(jnp.float32)
        steps[i] = (first, probs, jnp.broadcast_to(own_prob, (dim, lanes)).T * value)

    for first, probs, own_term in steps:
        for n in range(0, together, 2):
            span = slice(n * per_head, (n + 2) * per_head)
            mixed = jnp.zeros((2 * per_head, dim), jnp.float32)
            for b in range(rows):
                both = jnp.concatenate([values_ref[b, first + n + m] for m in range(2)], axis=1)
                one = jnp.dot(probs[span], both, preferred_element_type=jnp.float32)
                one = jnp.where(pair_row < per_head, one[:, :dim], one[:, dim:])
                mixed = jnp.where(pair_row % rows == b, one, mixed)
            mixed = (mixed + own_term[span]).astype(jnp.bfloat16)
            for g in range(2 * groups):
                at = ((first + n) * groups + g) * dim
                out_ref[:, at : at + dim] = mixed[g * rows : (g + 1) * rows]


def local(
    input_hidden,
    input_norm_gain,
    request_adapter,
    adapter_storage,
    lengths,
    projection_weight,
    output_weight,
    adapter_down,
    projection_up_adapter,
    output_up_adapter,
    cache_keys,
    cache_values,
    *,
    count,
):
    rows, width = input_hidden.shape
    rank = projection_up_adapter.shape[1]
    held = adapter_down.shape[0]
    kv_heads, context, head_dim = cache_keys.shape[1:]
    kv_width = kv_heads * head_dim
    total = rows * count
    bf16, f32 = jnp.bfloat16, jnp.float32
    params = pltpu.CompilerParams(vmem_limit_bytes=(16 if total <= 64 else 60) * 1024 * 1024)
    own_maps = jnp.swapaxes(adapter_down, 1, 2)

    normed = pl.pallas_call(
        norm_kernel,
        out_shape=VMEM((rows, width + LANES), bf16),
        in_specs=[spec(pltpu.HBM)] * 4,
        out_specs=spec(),
        scratch_shapes=[
            VMEM((rows, width), bf16),
            VMEM((width,), bf16),
            SMEM((rows,), jnp.int32),
            SMEM(adapter_storage.shape, jnp.int32),
            pltpu.SemaphoreType.DMA((4,)),
        ],
        compiler_params=params,
        name="norm",
    )(
        hbm(input_hidden),
        hbm(input_norm_gain),
        hbm(request_adapter.reshape(rows)),
        hbm(adapter_storage),
    )

    def load(after, weight, parts, maps=None):
        columns = weight.shape[1]
        outs = [VMEM((length, columns), bf16) for _, length in parts]
        sources, copies = [], sum(length // 1024 for _, length in parts)
        if maps is not None:
            outs = [VMEM((held, 3 * rank, width), bf16)] + outs
            sources, copies = [hbm(maps)], copies + held
        return pl.pallas_call(
            functools.partial(load_kernel, [start for start, _ in parts]),
            out_shape=outs,
            in_specs=[spec(pl.ANY)] + [spec(pltpu.HBM)] * (1 + len(sources)),
            out_specs=[spec()] * len(outs),
            scratch_shapes=[pltpu.SemaphoreType.DMA((copies,))],
            compiler_params=params,
            cost_estimate=pl.CostEstimate(
                flops=0,
                bytes_accessed=4 * columns * sum(length for _, length in parts),
                transcendentals=0,
            ),
            name="load",
        )(after, hbm(weight), *sources)

    def tag_specs(pieces):
        return [pl.BlockSpec((p.shape[0], LANES), lambda i: (0, width // LANES)) for p in pieces]

    def downs(own, sibling, pieces, tagged, low, high):
        ranks = high - low
        lanes = max(LANES, total)
        whole = lambda x: pl.BlockSpec(x.shape, lambda i: (0,) * len(x.shape))
        own_spec = pl.BlockSpec((held, ranks, width), lambda i: (0, low // ranks, 0))
        outs = [jax.ShapeDtypeStruct((ranks * total // lanes, lanes), bf16)]
        if low == 0:
            rest = sibling.shape[1] - ranks
            outs.append(jax.ShapeDtypeStruct((held, rest, width), bf16))
        return pl.pallas_call(
            functools.partial(down_kernel, count, rows, len(pieces), (low, high)),
            grid=(1,),
            out_shape=outs,
            in_specs=[own_spec, whole(sibling)]
            + [pl.BlockSpec((p.shape[0], width), lambda i: (0, 0)) for p in pieces]
            + tag_specs(tagged),
            out_specs=[whole(x) for x in outs],
            compiler_params=params,
            cost_estimate=pl.CostEstimate(
                flops=2 * total * width * held * ranks,
                bytes_accessed=2 * width * (2 * held * ranks + total),
                transcendentals=0,
            ),
            name="down",
        )(own, sibling, *pieces, *tagged)

    def base(pieces, weight, after, start, ready, length):
        columns = weight.shape[1]
        first = [] if ready is None else [ready]
        stream = length - sum(r.shape[0] for r in first)
        rest = columns % 256
        side = (2 * total, 256) if rest == 128 else (total, max(rest, 1))
        return pl.pallas_call(
            functools.partial(base_kernel, len(pieces), start, length - stream),
            out_shape=jax.ShapeDtypeStruct((total, columns), f32),
            in_specs=[spec()] * (len(pieces) + len(first)) + [spec(pltpu.HBM), spec(pl.ANY)],
            out_specs=spec(),
            scratch_shapes=[
                VMEM((stream, columns), bf16),
                pltpu.SemaphoreType.DMA((len(spans_of(stream)),)),
                VMEM(side, f32),
            ],
            compiler_params=params,
            cost_estimate=pl.CostEstimate(
                flops=2 * total * length * columns,
                bytes_accessed=4 * length * columns,
                transcendentals=0,
            ),
            name="base",
        )(*pieces, *first, hbm(weight), after)

    def lift(down, tagged, up, base_terms, bounds, ranks):
        columns = up.shape[2]
        whole = lambda x: pl.BlockSpec(x.shape, lambda i: (0,) * x.ndim)
        operands = [down, up] + base_terms
        return pl.pallas_call(
            functools.partial(lift_kernel, count, rows, len(tagged), bounds, ranks),
            grid=(1,),
            out_shape=jax.ShapeDtypeStruct((count, rows, columns), bf16),
            in_specs=tag_specs(tagged) + [whole(x) for x in operands],
            out_specs=pl.BlockSpec((count, rows, columns), lambda i: (0, 0, 0)),
            scratch_shapes=[VMEM((total, columns), f32)],
            compiler_params=params,
            name="lift",
        )(*tagged, *operands)

    def project(column, pieces, tagged, own, sibling, ready, low, high, weight, up, bounds):
        half = width // 2
        down, *rest = downs(own, sibling, column, tagged[: len(column)], low, high)

        def term(turn, after):
            if turn > 1:
                return None
            return base(pieces, weight, after, turn * half, ready[turn], half)

        down, base_terms = sum_over(down, count, term)
        columns = lift(down, tagged, up, base_terms, bounds, high - low)
        mine = exchange(columns)
        return jnp.swapaxes(mine, 0, 1).reshape(rows, -1), rest

    bounds = (0, width, width + kv_width, width + 2 * kv_width)
    sibling_maps = jnp.swapaxes(swap(adapter_down, count, 1), 1, 2)
    parts = ((0, 2048), (width // 2, 2048))
    column, tagged, (first_maps, *ready) = gather_rows(
        normed, count, lambda piece: load(piece, projection_weight, parts, own_maps)
    )
    qkv_mine, rest = project(
        column,
        tagged,
        tagged,
        first_maps,
        sibling_maps,
        ready,
        0,
        3 * rank,
        projection_weight,
        projection_up_adapter,
        bounds,
    )
    attended = pl.pallas_call(
        attend_kernel,
        out_shape=jax.ShapeDtypeStruct((rows, width), bf16),
        in_specs=[spec(SMEM)] + [spec()] * 3,
        out_specs=spec(),
        compiler_params=params,
        cost_estimate=pl.CostEstimate(
            flops=4 * rows * width * context,
            bytes_accessed=4 * cache_keys.size,
            transcendentals=rows * width // head_dim * context,
        ),
        name="attend",
    )(lengths, qkv_mine, cache_keys, cache_values)
    parts = ((0, 1024), (width // 2, 2048))
    column, pieces, ready = gather_rows(
        attended, count, lambda piece: load(piece, output_weight, parts)
    )
    output, _ = project(
        column,
        pieces,
        tagged,
        own_maps,
        rest[0],
        ready,
        3 * rank,
        4 * rank,
        output_weight,
        output_up_adapter,
        (0, width),
    )
    return output


def solution(mesh):
    count = mesh.shape[AXIS]

    def body(*arrays):
        return local(*arrays, count=count)

    return jax.shard_map(
        body,
        mesh=mesh,
        in_specs=(
            P(("groups", "tensor"), None),
            P(),
            P(("groups", "tensor"), None),
            P(),
            P(("groups", "tensor")),
            P(None, "tensor"),
            P(None, "tensor"),
            P("tensor", None, None),
            P(None, None, "tensor"),
            P(None, None, "tensor"),
            P(("groups", "tensor"), None, None, None),
            P(("groups", "tensor"), None, None, None),
        ),
        out_specs=P(("groups", "tensor"), None),
        check_vma=False,
    )
```
